32 devices in a mesh: section: 4 (over x, core), seq: 8 (over z, y).
Axes of the slice: x: 2, y: 2, z: 4, core: 2. Of those that a mesh axis runs over, the one named last changes fastest.
Arguments:
- query: bfloat16 [4, 4096, 1024], P('section', 'seq'), may hold values from -6 to 6
- key: bfloat16 [4, 4096, 1024], P('section', 'seq'), may hold values from -6 to 6
- value: bfloat16 [4, 4096, 1024], P('section', 'seq'), may hold values from -6 to 6
- grad_sent: bfloat16 [4, 4096, 2048], P('section', 'seq'), may hold values from -6 to 6
- out_weight: bfloat16 [4, 1024, 2048], P('section'), may hold values from -0.125 to 0.125
- assign: int32 [4, 4, 4096], P('section', None, 'seq'), may hold values from 0 to 1, as said below
Outputs:
- grad_query: bfloat16 [4, 4096, 1024], P('section', 'seq')
- grad_key: bfloat16 [4, 4096, 1024], P('section', 'seq')
- grad_value: bfloat16 [4, 4096, 1024], P('section', 'seq')
The draws below stay inside these ranges and needn't reach their ends.
Inputs may be any that keep to these rules, and one draw needn't show every extreme that they name: `assign`: for each section and routing head, every cluster holds exactly 2048 tokens. The 512 tokens of one device put 1, 3, 5 or 7 times 448 // 7 tokens into one cluster, so at most 448, and some device reaches 448 for every section and head.
All inputs are finite; a program needn't handle non-finite values.
Results may differ from the reference program's by a relative error of at most 0.0058.
Values may be sent and summed in bfloat16 or wider, within the bound.
No kernel may reach another device: no remote copies, remote signals or barrier semaphores. Data moves between devices by JAX's collectives and lax.ppermute only.
A program may use at most 128 MiB of HBM per device.

```python
import jax
import jax.numpy as jnp
from jax import lax

D = 2048
HR = 4
HL = 4
HD = 128
CS = 2048
WIN = 512
TOK_DEV = 512
SECTIONS = 4
TOKENS = 4096
NCL = 2
HH = 1024


def balanced_assign(key):
    devices = TOKENS // TOK_DEV
    clusters = TOKENS // CS
    average = CS // devices
    slots = jnp.arange(TOK_DEV, dtype=jnp.int32)

    def one_head(head_key):
        parts = jax.random.split(head_key, 3)
        device_order = jax.random.permutation(parts[0], devices).astype(jnp.int32)
        cluster_order = jax.random.permutation(parts[1], clusters).astype(jnp.int32)
        first_sign = 1 - 2 * (device_order % 2)
        second_sign = 1 - 2 * (device_order // 2 % 2)
        column_sign = 1 - 2 * (cluster_order % 2)
        counts = average + column_sign[None, :] * (first_sign[:, None] * (average // 2) + second_sign[:, None] * (average // 4))
        bounds = jnp.cumsum(counts, axis=1).astype(jnp.int32)
        labels = jax.vmap(lambda edge: jnp.searchsorted(edge, slots, side='right'))(bounds).astype(jnp.int32)
        shuffles = jax.vmap(lambda part_key: jax.random.permutation(part_key, TOK_DEV))(jax.random.split(parts[2], devices)).astype(jnp.int32)
        device_rows = jnp.arange(devices, dtype=jnp.int32)[:, None]
        placed = jnp.zeros((devices, TOK_DEV), jnp.int32).at[device_rows, shuffles].set(labels)
        return placed.reshape(TOKENS)
    head_keys = jax.random.split(jax.random.fold_in(key, 17), SECTIONS * HR)
    return jax.vmap(one_head)(head_keys).reshape(SECTIONS, HR, TOKENS)


def base_values(key, salt):
    shape = (SECTIONS, TOKENS, HR + HL, HD)
    values = jax.random.truncated_normal(jax.random.fold_in(key, salt), -6.0, 6.0, shape, jnp.float32)
    return values


def draw_assign(key, part):
    return balanced_assign(key)


def draw_query(key, part):
    values = base_values(key, 1)
    return values.reshape(SECTIONS, TOKENS, (HR + HL) * HD).astype(jnp.bfloat16)


def draw_key(key, part):
    values = base_values(key, 2)
    return values.reshape(SECTIONS, TOKENS, (HR + HL) * HD).astype(jnp.bfloat16)


def shard_levels(rng, dims, cuts, low, high):
    level = 1.0
    for dim, blocks in cuts:
        steps = jax.random.uniform(jax.random.fold_in(jax.random.fold_in(rng, 6), dim), (blocks,), jnp.float32, low / len(cuts), high / len(cuts))
        level = level * jnp.repeat(jnp.exp(steps), dims[dim] // blocks).reshape((-1,) + (1,) * (len(dims) - 1 - dim))
    return level


def scatter_about(stream_key, extent, spread, most, cuts=(), kind=jnp.bfloat16):
    level = shard_levels(stream_key, extent, cuts, -0.22, 0.18) if cuts else 1.0
    values = jax.random.normal(stream_key, extent, jnp.float32) * spread * level
    return jnp.minimum(jnp.maximum(values, -most), most).astype(kind)


def setup_inputs(seed: int = 0) -> dict:
    key_list = jax.random.split(jax.random.key(seed), 7)
    query = draw_query(jax.random.fold_in(key_list[6], 71), 0)
    key = draw_key(jax.random.fold_in(key_list[6], 71), 0)
    value = scatter_about(key_list[2], (SECTIONS, TOKENS, HH), 1.0, 6.0, ((0, 4), (1, 8)))
    grad_sent = scatter_about(key_list[3], (SECTIONS, TOKENS, D), 1.0, 6.0, ((0, 4), (1, 8)))
    out_weight = scatter_about(key_list[4], (SECTIONS, HH, D), D ** -0.5, 0.125, ((0, 4),))
    assign = draw_assign(jax.random.fold_in(key_list[6], 71), 0)
    return dict(query=query, key=key, value=value, grad_sent=grad_sent, out_weight=out_weight, assign=assign)


def cluster_block(query_rows, key_rows, value_rows, grad_rows, allowed, factor):
    scores = jnp.dot(query_rows, key_rows.T, preferred_element_type=jnp.float32) * factor
    scores = jnp.where(allowed, scores, -1e30)
    highest = jnp.max(scores, axis=1, keepdims=True)
    weights = jnp.exp(scores - highest)
    probs = weights / jnp.sum(weights, axis=1, keepdims=True)
    dprob = jnp.dot(grad_rows, value_rows.T, preferred_element_type=jnp.float32)
    delta = jnp.sum(probs * dprob, axis=1, keepdims=True)
    dscore = probs * (dprob - delta)
    probs_b = probs.astype(jnp.bfloat16)
    dscore_b = dscore.astype(jnp.bfloat16)
    grad_query = jnp.dot(dscore_b, key_rows, preferred_element_type=jnp.float32) * factor
    grad_key = jnp.dot(dscore_b.T, query_rows, preferred_element_type=jnp.float32) * factor
    grad_value = jnp.dot(probs_b.T, grad_rows, preferred_element_type=jnp.float32)
    return grad_query, grad_key, grad_value


def cluster_grads(query_rows, key_rows, value_rows, grad_rows, factor):
    length = query_rows.shape[0]
    span = min(512, length)
    pieces = []
    total_key = jnp.zeros(key_rows.shape, jnp.float32)
    total_value = jnp.zeros(value_rows.shape, jnp.float32)
    for index in range(length // span):
        first = index * span
        end = first + span
        allowed = jnp.arange(end, dtype=jnp.int32)[None, :] <= (first + jnp.arange(span, dtype=jnp.int32))[:, None]
        part_query, part_key, part_value = cluster_block(query_rows[first:end], key_rows[:end], value_rows[:end], grad_rows[first:end], allowed, factor)
        pieces.append(part_query)
        total_key = total_key.at[:end].add(part_key)
        total_value = total_value.at[:end].add(part_value)
    return jnp.concatenate(pieces, axis=0), total_key, total_value


def window_block(query_rows, key_rows, value_rows, grad_rows, allowed, factor):
    query_float = query_rows.astype(jnp.float32)
    key_float = key_rows.astype(jnp.float32)
    value_float = value_rows.astype(jnp.float32)
    grad_float = grad_rows.astype(jnp.float32)
    scores = jnp.einsum('qhd,khd->hqk', query_float, key_float) * factor
    scores = jnp.where(allowed[None], scores, -1e30)
    highest = jnp.max(scores, axis=2, keepdims=True)
    weights = jnp.exp(scores - highest)
    probs = weights / jnp.sum(weights, axis=2, keepdims=True)
    dprob = jnp.einsum('qhd,khd->hqk', grad_float, value_float)
    delta = jnp.sum(probs * dprob, axis=2, keepdims=True)
    dscore = probs * (dprob - delta)
    probs_b = lax.optimization_barrier(probs.astype(jnp.bfloat16)).astype(jnp.float32)
    dscore_b = lax.optimization_barrier(dscore.astype(jnp.bfloat16)).astype(jnp.float32)
    grad_query = jnp.einsum('hqk,khd->qhd', dscore_b, key_float) * factor
    grad_key = jnp.einsum('hqk,qhd->khd', dscore_b, query_float) * factor
    grad_value = jnp.einsum('hqk,qhd->khd', probs_b, grad_float)
    return grad_query, grad_key, grad_value


def section_grads(operands):
    query, key, value, boundary, weight, labels = operands
    factor = HD ** -0.5
    heads = HR + HL
    attn_grad = jnp.dot(boundary, weight.T, preferred_element_type=jnp.float32).astype(jnp.bfloat16)
    query_heads = query.reshape(TOKENS, heads, HD)
    key_heads = key.reshape(TOKENS, heads, HD)
    value_heads = value.reshape(TOKENS, heads, HD)
    grad_heads = attn_grad.reshape(TOKENS, heads, HD)
    positions = jnp.arange(TOKENS, dtype=jnp.int32)
    routed = ([], [], [])
    for head in range(HR):
        order = jnp.argsort(labels[head] * TOKENS + positions).astype(jnp.int32)

        def grouped(array):
            return array[order, head].reshape(NCL, CS, HD)

        results = lax.map(lambda group: cluster_grads(group[0], group[1], group[2], group[3], factor),
                          (grouped(query_heads), grouped(key_heads), grouped(value_heads), grouped(grad_heads)))
        for bucket, result in zip(routed, results):
            placed = jnp.zeros((TOKENS, HD), jnp.bfloat16).at[order].set(result.astype(jnp.bfloat16).reshape(TOKENS, HD))
            bucket.append(placed)
    local_query = query_heads[:, HR:]
    local_key = key_heads[:, HR:]
    local_value = value_heads[:, HR:]
    local_grad = grad_heads[:, HR:]
    padding = jnp.zeros((WIN, HL, HD), local_key.dtype)
    keys_padded = jnp.concatenate([padding, local_key], axis=0)
    values_padded = jnp.concatenate([padding, local_value], axis=0)
    span = min(512, TOK_DEV)

    def local_step(carry, index):
        total_key, total_value = carry
        first = index * span
        query_rows = lax.dynamic_slice_in_dim(local_query, first, span, 0)
        grad_rows = lax.dynamic_slice_in_dim(local_grad, first, span, 0)
        key_rows = lax.dynamic_slice_in_dim(keys_padded, first, span + WIN, 0)
        value_rows = lax.dynamic_slice_in_dim(values_padded, first, span + WIN, 0)
        query_pos = first + jnp.arange(span, dtype=jnp.int32)
        key_pos = first - WIN + jnp.arange(span + WIN, dtype=jnp.int32)
        allowed = (key_pos[None, :] > query_pos[:, None] - WIN) & (key_pos[None, :] <= query_pos[:, None]) & (key_pos[None, :] >= 0)
        part_query, part_key, part_value = window_block(query_rows, key_rows, value_rows, grad_rows, allowed, factor)
        total_key = lax.dynamic_update_slice_in_dim(total_key, lax.dynamic_slice_in_dim(total_key, first, span + WIN, 0) + part_key, first, 0)
        total_value = lax.dynamic_update_slice_in_dim(total_value, lax.dynamic_slice_in_dim(total_value, first, span + WIN, 0) + part_value, first, 0)
        return (total_key, total_value), part_query

    empty = jnp.zeros((TOKENS + WIN, HL, HD), jnp.float32)
    (total_key, total_value), local_dq = lax.scan(local_step, (empty, empty), jnp.arange(TOKENS // span, dtype=jnp.int32))
    local_dq = local_dq.reshape(TOKENS, HL, HD).astype(jnp.bfloat16)
    local_dk = total_key[WIN:].astype(jnp.bfloat16)
    local_dv = total_value[WIN:].astype(jnp.bfloat16)
    out_query = jnp.concatenate([jnp.stack(routed[0], axis=1), local_dq], axis=1).reshape(TOKENS, heads * HD)
    out_key = jnp.concatenate([jnp.stack(routed[1], axis=1), local_dk], axis=1).reshape(TOKENS, heads * HD)
    out_value = jnp.concatenate([jnp.stack(routed[2], axis=1), local_dv], axis=1).reshape(TOKENS, heads * HD)
    return out_query, out_key, out_value


def reference(query, key, value, grad_sent, out_weight, assign):
    boundary = jnp.roll(grad_sent, -1, axis=0)
    grad_query, grad_key, grad_value = lax.map(section_grads, (query, key, value, boundary, out_weight, assign))
    return grad_query, grad_key, grad_value
```

```python
import functools

import jax
import jax.numpy as jnp
from jax import lax
from jax.experimental import pallas as pl
from jax.experimental.pallas import tpu as pltpu
from jax.sharding import PartitionSpec as P

HR = 4
HL = 4
HD = 128
CS = 2048
WIN = 512
QB = 256
MIB = 1024 * 1024
NT = (((1,), (1,)), ((), ()))
F32 = jnp.float32
BF16 = jnp.bfloat16


def vmem(count=1):
    return [pl.BlockSpec(memory_space=pltpu.VMEM)] * count


def smem(count=1):
    return [pl.BlockSpec(memory_space=pltpu.SMEM)] * count


def params(mib):
    return pltpu.CompilerParams(vmem_limit_bytes=mib * MIB)


def dot(a, b):
    return jnp.dot(a, b, preferred_element_type=F32)


def dot_nt(a, b):
    return lax.dot_general(a, b, NT, preferred_element_type=F32)


def rows(start, size):
    return pl.ds(pl.multiple_of(start, size), size)


def pack_kernel(unit, place, x0, x1, x2, x3, sorted_ref, send_ref, slot_row, slot_col, kept_ref):
    tok = x0.shape[0] - 16
    tok = tok // 3
    side = place[1]
    lane = lax.broadcasted_iota(jnp.int32, (1, tok), 1).astype(F32)
    labels = []
    for x in (x0, x1, x2, x3):
        block = x[3 * tok :, :].astype(F32)
        labels.append(jnp.concatenate([block[r : r + 1, :] for r in range(tok // 128)], axis=1))
    label = jnp.concatenate(labels + [jnp.zeros((4, tok), F32)], axis=0)
    upper = (
        lax.broadcasted_iota(jnp.int32, (tok, tok), 0) <= lax.broadcasted_iota(jnp.int32, (tok, tok), 1)
    ).astype(BF16)
    ones = dot(label.astype(BF16), upper)
    totals = [jnp.sum(row).astype(jnp.int32) for row in labels]
    whole = totals[0] + totals[1] + totals[2] + totals[3]
    half = CS // 2
    keep_one = jnp.where(side == 0, (whole > half).astype(jnp.int32), (whole >= half).astype(jnp.int32))
    keep_f = keep_one.astype(F32)
    slots = []
    for d in range(4):
        kept = jnp.where(keep_one == 1, totals[d], tok - totals[d])
        kept_ref[d] = kept // unit
        is_kept = labels[d] * keep_f + (1.0 - labels[d]) * (1.0 - keep_f)
        ones_d = ones[d : d + 1, :]
        count = ones_d * keep_f + (lane + 1.0 - ones_d) * (1.0 - keep_f)
        slot = jnp.where(is_kept > 0.5, count - 1.0, kept.astype(F32) + lane - count)
        slots.append(slot)
    slots_all = jnp.concatenate(slots + [jnp.zeros((124, tok), F32)], axis=0)
    slot_row[...] = slots_all[:8, :]
    slot_col[...] = slots_all.T
    row_index = lax.broadcasted_iota(jnp.int32, (tok, tok), 0).astype(F32)
    for d, x in enumerate((x0, x1, x2, x3)):
        move = (row_index == slots[d]).astype(BF16)
        for i in range(3):
            sorted_ref[d, i] = dot(move, x[i * tok : (i + 1) * tok, :]).astype(BF16)
    offset = jnp.int32(0)
    info_row = lax.broadcasted_iota(jnp.int32, (16, HD), 0)
    info = jnp.zeros((16, HD), F32)
    for d in range(4):
        kept = kept_ref[d]
        info = jnp.where(info_row == d, kept.astype(F32), info)

        def put(u, carry, d=d, offset=offset, kept=kept):
            for i in range(3):
                send_ref[rows(i * half + (offset + u - kept) * unit, unit), :] = sorted_ref[d, i, rows(u * unit, unit), :]
            return carry

        lax.fori_loop(kept, tok // unit, put, 0)
        offset = offset + tok // unit - kept
    send_ref[3 * half :, :] = info.astype(BF16)


def pack_one_kernel(unit, slot_row, kept_ref, x0, x1, x2, x3, sorted_ref, send_ref):
    tok = x0.shape[0]
    row_index = lax.broadcasted_iota(jnp.int32, (tok, tok), 0).astype(F32)
    for d, x in enumerate((x0, x1, x2, x3)):
        move = (row_index == slot_row[d : d + 1, :]).astype(BF16)
        sorted_ref[d] = dot(move, x[...]).astype(BF16)
    offset = jnp.int32(0)
    for d in range(4):
        kept = kept_ref[d]

        def put(u, carry, d=d, offset=offset, kept=kept):
            send_ref[rows((offset + u - kept) * unit, unit), :] = sorted_ref[d, rows(u * unit, unit), :]
            return carry

        lax.fori_loop(kept, tok // unit, put, 0)
        offset = offset + tok // unit - kept


def each_unit(units, place, kept_ref, got_ref, own, got):
    first, side = place[0], place[1]
    pos = jnp.int32(0)
    for z in range(4):
        d = lax.rem(first - z + 4, 4)
        kept = kept_ref[d]
        came = units - got_ref[d]
        at = jnp.int32(0)
        for e in range(4):
            at = at + jnp.where(e < d, units - got_ref[e], 0)
        own_pos = pos + jnp.where(side == 0, 0, came)
        got_pos = pos + jnp.where(side == 0, kept, 0)

        def own_step(u, carry, d=d, own_pos=own_pos):
            own(d, u, own_pos + u)
            return carry

        def got_step(u, carry, at=at, got_pos=got_pos):
            got(at + u, got_pos + u)
            return carry

        lax.fori_loop(0, kept, own_step, 0)
        lax.fori_loop(0, came, got_step, 0)
        pos = pos + kept + came


def probs_kernel(unit, place, kept_ref, sorted_ref, came_ref, got_ref, q_ref, k_ref, v_ref, kt_ref, ot_ref, p_ref, vt, s_ref):
    tok = sorted_ref.shape[2]
    half = CS // 2
    info = came_ref[3 * half :, :].astype(F32)
    for d in range(4):
        got_ref[d] = jnp.max(info[d : d + 1, :]).astype(jnp.int32)
    outs = (q_ref, k_ref, v_ref)

    def own(d, u, to):
        for i in range(3):
            outs[i][rows(to * unit, unit), :] = sorted_ref[d, i, rows(u * unit, unit), :]

    def got(at, to):
        for i in range(3):
            outs[i][rows(to * unit, unit), :] = came_ref[rows(i * half + at * unit, unit), :]

    each_unit(tok // unit, place, kept_ref, got_ref, own, got)
    kt_ref[...] = k_ref[...].astype(F32).T.astype(BF16)
    vt[...] = v_ref[...].astype(F32).T.astype(BF16)
    factor = HD**-0.5
    low = lax.broadcasted_iota(jnp.int32, (QB, QB), 0) <= lax.broadcasted_iota(jnp.int32, (QB, QB), 1)
    for j in range(CS // QB):
        q = q_ref[j * QB : (j + 1) * QB, :]
        top = None
        for i in range(j + 1):
            s = dot_nt(k_ref[i * QB : (i + 1) * QB, :], q) * factor
            if i == j:
                s = jnp.where(low, s, -1e30)
            s_ref[i * QB : (i + 1) * QB, :] = s
            peak = jnp.max(s.reshape(QB // 8, 8, QB), axis=0)
            top = peak if top is None else jnp.maximum(top, peak)
        top = jnp.max(top, axis=0, keepdims=True)
        total = None
        for i in range(j + 1):
            w = jnp.exp(s_ref[i * QB : (i + 1) * QB, :] - top)
            s_ref[i * QB : (i + 1) * QB, :] = w
            part = jnp.sum(w.reshape(QB // 8, 8, QB), axis=0)
            total = part if total is None else total + part
        scale = 1.0 / jnp.sum(total, axis=0, keepdims=True)
        for i in range(j + 1):
            p_ref[i * QB : (i + 1) * QB, j * QB : (j + 1) * QB] = (s_ref[i * QB : (i + 1) * QB, :] * scale).astype(BF16)
        end = (j + 1) * QB
        ot_ref[:, j * QB : end] = dot(vt[:, :end], p_ref[:end, j * QB : end])


def grads_kernel(
    unit, place, kept_ref, got_ref, sorted_ref, came_ref, q_ref, k_ref, v_ref, kt_ref, ot_ref, p_hbm,
    own_ref, back_ref, g_ref, p_ref, dqt, res, sems,
):
    tok = sorted_ref.shape[1]
    half = CS // 2
    count = CS // QB
    copies = []
    for i in range(count):
        span = (slice(i * QB, (i + 1) * QB), slice(i * QB, CS))
        copy = pltpu.make_async_copy(p_hbm.at[span], p_ref.at[span], sems.at[i])
        copy.start()
        copies.append(copy)

    def own(d, u, to):
        g_ref[rows(to * unit, unit), :] = sorted_ref[d, rows(u * unit, unit), :]

    def got(at, to):
        g_ref[rows(to * unit, unit), :] = came_ref[rows(at * unit, unit), :]

    each_unit(tok // unit, place, kept_ref, got_ref, own, got)
    delta = jnp.sum(g_ref[...].astype(F32).T * ot_ref[...], axis=0, keepdims=True)
    factor = HD**-0.5
    for i in range(count):
        copies[i].wait()
        lo, hi = i * QB, (i + 1) * QB
        p = p_ref[lo:hi, lo:]
        g = g_ref[lo:, :]
        res[2, lo:hi, :] = dot(p, g).astype(BF16)
        dp = dot_nt(v_ref[lo:hi, :], g)
        ds = (p.astype(F32) * (dp - delta[:, lo:])).astype(BF16)
        res[1, lo:hi, :] = (dot(ds, q_ref[lo:, :]) * factor).astype(BF16)
        part = dot(kt_ref[:, lo:hi], ds)
        dqt[:, lo:] = part if i == 0 else dqt[:, lo:] + part
    res[0] = (dqt[...].T * factor).astype(BF16)

    def own_out(d, u, to):
        for i in range(3):
            own_ref[d, i, rows(u * unit, unit), :] = res[i, rows(to * unit, unit), :]

    def got_out(at, to):
        for i in range(3):
            back_ref[i, rows(at * unit, unit), :] = res[i, rows(to * unit, unit), :]

    each_unit(tok // unit, place, kept_ref, got_ref, own_out, got_out)


def unsort_kernel(unit, kept_ref, slot_col, own_ref, back_ref, y0, y1, y2, y3, full):
    tok = own_ref.shape[2]
    col_index = lax.broadcasted_iota(jnp.int32, (tok, tok), 1).astype(F32)
    offset = jnp.int32(0)
    for d, y in enumerate((y0, y1, y2, y3)):
        kept = kept_ref[d]

        def own(u, carry, d=d):
            for i in range(3):
                full[i, rows(u * unit, unit), :] = own_ref[d, i, rows(u * unit, unit), :]
            return carry

        def got(u, carry, offset=offset, kept=kept):
            for i in range(3):
                full[i, rows(u * unit, unit), :] = back_ref[i, rows((offset + u - kept) * unit, unit), :]
            return carry

        lax.fori_loop(0, kept, own, 0)
        lax.fori_loop(kept, tok // unit, got, 0)
        offset = offset + tok // unit - kept
        move = (col_index == slot_col[:, d : d + 1]).astype(BF16)
        for i in range(3):
            y[i] = dot(move, full[i]).astype(BF16)


def window_kernel(place, q_ref, k_ref, v_ref, g_ref, prior_ref, dq_ref, own_ref, carry_ref, keys, values, kt, dk, dv):
    tok = q_ref.shape[0]
    keys[:tok, :] = prior_ref[0]
    keys[tok:, :] = k_ref[...]
    values[:tok, :] = prior_ref[1]
    values[tok:, :] = v_ref[...]
    kt[...] = keys[...].astype(F32).T.astype(BF16)
    factor = HD**-0.5
    r = lax.broadcasted_iota(jnp.int32, (QB, QB), 0)
    c = lax.broadcasted_iota(jnp.int32, (QB, QB), 1)
    span = tok + QB
    edge = tok - (tok // QB - 1) * QB
    started = place[0] > 0
    for j in range(tok // QB):
        lo, hi = j * QB, j * QB + span
        q = q_ref[j * QB : (j + 1) * QB, :]
        g = g_ref[j * QB : (j + 1) * QB, :]
        s = dot_nt(keys[lo:hi, :], q) * factor
        first = jnp.where(r > c, s[:QB], -1e30)
        last = jnp.where(r <= c, s[span - QB :], -1e30)
        s = jnp.concatenate([first, s[QB : span - QB], last], axis=0)
        before = tok - lo
        s = jnp.concatenate([jnp.where(started, s[:before], -1e30), s[before:]], axis=0)
        top = jnp.max(s, axis=0, keepdims=True)
        w = jnp.exp(s - top)
        p = w * (1.0 / jnp.sum(w, axis=0, keepdims=True))
        dp = dot_nt(values[lo:hi, :], g)
        delta = jnp.sum(p * dp, axis=0, keepdims=True)
        pb = p.astype(BF16)
        ds = (p * (dp - delta)).astype(BF16)
        dq_ref[j * QB : (j + 1) * QB, :] = (dot(kt[:, lo:hi], ds).T * factor).astype(BF16)
        part_k = dot(ds, q) * factor
        part_v = dot(pb, g)
        if j == 0:
            dk[lo:hi, :] = part_k
            dv[lo:hi, :] = part_v
        else:
            dk[lo : hi - QB, :] = dk[lo : hi - QB, :] + part_k[:-QB]
            dv[lo : hi - QB, :] = dv[lo : hi - QB, :] + part_v[:-QB]
            dk[hi - QB : hi, :] = part_k[-QB:]
            dv[hi - QB : hi, :] = part_v[-QB:]
    carry_ref[0] = dk[:tok, :].astype(BF16)
    carry_ref[1] = dv[:tok, :].astype(BF16)
    own_ref[0] = dk[tok:, :]
    own_ref[1] = dv[tok:, :]


def join_kernel(place, y0, y1, y2, y3, local_dq, own_ref, carry_ref, dq_ref, dk_ref, dv_ref):
    outs = (dq_ref, dk_ref, dv_ref)
    for d, y in enumerate((y0, y1, y2, y3)):
        at = lax.rem(place[0] + d, 4) * HD
        for i in range(3):
            outs[i][:, pl.ds(pl.multiple_of(at, HD), HD)] = y[i]
    side = HR * HD
    dq_ref[:, side:] = local_dq[...]
    dk_ref[:, side:] = (own_ref[0] + carry_ref[0].astype(F32)).astype(BF16)
    dv_ref[:, side:] = (own_ref[1] + carry_ref[1].astype(F32)).astype(BF16)


def struct(*shape, dtype=BF16):
    return jax.ShapeDtypeStruct(shape, dtype)


def pair_body(query, key, value, grad_sent, out_weight, assign):
    tok = query.shape[1]
    devices = lax.axis_size("seq")
    place = lax.axis_index("seq")
    first, side = place // 2, place % 2
    where = jnp.stack([first, side]).astype(jnp.int32)
    unit = CS // (4 * devices)
    half = CS // 2

    def among_groups(block, shift):
        route = [(i, ((i // 2 + shift) % HR) * 2 + i % 2) for i in range(devices)]
        return lax.ppermute(block, "seq", route)

    def swap(block):
        return lax.ppermute(block, "seq", [(i, i ^ 1) for i in range(devices)])

    boundary = from_behind(grad_sent, "section", -1)[0]
    labels = assign[0].astype(BF16).reshape(HR, tok // HD, HD)
    labels = jnp.pad(labels, ((0, 0), (0, 16 - tok // HD), (0, 0)))

    def head_of(array, head):
        return lax.dynamic_slice_in_dim(array, head * HD, HD, 1)

    sent = []
    for d in range(HR):
        head = (first + d) % HR
        sent.append(
            jnp.concatenate(
                [head_of(query[0], head), head_of(key[0], head), head_of(value[0], head)]
                + [lax.dynamic_index_in_dim(labels, head, 0, keepdims=False)],
                axis=0,
            )
        )
    arrived = [sent[0]] + [among_groups(sent[d], d) for d in range(1, HR)]

    local = slice(HR * HD, (HR + HL) * HD)
    prior = shifted(jnp.stack([key[0][:, local], value[0][:, local]]), "seq", 1)

    attn_grad = lax.dot_general(
        boundary, out_weight[0], (((1,), (1,)), ((), ())), preferred_element_type=F32
    ).astype(BF16)
    g_sent = [head_of(attn_grad, (first + d) % HR) for d in range(HR)]
    g_arrived = [g_sent[0]] + [among_groups(g_sent[d], d) for d in range(1, HR)]

    ordered, send, slot_row, slot_col, kept = pl.pallas_call(
        functools.partial(pack_kernel, unit),
        out_shape=[
            struct(HR, 3, tok, HD),
            struct(3 * half + 16, HD),
            struct(8, tok, dtype=F32),
            struct(tok, HD, dtype=F32),
            struct(HR, dtype=jnp.int32),
        ],
        in_specs=smem() + vmem(4),
        out_specs=vmem(4) + smem(),
        compiler_params=params(32),
        name="pack",
    )(where, *arrived)
    came = swap(send)
    got, q, k, v, kt, ot, p = pl.pallas_call(
        functools.partial(probs_kernel, unit),
        out_shape=[struct(HR, dtype=jnp.int32)]
        + [struct(CS, HD)] * 3
        + [struct(HD, CS), struct(HD, CS, dtype=F32), struct(CS, CS)],
        in_specs=smem(2) + vmem(2),
        out_specs=smem() + vmem(6),
        scratch_shapes=[pltpu.VMEM((HD, CS), BF16), pltpu.VMEM((CS, QB), F32)],
        compiler_params=params(40),
        name="probs",
    )(where, kept, ordered, came)

    g_ordered, g_out = pl.pallas_call(
        functools.partial(pack_one_kernel, unit),
        out_shape=[struct(HR, tok, HD), struct(half, HD)],
        in_specs=vmem() + smem() + vmem(4),
        out_specs=vmem(2),
        compiler_params=params(32),
        name="pack_grad",
    )(slot_row, kept, *g_arrived)
    g_came = swap(g_out)

    own, back = pl.pallas_call(
        functools.partial(grads_kernel, unit),
        out_shape=[struct(HR, 3, tok, HD), struct(3, half, HD)],
        in_specs=smem(3) + vmem(7) + [pl.BlockSpec(memory_space=pl.ANY)],
        out_specs=vmem(2),
        scratch_shapes=[
            pltpu.VMEM((CS, HD), BF16),
            pltpu.VMEM((CS, CS), BF16),
            pltpu.VMEM((HD, CS), F32),
            pltpu.VMEM((3, CS, HD), BF16),
            pltpu.SemaphoreType.DMA((CS // QB,)),
        ],
        compiler_params=params(40),
        name="grads",
    )(where, kept, got, g_ordered, g_came, q, k, v, kt, ot, p)
    returned = swap(back)
    natural = pl.pallas_call(
        functools.partial(unsort_kernel, unit),
        out_shape=[struct(3, tok, HD)] * 4,
        in_specs=smem() + vmem(3),
        out_specs=vmem(4),
        scratch_shapes=[pltpu.VMEM((3, tok, HD), BF16)],
        compiler_params=params(32),
        name="unsort",
    )(kept, slot_col, own, returned)
    home = [natural[0]] + [among_groups(natural[d], -d) for d in range(1, HR)]

    local_dq, local_own, carry = pl.pallas_call(
        window_kernel,
        grid=(HL,),
        out_shape=[struct(tok, HL * HD), struct(2, tok, HL * HD, dtype=F32), struct(2, tok, HL * HD)],
        in_specs=smem()
        + [pl.BlockSpec((tok, HD), lambda h: (0, HR + h))] * 4
        + [pl.BlockSpec((2, tok, HD), lambda h: (0, 0, h))],
        out_specs=[
            pl.BlockSpec((tok, HD), lambda h: (0, h)),
            pl.BlockSpec((2, tok, HD), lambda h: (0, 0, h)),
            pl.BlockSpec((2, tok, HD), lambda h: (0, 0, h)),
        ],
        scratch_shapes=[
            pltpu.VMEM((2 * tok, HD), BF16),
            pltpu.VMEM((2 * tok, HD), BF16),
            pltpu.VMEM((HD, 2 * tok), BF16),
            pltpu.VMEM((2 * tok, HD), F32),
            pltpu.VMEM((2 * tok, HD), F32),
        ],
        compiler_params=params(32),
        name="window",
    )(place.astype(jnp.int32).reshape(1), query[0], key[0], value[0], attn_grad, prior)
    carried = shifted(carry, "seq", -1)

    outs = pl.pallas_call(
        join_kernel,
        out_shape=[struct(tok, (HR + HL) * HD)] * 3,
        in_specs=smem() + vmem(7),
        out_specs=vmem(3),
        compiler_params=params(32),
        name="join",
    )(where, *home, local_dq, local_own, carried)
    return tuple(out[None] for out in outs)


def from_behind(block, axis, distance):
    devices = range(lax.axis_size(axis))
    route = [((i - distance) % len(devices), i) for i in devices]
    return lax.ppermute(block, axis, route)


def shifted(block, axis, distance):
    devices = range(lax.axis_size(axis))
    route = [(i - distance, i) for i in devices if i - distance in devices]
    return lax.ppermute(block, axis, route)


def cluster_block(query_rows, key_rows, value_rows, grad_rows, allowed, factor):
    scores = jnp.dot(query_rows, key_rows.T, preferred_element_type=jnp.float32) * factor
    scores = jnp.where(allowed, scores, -1e30)
    highest = jnp.max(scores, axis=1, keepdims=True)
    weights = jnp.exp(scores - highest)
    probs = weights / jnp.sum(weights, axis=1, keepdims=True)
    dprob = jnp.dot(grad_rows, value_rows.T, preferred_element_type=jnp.float32)
    delta = jnp.sum(probs * dprob, axis=1, keepdims=True)
    dscore = probs * (dprob - delta)
    probs_b = probs.astype(jnp.bfloat16)
    dscore_b = dscore.astype(jnp.bfloat16)
    grad_query = jnp.dot(dscore_b, key_rows, preferred_element_type=jnp.float32) * factor
    grad_key = jnp.dot(dscore_b.T, query_rows, preferred_element_type=jnp.float32) * factor
    grad_value = jnp.dot(probs_b.T, grad_rows, preferred_element_type=jnp.float32)
    return (grad_query, grad_key, grad_value)


def cluster_grads(query_rows, key_rows, value_rows, grad_rows, factor):
    length = query_rows.shape[0]
    span = min(512, length)
    pieces = []
    total_key = jnp.zeros(key_rows.shape, jnp.float32)
    total_value = jnp.zeros(value_rows.shape, jnp.float32)
    for index in range(length // span):
        first = index * span
        end = first + span
        allowed = (
            jnp.arange(end, dtype=jnp.int32)[None, :]
            <= (first + jnp.arange(span, dtype=jnp.int32))[:, None]
        )
        part_query, part_key, part_value = cluster_block(
            query_rows[first:end],
            key_rows[:end],
            value_rows[:end],
            grad_rows[first:end],
            allowed,
            factor,
        )
        pieces.append(part_query)
        total_key = total_key.at[:end].add(part_key)
        total_value = total_value.at[:end].add(part_value)
    return (jnp.concatenate(pieces, axis=0), total_key, total_value)


def window_block(query_rows, key_rows, value_rows, grad_rows, allowed, factor):
    scores = (
        jnp.einsum("qhd,khd->hqk", query_rows, key_rows, preferred_element_type=jnp.float32)
        * factor
    )
    scores = jnp.where(allowed[None], scores, -1e30)
    highest = jnp.max(scores, axis=2, keepdims=True)
    weights = jnp.exp(scores - highest)
    probs = weights / jnp.sum(weights, axis=2, keepdims=True)
    dprob = jnp.einsum("qhd,khd->hqk", grad_rows, value_rows, preferred_element_type=jnp.float32)
    delta = jnp.sum(probs * dprob, axis=2, keepdims=True)
    dscore = probs * (dprob - delta)
    probs_b = probs.astype(jnp.bfloat16)
    dscore_b = dscore.astype(jnp.bfloat16)
    grad_query = (
        jnp.einsum("hqk,khd->qhd", dscore_b, key_rows, preferred_element_type=jnp.float32) * factor
    )
    grad_key = (
        jnp.einsum("hqk,qhd->khd", dscore_b, query_rows, preferred_element_type=jnp.float32)
        * factor
    )
    grad_value = jnp.einsum("hqk,qhd->khd", probs_b, grad_rows, preferred_element_type=jnp.float32)
    return (grad_query, grad_key, grad_value)


def window_mask(query_pos, key_pos):
    return (
        (key_pos[None, :] > query_pos[:, None] - WIN)
        & (key_pos[None, :] <= query_pos[:, None])
        & (key_pos[None, :] >= 0)
    )


def general_body(query, key, value, grad_sent, out_weight, assign):
    tok_rows = query.shape[1]
    heads = HR + HL
    devices = lax.axis_size("seq")
    place = lax.axis_index("seq")
    factor = HD ** (-0.5)
    boundary = from_behind(grad_sent, "section", -1)[0]
    attn_grad = lax.dot_general(
        boundary, out_weight[0], (((1,), (1,)), ((), ())), preferred_element_type=jnp.float32
    ).astype(jnp.bfloat16)
    query_heads = query[0].reshape(tok_rows, heads, HD)
    key_heads = key[0].reshape(tok_rows, heads, HD)
    value_heads = value[0].reshape(tok_rows, heads, HD)
    grad_heads = attn_grad.reshape(tok_rows, heads, HD)
    clusters = tok_rows * devices // CS
    owned = HR * tok_rows // CS
    capacity = 7 * CS // (4 * devices)
    unit_rows = capacity // 7
    width = owned * capacity
    head_slots = clusters * capacity
    labels = assign[0]
    members = (labels[:, :, None] == jnp.arange(clusters, dtype=jnp.int32)[None, None, :]).astype(
        jnp.bfloat16
    )
    token_ids = jnp.arange(tok_rows, dtype=jnp.int32)
    lower = (token_ids[:, None] >= token_ids[None, :]).astype(jnp.bfloat16)
    running_counts = jnp.einsum("ts,hsc->htc", lower, members, preferred_element_type=jnp.float32)
    ranks = (jnp.sum(running_counts * members.astype(jnp.float32), axis=2) - 1.0).astype(jnp.int32)
    local_slot = labels * capacity + ranks
    slot_hit = jnp.arange(head_slots, dtype=jnp.int32)[None, :, None] == local_slot[:, None, :]
    slot_table = slot_hit.astype(jnp.bfloat16)
    routed_in = jnp.concatenate(
        [query_heads[:, :HR], key_heads[:, :HR], value_heads[:, :HR], grad_heads[:, :HR]], axis=2
    )
    packed = jnp.einsum(
        "hst,thd->hsd", slot_table, routed_in, preferred_element_type=jnp.float32
    ).astype(jnp.bfloat16)
    packed = packed.reshape(devices, width, 4 * HD)
    token_pos = place * tok_rows + token_ids
    slot_pos = jnp.max(jnp.where(slot_hit, token_pos[None, None, :], -1), axis=2).reshape(
        devices, width
    )
    send_query = packed[:, :, :HD]
    send_key = packed[:, :, HD : 2 * HD]
    send_value = packed[:, :, 2 * HD : 3 * HD]
    send_grad = packed[:, :, 3 * HD :]
    arrived_query, arrived_key, arrived_value, arrived_grad, arrived_pos = (
        lax.all_to_all(send_query, "seq", split_axis=0, concat_axis=0, tiled=True),
        lax.all_to_all(send_key, "seq", split_axis=0, concat_axis=0, tiled=True),
        lax.all_to_all(send_value, "seq", split_axis=0, concat_axis=0, tiled=True),
        lax.all_to_all(send_grad, "seq", split_axis=0, concat_axis=0, tiled=True),
        lax.all_to_all(slot_pos, "seq", split_axis=0, concat_axis=0, tiled=True),
    )
    arrived_all = jnp.concatenate([arrived_query, arrived_key, arrived_value, arrived_grad], axis=2)
    unit_index = jnp.arange(7, dtype=jnp.int32)
    target_units = jnp.arange(CS // unit_rows, dtype=jnp.int32)
    block = arrived_all.reshape(devices * 7, unit_rows * 4 * HD)
    live_counts = jnp.sum((arrived_pos >= 0).astype(jnp.int32), axis=1)
    units = live_counts // unit_rows
    starts = jnp.cumsum(units) - units
    picker = (target_units[:, None, None] == starts[None, :, None] + unit_index[None, None, :]) & (
        unit_index[None, None, :] < units[None, :, None]
    )
    picker = picker.reshape(CS // unit_rows, devices * 7).astype(jnp.bfloat16)
    compact = (
        jnp.dot(picker, block, preferred_element_type=jnp.float32)
        .astype(jnp.bfloat16)
        .reshape(CS, 4 * HD)
    )
    results = cluster_grads(
        compact[:, :HD],
        compact[:, HD : 2 * HD],
        compact[:, 2 * HD : 3 * HD],
        compact[:, 3 * HD :],
        factor,
    )
    answer = jnp.concatenate([result.astype(jnp.bfloat16) for result in results], axis=1).reshape(
        CS // unit_rows, unit_rows * 3 * HD
    )
    spread = jnp.dot(picker.T, answer, preferred_element_type=jnp.float32).astype(jnp.bfloat16)
    outgoing = spread.reshape(devices, capacity, 3 * HD)
    back_query, back_key, back_value = (
        lax.all_to_all(outgoing[:, :, :HD], "seq", split_axis=0, concat_axis=0, tiled=True),
        lax.all_to_all(outgoing[:, :, HD : 2 * HD], "seq", split_axis=0, concat_axis=0, tiled=True),
        lax.all_to_all(outgoing[:, :, 2 * HD :], "seq", split_axis=0, concat_axis=0, tiled=True),
    )
    back_all = jnp.concatenate([back_query, back_key, back_value], axis=2).reshape(
        HR, head_slots, 3 * HD
    )
    routed_out = jnp.einsum(
        "hst,hsd->thd", slot_table, back_all, preferred_element_type=jnp.float32
    ).astype(jnp.bfloat16)
    routed_query = routed_out[:, :, :HD]
    routed_key = routed_out[:, :, HD : 2 * HD]
    routed_value = routed_out[:, :, 2 * HD :]
    local_query = query_heads[:, HR:]
    local_key = key_heads[:, HR:]
    local_value = value_heads[:, HR:]
    local_grad = grad_heads[:, HR:]
    prior_key, prior_value = shifted((local_key, local_value), "seq", 1)
    keys_all = jnp.concatenate([prior_key, local_key], axis=0)
    values_all = jnp.concatenate([prior_value, local_value], axis=0)
    key_positions = (place - 1) * tok_rows + jnp.arange(2 * tok_rows, dtype=jnp.int32)
    query_positions = place * tok_rows + jnp.arange(tok_rows, dtype=jnp.int32)
    span = min(512, tok_rows)
    total_key = jnp.zeros((2 * tok_rows, HL, HD), jnp.float32)
    total_value = jnp.zeros((2 * tok_rows, HL, HD), jnp.float32)
    start = tok_rows - WIN
    allowed = window_mask(query_positions, key_positions)
    part_query, part_key, part_value = window_block(
        local_query, keys_all, values_all, local_grad, allowed, factor
    )
    total_key = total_key.at[start : start + span + WIN].add(part_key)
    total_value = total_value.at[start : start + span + WIN].add(part_value)
    tail = tok_rows - WIN
    carried_key, carried_value = (
        shifted(total_key[tail:tok_rows].astype(jnp.bfloat16), "seq", -1).astype(jnp.float32),
        shifted(total_value[tail:tok_rows].astype(jnp.bfloat16), "seq", -1).astype(jnp.float32),
    )
    local_dk = total_key[tok_rows:].at[tail:].add(carried_key)
    local_dv = total_value[tok_rows:].at[tail:].add(carried_value)
    local_dq = part_query.astype(jnp.bfloat16)
    grad_query = jnp.concatenate([routed_query, local_dq], axis=1).reshape(1, tok_rows, heads * HD)
    grad_key = jnp.concatenate([routed_key, local_dk.astype(jnp.bfloat16)], axis=1).reshape(
        1, tok_rows, heads * HD
    )
    grad_value = jnp.concatenate([routed_value, local_dv.astype(jnp.bfloat16)], axis=1).reshape(
        1, tok_rows, heads * HD
    )
    return (grad_query, grad_key, grad_value)


def body(query, key, value, grad_sent, out_weight, assign):
    clusters = query.shape[1] * lax.axis_size("seq") // CS
    plan = pair_body if clusters == 2 else general_body
    return plan(query, key, value, grad_sent, out_weight, assign)


def solution(mesh):
    placed = (
        P("section", "seq", None),
        P("section", "seq", None),
        P("section", "seq", None),
        P("section", "seq", None),
        P("section", None, None),
        P("section", None, "seq"),
    )
    return jax.shard_map(
        body,
        mesh=mesh,
        in_specs=placed,
        out_specs=(P("section", "seq", None), P("section", "seq", None), P("section", "seq", None)),
        check_vma=False,
    )
```

```python
import functools

import jax
import jax.numpy as jnp
from jax import lax
from jax.experimental import pallas as pl
from jax.experimental.pallas import tpu as pltpu
from jax.sharding import PartitionSpec as P

HR = 4
HL = 4
HD = 128
CS = 2048
WIN = 512
QB = 256
MIB = 1024 * 1024
SPLIT_MIB = 56
NT = (((1,), (1,)), ((), ()))
F32 = jnp.float32
BF16 = jnp.bfloat16


def vmem(count=1):
    return [pl.BlockSpec(memory_space=pltpu.VMEM)] * count


def smem(count=1):
    return [pl.BlockSpec(memory_space=pltpu.SMEM)] * count


def params(mib):
    return pltpu.CompilerParams(vmem_limit_bytes=mib * MIB)


def dot(a, b):
    return jnp.dot(a, b, preferred_element_type=F32)


def dot_nt(a, b):
    return lax.dot_general(a, b, NT, preferred_element_type=F32)


def takes(microseconds):
    return pl.CostEstimate(
        flops=int(microseconds * 1.1e9), bytes_accessed=int(microseconds * 3.5e6), transcendentals=0
    )


def rows(start, size):
    return pl.ds(pl.multiple_of(start, size), size)


def start_all(copies):
    for copy in copies:
        copy.start()


def wait_all(copies):
    for copy in copies:
        copy.wait()


def head_columns(place, d):
    return pl.ds(pl.multiple_of(lax.rem(place[0] + d, HR) * HD, HD), HD)


def split_kernel(place, labels, q_hbm, k_hbm, v_hbm, x0, x1, x2, x3, own, send, held, sems):
    tok = q_hbm.shape[0]
    copies = [pltpu.make_async_copy(source, held.at[i], sems.at[i]) for i, source in enumerate((q_hbm, k_hbm, v_hbm))]
    start_all(copies)
    for d, x in enumerate((x0, x1, x2, x3)):
        line = labels[pl.ds(lax.rem(place[0] + d, HR), 1), :].astype(F32)
        parts = [line[:, r * HD : (r + 1) * HD] for r in range(tok // HD)]
        parts.append(jnp.zeros((16 - tok // HD, HD), F32))
        x[2 * tok :, :] = jnp.concatenate(parts, axis=0).astype(BF16)
    width = HL * HD // 2
    for i in range(3):
        copies[i].wait()
        for d, x in enumerate((x0, x1, x2, x3)):
            if i < 2:
                x[i * tok : (i + 1) * tok, :] = held[i, :, head_columns(place, d)]
        for out, side in ((send, 1 - place[1]), (own, place[1])):
            out[i] = held[i, :, pl.ds(pl.multiple_of(HR * HD + side * width, width), width)]


def split_value_kernel(place, _after1, _after2, _after3, v_ref, x0, x1, x2, x3):
    for d, x in enumerate((x0, x1, x2, x3)):
        x[...] = v_ref[:, head_columns(place, d)]


def project_kernel(place, _after, _after_local, rows_ref, weight, g0, g1, g2, g3, own_ref, send_ref):
    step = pl.program_id(0)
    part = dot_nt(rows_ref[...], weight[...]).astype(BF16)

    @pl.when(step < HR // 2)
    def _():
        for i in range(2):
            d = lax.rem(2 * step + i - place[0] + 4, 4)
            for e, g in enumerate((g0, g1, g2, g3)):

                @pl.when(d == e)
                def _(g=g, i=i):
                    g[...] = part[:, i * HD : (i + 1) * HD]

    @pl.when(step >= HR // 2)
    def _():
        @pl.when(step - HR // 2 == place[1])
        def _():
            own_ref[...] = part

        @pl.when(step - HR // 2 != place[1])
        def _():
            send_ref[...] = part


def edge_kernel(place, _after, own, got, out):
    @pl.when(place[1] == 1)
    def _():
        out[...] = own[1:]

    @pl.when(place[1] == 0)
    def _():
        out[...] = got[1:]


def pack_kernel(unit, place, _after, x0, x1, x2, x3, sorted_ref, send_ref, slot_row, slot_col, kept_ref):
    tok = x0.shape[0] - 16
    tok = tok // 2
    side = place[1]
    lane = lax.broadcasted_iota(jnp.int32, (1, tok), 1).astype(F32)
    labels = []
    for x in (x0, x1, x2, x3):
        block = x[2 * tok :, :].astype(F32)
        labels.append(jnp.concatenate([block[r : r + 1, :] for r in range(tok // 128)], axis=1))
    label = jnp.concatenate(labels + [jnp.zeros((4, tok), F32)], axis=0)
    upper = (
        lax.broadcasted_iota(jnp.int32, (tok, tok), 0) <= lax.broadcasted_iota(jnp.int32, (tok, tok), 1)
    ).astype(BF16)
    ones = dot(label.astype(BF16), upper)
    totals = [jnp.sum(row).astype(jnp.int32) for row in labels]
    whole = totals[0] + totals[1] + totals[2] + totals[3]
    half = CS // 2
    keep_one = jnp.where(side == 0, (whole > half).astype(jnp.int32), (whole >= half).astype(jnp.int32))
    keep_f = keep_one.astype(F32)
    slots = []
    for d in range(4):
        kept = jnp.where(keep_one == 1, totals[d], tok - totals[d])
        kept_ref[d] = kept // unit
        is_kept = labels[d] * keep_f + (1.0 - labels[d]) * (1.0 - keep_f)
        ones_d = ones[d : d + 1, :]
        count = ones_d * keep_f + (lane + 1.0 - ones_d) * (1.0 - keep_f)
        slot = jnp.where(is_kept > 0.5, count - 1.0, kept.astype(F32) + lane - count)
        slots.append(slot)
    slots_all = jnp.concatenate(slots + [jnp.zeros((124, tok), F32)], axis=0)
    slot_row[...] = slots_all[:8, :]
    slot_col[...] = slots_all.T
    row_index = lax.broadcasted_iota(jnp.int32, (tok, tok), 0).astype(F32)
    for d, x in enumerate((x0, x1, x2, x3)):
        move = (row_index == slots[d]).astype(BF16)
        for i in range(2):
            sorted_ref[d, i] = dot(move, x[i * tok : (i + 1) * tok, :]).astype(BF16)
    offset = jnp.int32(0)
    info_row = lax.broadcasted_iota(jnp.int32, (16, HD), 0)
    info = jnp.zeros((16, HD), F32)
    for d in range(4):
        kept = kept_ref[d]
        info = jnp.where(info_row == d, kept.astype(F32), info)

        def put(u, carry, d=d, offset=offset, kept=kept):
            for i in range(2):
                send_ref[rows(i * half + (offset + u - kept) * unit, unit), :] = sorted_ref[d, i, rows(u * unit, unit), :]
            return carry

        lax.fori_loop(kept, tok // unit, put, 0)
        offset = offset + tok // unit - kept
    send_ref[2 * half :, :] = info.astype(BF16)


def pack_one_kernel(unit, kept_ref, _after, slot_row, x0, x1, x2, x3, sorted_ref, send_ref):
    tok = x0.shape[0]
    row_index = lax.broadcasted_iota(jnp.int32, (tok, tok), 0).astype(F32)
    for d, x in enumerate((x0, x1, x2, x3)):
        move = (row_index == slot_row[d : d + 1, :]).astype(BF16)
        sorted_ref[d] = dot(move, x[...]).astype(BF16)
    offset = jnp.int32(0)
    for d in range(4):
        kept = kept_ref[d]

        def put(u, carry, d=d, offset=offset, kept=kept):
            send_ref[rows((offset + u - kept) * unit, unit), :] = sorted_ref[d, rows(u * unit, unit), :]
            return carry

        lax.fori_loop(kept, tok // unit, put, 0)
        offset = offset + tok // unit - kept


def each_unit(units, place, kept_ref, got_ref, own, got):
    first, side = place[0], place[1]
    pos = jnp.int32(0)
    for z in range(4):
        d = lax.rem(first - z + 4, 4)
        kept = kept_ref[d]
        came = units - got_ref[d]
        at = jnp.int32(0)
        for e in range(4):
            at = at + jnp.where(e < d, units - got_ref[e], 0)
        own_pos = pos + jnp.where(side == 0, 0, came)
        got_pos = pos + jnp.where(side == 0, kept, 0)

        def own_step(u, carry, d=d, own_pos=own_pos):
            own(d, u, own_pos + u)
            return carry

        def got_step(u, carry, at=at, got_pos=got_pos):
            got(at + u, got_pos + u)
            return carry

        lax.fori_loop(0, kept, own_step, 0)
        lax.fori_loop(0, came, got_step, 0)
        pos = pos + kept + came


def probs_kernel(unit, place, kept_ref, _after, sorted_ref, came_ref, got_ref, q_ref, k_ref, kt_ref, p_ref, s_ref):
    tok = sorted_ref.shape[2]
    half = CS // 2
    info = came_ref[2 * half :, :].astype(F32)
    for d in range(4):
        got_ref[d] = jnp.max(info[d : d + 1, :]).astype(jnp.int32)
    outs = (q_ref, k_ref)

    def own(d, u, to):
        for i in range(2):
            outs[i][rows(to * unit, unit), :] = sorted_ref[d, i, rows(u * unit, unit), :]

    def got(at, to):
        for i in range(2):
            outs[i][rows(to * unit, unit), :] = came_ref[rows(i * half + at * unit, unit), :]

    each_unit(tok // unit, place, kept_ref, got_ref, own, got)
    kt_ref[...] = k_ref[...].astype(F32).T.astype(BF16)
    factor = HD**-0.5
    low = lax.broadcasted_iota(jnp.int32, (QB, QB), 0) <= lax.broadcasted_iota(jnp.int32, (QB, QB), 1)
    for j in range(CS // QB):
        q = q_ref[j * QB : (j + 1) * QB, :]
        top = None
        for i in range(j + 1):
            s = dot_nt(k_ref[i * QB : (i + 1) * QB, :], q) * factor
            if i == j:
                s = jnp.where(low, s, -1e30)
            s_ref[i * QB : (i + 1) * QB, :] = s
            peak = jnp.max(s.reshape(QB // 8, 8, QB), axis=0)
            top = peak if top is None else jnp.maximum(top, peak)
        top = jnp.max(top, axis=0, keepdims=True)
        total = None
        for i in range(j + 1):
            w = jnp.exp(s_ref[i * QB : (i + 1) * QB, :] - top)
            s_ref[i * QB : (i + 1) * QB, :] = w
            part = jnp.sum(w.reshape(QB // 8, 8, QB), axis=0)
            total = part if total is None else total + part
        scale = 1.0 / jnp.sum(total, axis=0, keepdims=True)
        for i in range(j + 1):
            p_ref[i * QB : (i + 1) * QB, j * QB : (j + 1) * QB] = (s_ref[i * QB : (i + 1) * QB, :] * scale).astype(BF16)


def mix_kernel(unit, place, kept_ref, got_ref, _after, sorted_ref, came_ref, p_ref, v_ref, ot_ref, vt):
    def own(d, u, to):
        v_ref[rows(to * unit, unit), :] = sorted_ref[d, rows(u * unit, unit), :]

    def got(at, to):
        v_ref[rows(to * unit, unit), :] = came_ref[rows(at * unit, unit), :]

    each_unit(sorted_ref.shape[1] // unit, place, kept_ref, got_ref, own, got)
    vt[...] = v_ref[...].astype(F32).T.astype(BF16)
    for j in range(CS // QB):
        end = (j + 1) * QB
        ot_ref[:, j * QB : end] = dot(vt[:, :end], p_ref[:end, j * QB : end])


def grads_kernel(
    unit, place, kept_ref, got_ref, sorted_ref, came_ref, q_ref, k_ref, v_ref, kt_ref, ot_ref, p_ref,
    own_v, back_v, own_ref, back_ref, g_ref, dqt, res,
):
    tok = sorted_ref.shape[1]
    half = CS // 2
    count = CS // QB
    def own(d, u, to):
        g_ref[rows(to * unit, unit), :] = sorted_ref[d, rows(u * unit, unit), :]

    def got(at, to):
        g_ref[rows(to * unit, unit), :] = came_ref[rows(at * unit, unit), :]

    each_unit(tok // unit, place, kept_ref, got_ref, own, got)
    delta = jnp.sum(g_ref[...].astype(F32).T * ot_ref[...], axis=0, keepdims=True)
    factor = HD**-0.5
    for i in range(count):
        lo, hi = i * QB, (i + 1) * QB
        p = p_ref[lo:hi, lo:]
        g = g_ref[lo:, :]
        res[2, lo:hi, :] = dot(p, g).astype(BF16)
        dp = dot_nt(v_ref[lo:hi, :], g)
        ds = (p.astype(F32) * (dp - delta[:, lo:])).astype(BF16)
        res[1, lo:hi, :] = (dot(ds, q_ref[lo:, :]) * factor).astype(BF16)
        part = dot(kt_ref[:, lo:hi], ds)
        dqt[:, lo:] = part if i == 0 else dqt[:, lo:] + part
    res[0] = (dqt[...].T * factor).astype(BF16)

    def own_out(d, u, to):
        own_v[d, 0, rows(u * unit, unit), :] = res[2, rows(to * unit, unit), :]
        for i in range(2):
            own_ref[d, i, rows(u * unit, unit), :] = res[i, rows(to * unit, unit), :]

    def got_out(at, to):
        back_v[0, rows(at * unit, unit), :] = res[2, rows(to * unit, unit), :]
        for i in range(2):
            back_ref[i, rows(at * unit, unit), :] = res[i, rows(to * unit, unit), :]

    each_unit(tok // unit, place, kept_ref, got_ref, own_out, got_out)


def unsort_kernel(unit, kept_ref, _after, slot_col, own_ref, back_ref, y0, y1, y2, y3, full):
    tok = own_ref.shape[2]
    col_index = lax.broadcasted_iota(jnp.int32, (tok, tok), 1).astype(F32)
    offset = jnp.int32(0)
    for d, y in enumerate((y0, y1, y2, y3)):
        kept = kept_ref[d]

        def own(u, carry, d=d):
            for i in range(full.shape[0]):
                full[i, rows(u * unit, unit), :] = own_ref[d, i, rows(u * unit, unit), :]
            return carry

        def got(u, carry, offset=offset, kept=kept):
            for i in range(full.shape[0]):
                full[i, rows(u * unit, unit), :] = back_ref[i, rows((offset + u - kept) * unit, unit), :]
            return carry

        lax.fori_loop(0, kept, own, 0)
        lax.fori_loop(kept, tok // unit, got, 0)
        offset = offset + tok // unit - kept
        move = (col_index == slot_col[:, d : d + 1]).astype(BF16)
        for i in range(full.shape[0]):
            y[i] = dot(move, full[i]).astype(BF16)


def window_kernel(
    place, _after, own, got, g_own, g_got, edge, dq_ref, early_ref, late_ref, carry_ref, *scratch
):
    tok = own.shape[1]
    pair = 2 * tok
    factor = HD**-0.5
    r = lax.broadcasted_iota(jnp.int32, (QB, QB), 0)
    c = lax.broadcasted_iota(jnp.int32, (QB, QB), 1)
    span = WIN + QB
    started = place[0] > 0
    own_at, got_at = place[1] * tok, (1 - place[1]) * tok
    for h in range(HL // 2):
        part = slice(h * HD, (h + 1) * HD)
        queries, grads, keys, values, kt, dk, dv = (ref.at[h] for ref in scratch)
        for at, block, g_block in ((own_at, own, g_own), (got_at, got, g_got)):
            queries[rows(at, tok), :] = block[0, :, part]
            grads[rows(at, tok), :] = g_block[:, part]
            keys[rows(at + WIN, tok), :] = block[1, :, part]
            values[rows(at + WIN, tok), :] = block[2, :, part]
        keys[:WIN, :] = edge[0, :, part]
        values[:WIN, :] = edge[1, :, part]
        kt[...] = keys[...].astype(F32).T.astype(BF16)
        for j in range(pair // QB):
            lo, hi = j * QB, j * QB + span
            q = queries[j * QB : (j + 1) * QB, :]
            g = grads[j * QB : (j + 1) * QB, :]
            s = dot_nt(keys[lo:hi, :], q) * factor
            first = jnp.where(r > c, s[:QB], -1e30)
            last = jnp.where(r <= c, s[span - QB :], -1e30)
            s = jnp.concatenate([first, s[QB : span - QB], last], axis=0)
            if lo < WIN:
                s = jnp.concatenate([jnp.where(started, s[: WIN - lo], -1e30), s[WIN - lo :]], axis=0)
            top = jnp.max(s, axis=0, keepdims=True)
            w = jnp.exp(s - top)
            p = w * (1.0 / jnp.sum(w, axis=0, keepdims=True))
            dp = dot_nt(values[lo:hi, :], g)
            delta = jnp.sum(p * dp, axis=0, keepdims=True)
            pb = p.astype(BF16)
            ds = (p * (dp - delta)).astype(BF16)
            side, at = divmod(j * QB, tok)
            dq_ref[side, at : at + QB, part] = (dot(kt[:, lo:hi], ds).T * factor).astype(BF16)
            part_k = dot(ds, q) * factor
            part_v = dot(pb, g)
            if j == 0:
                dk[lo:hi, :] = part_k
                dv[lo:hi, :] = part_v
            else:
                dk[lo : hi - QB, :] = dk[lo : hi - QB, :] + part_k[:-QB]
                dv[lo : hi - QB, :] = dv[lo : hi - QB, :] + part_v[:-QB]
                dk[hi - QB : hi, :] = part_k[-QB:]
                dv[hi - QB : hi, :] = part_v[-QB:]
        for i, total in enumerate((dk, dv)):
            carry_ref[i, :, part] = total[:WIN, :].astype(BF16)
            early_ref[i, :, part] = total[WIN : WIN + tok, :].astype(BF16)
            late_ref[i, :, part] = total[WIN + tok :, :]


def settle_kernel(place, _after, dq_ref, early_ref, late_ref, carry_ref, own, send):
    late = (late_ref[...] + carry_ref[...].astype(F32)).astype(BF16)
    for side, (near, far) in enumerate(((own, send), (send, own))):

        @pl.when(place[1] == side)
        def _(near=near, far=far):
            near[0] = dq_ref[0]
            near[1:] = early_ref[...]
            far[0] = dq_ref[1]
            far[1:] = late


def join_value_kernel(place, _after, v0, v1, v2, v3, out):
    for d, v in enumerate((v0, v1, v2, v3)):
        out[:, head_columns(place, d)] = v[0]


def join_kernel(place, value_ref, y0, y1, y2, y3, own, got, dq_ref, dk_ref, dv_ref):
    outs = (dq_ref, dk_ref, dv_ref)
    dv_ref[:, : HR * HD] = value_ref[...]
    for d, y in enumerate((y0, y1, y2, y3)):
        at = head_columns(place, d)
        for i in range(2):
            outs[i][:, at] = y[i]
    width = HL * HD // 2
    for block, side in ((own, place[1]), (got, 1 - place[1])):
        at = pl.ds(pl.multiple_of(HR * HD + side * width, width), width)
        for i in range(3):
            outs[i][:, at] = block[i]


def struct(*shape, dtype=BF16):
    return jax.ShapeDtypeStruct(shape, dtype)


def pair_body(query, key, value, grad_sent, out_weight, assign):
    tok = query.shape[1]
    devices = lax.axis_size("seq")
    place = lax.axis_index("seq")
    first, side = place // 2, place % 2
    where = jnp.stack([first, side]).astype(jnp.int32)
    unit = CS // (4 * devices)
    half = CS // 2

    def among_groups(block, shift):
        route = [(i, ((i // 2 + shift) % HR) * 2 + i % 2) for i in range(devices)]
        return lax.ppermute(block, "seq", route)

    def swap(block):
        return lax.ppermute(block, "seq", [(i, i ^ 1) for i in range(devices)])

    hbm = [pl.BlockSpec(memory_space=pltpu.HBM)]
    width = HL * HD // 2
    boundary = from_behind(grad_sent, "section", -1)[0]
    *sent, local_own, local_send = pl.pallas_call(
        split_kernel,
        out_shape=[struct(2 * tok + 16, HD)] * HR + [struct(3, tok, width)] * 2,
        in_specs=smem() + vmem() + hbm * 3,
        out_specs=vmem(6),
        scratch_shapes=[pltpu.VMEM((3, tok, query.shape[2]), BF16), pltpu.SemaphoreType.DMA((3,))],
        compiler_params=params(SPLIT_MIB),
        cost_estimate=takes(2),
        name="split",
    )(where, assign[0], query[0], key[0], value[0])
    arrived = [sent[0]] + [among_groups(sent[d], d) for d in range(1, HR)]
    local_got = swap(local_send)
    v_sent = pl.pallas_call(
        split_value_kernel,
        out_shape=[struct(tok, HD)] * HR,
        in_specs=smem() + vmem(4),
        out_specs=vmem(4),
        compiler_params=params(20),
        cost_estimate=takes(1),
        name="split_value",
    )(where, *arrived[1:], value[0])
    v_arrived = [v_sent[0]] + [among_groups(v_sent[d], d) for d in range(1, HR)]

    ordered, send, slot_row, slot_col, kept = pl.pallas_call(
        functools.partial(pack_kernel, unit),
        out_shape=[
            struct(HR, 2, tok, HD),
            struct(2 * half + 16, HD),
            struct(8, tok, dtype=F32),
            struct(tok, HD, dtype=F32),
            struct(HR, dtype=jnp.int32),
        ],
        in_specs=smem() + vmem(5),
        out_specs=vmem(4) + smem(),
        compiler_params=params(32),
        cost_estimate=takes(2.6),
        name="pack",
    )(where, v_sent[0], *arrived)
    came = swap(send)

    *g_sent, g_own, g_send = pl.pallas_call(
        project_kernel,
        grid=(4,),
        out_shape=[struct(tok, HD)] * HR + [struct(tok, width)] * 2,
        in_specs=smem()
        + [
            pl.BlockSpec((16, HD), lambda n: (0, 0)),
            pl.BlockSpec((1, 16, HD), lambda n: (0, 0, 0)),
            pl.BlockSpec(boundary.shape, lambda n: (0, 0)),
            pl.BlockSpec((2 * HD, boundary.shape[1]), lambda n: (n, 0)),
        ],
        out_specs=[pl.BlockSpec((tok, HD), lambda n: (0, 0))] * HR
        + [pl.BlockSpec((tok, width), lambda n: (0, 0))] * 2,
        compiler_params=params(32),
        cost_estimate=takes(3.8),
        name="project",
    )(where, send, local_got, boundary, out_weight[0])
    g_arrived = [g_sent[0]] + [among_groups(g_sent[d], d) for d in range(1, HR)]

    def pack_one(after, blocks, name):
        return pl.pallas_call(
            functools.partial(pack_one_kernel, unit),
            out_shape=[struct(HR, tok, HD), struct(half, HD)],
            in_specs=smem() + vmem(6),
            out_specs=vmem(2),
            compiler_params=params(20),
            cost_estimate=takes(1.4),
            name=name,
        )(kept, after, slot_row, *blocks)

    v_ordered, v_out = pack_one(g_sent[0], v_arrived, "pack_value")
    v_came = swap(v_out)

    got, q, k, kt, p = pl.pallas_call(
        functools.partial(probs_kernel, unit),
        out_shape=[struct(HR, dtype=jnp.int32)] + [struct(CS, HD)] * 2 + [struct(HD, CS), struct(CS, CS)],
        in_specs=smem(2) + vmem(3),
        out_specs=smem() + vmem(4),
        scratch_shapes=[pltpu.VMEM((CS, QB), F32)],
        compiler_params=params(24),
        cost_estimate=takes(5),
        name="probs",
    )(where, kept, v_out, ordered, came)

    g_ordered, g_out = pack_one(kt, g_arrived, "pack_grad")
    g_came = swap(g_out)

    edge = pl.pallas_call(
        edge_kernel,
        out_shape=struct(2, tok, width),
        in_specs=smem() + vmem(3),
        out_specs=vmem()[0],
        compiler_params=params(16),
        cost_estimate=takes(0.6),
        name="edge",
    )(where, g_out, local_own, local_got)
    edge_got = lax.ppermute(edge, "seq", [(i, i + 2) for i in range(devices - 2)])
    g_got = swap(g_send)

    v, ot = pl.pallas_call(
        functools.partial(mix_kernel, unit),
        out_shape=[struct(CS, HD), struct(HD, CS, dtype=F32)],
        in_specs=smem(3) + vmem(4),
        out_specs=vmem(2),
        scratch_shapes=[pltpu.VMEM((HD, CS), BF16)],
        compiler_params=params(20),
        cost_estimate=takes(1.7),
        name="mix",
    )(where, kept, got, edge, v_ordered, v_came, p)

    own_v, back_v, own, back = pl.pallas_call(
        functools.partial(grads_kernel, unit),
        out_shape=[struct(HR, 1, tok, HD), struct(1, half, HD), struct(HR, 2, tok, HD), struct(2, half, HD)],
        in_specs=smem(3) + vmem(8),
        out_specs=vmem(4),
        scratch_shapes=[
            pltpu.VMEM((CS, HD), BF16),
            pltpu.VMEM((HD, CS), F32),
            pltpu.VMEM((3, CS, HD), BF16),
        ],
        compiler_params=params(24),
        cost_estimate=takes(6.3),
        name="grads",
    )(where, kept, got, g_ordered, g_came, q, k, v, kt, ot, p)

    def bring_home(after, own, back, name):
        count = own.shape[1]
        returned = swap(back)
        natural = pl.pallas_call(
            functools.partial(unsort_kernel, unit),
            out_shape=[struct(count, tok, HD)] * HR,
            in_specs=smem() + vmem(4),
            out_specs=vmem(4),
            scratch_shapes=[pltpu.VMEM((count, tok, HD), BF16)],
            compiler_params=params(32),
        cost_estimate=takes(2),
            name=name,
        )(kept, after, slot_col, own, returned)
        return [natural[0]] + [among_groups(natural[d], -d) for d in range(1, HR)]

    pair = 2 * tok
    dq_local, early, late, carry = pl.pallas_call(
        window_kernel,
        out_shape=[
            struct(2, tok, width),
            struct(2, tok, width),
            struct(2, tok, width, dtype=F32),
            struct(2, tok, width),
        ],
        in_specs=smem() + vmem(6),
        out_specs=vmem(4),
        scratch_shapes=[
            pltpu.VMEM((HL // 2, pair, HD), BF16),
            pltpu.VMEM((HL // 2, pair, HD), BF16),
            pltpu.VMEM((HL // 2, pair + WIN, HD), BF16),
            pltpu.VMEM((HL // 2, pair + WIN, HD), BF16),
            pltpu.VMEM((HL // 2, HD, pair + WIN), BF16),
            pltpu.VMEM((HL // 2, pair + WIN, HD), F32),
            pltpu.VMEM((HL // 2, pair + WIN, HD), F32),
        ],
        compiler_params=params(24),
        cost_estimate=takes(7.8),
        name="window",
    )(where, back_v, local_own, local_got, g_own, g_got, edge_got)
    carry_got = lax.ppermute(carry, "seq", [(i + 2, i) for i in range(devices - 2)])
    home_v = bring_home(carry, own_v, back_v, "unsort_value")
    home = bring_home(home_v[0], own, back, "unsort_query_key")
    settled_own, settled_send = pl.pallas_call(
        settle_kernel,
        out_shape=[struct(3, tok, width)] * 2,
        in_specs=smem() + vmem(5),
        out_specs=vmem(2),
        compiler_params=params(16),
        cost_estimate=takes(0.8),
        name="settle",
    )(where, home[0], dq_local, early, late, carry_got)
    settled_got = swap(settled_send)
    value_left = pl.pallas_call(
        join_value_kernel,
        out_shape=struct(tok, HR * HD),
        in_specs=smem() + vmem(5),
        out_specs=vmem()[0],
        compiler_params=params(16),
        cost_estimate=takes(0.7),
        name="join_value",
    )(where, settled_send, *home_v)

    outs = pl.pallas_call(
        join_kernel,
        out_shape=[struct(tok, (HR + HL) * HD)] * 3,
        in_specs=smem() + vmem(7),
        out_specs=vmem(3),
        compiler_params=params(32),
        cost_estimate=takes(2.8),
        name="join",
    )(where, value_left, *home, settled_own, settled_got)
    return tuple(out[None] for out in outs)


def from_behind(block, axis, distance):
    devices = range(lax.axis_size(axis))
    route = [((i - distance) % len(devices), i) for i in devices]
    return lax.ppermute(block, axis, route)


def shifted(block, axis, distance):
    devices = range(lax.axis_size(axis))
    route = [(i - distance, i) for i in devices if i - distance in devices]
    return lax.ppermute(block, axis, route)


def cluster_block(query_rows, key_rows, value_rows, grad_rows, allowed, factor):
    scores = jnp.dot(query_rows, key_rows.T, preferred_element_type=jnp.float32) * factor
    scores = jnp.where(allowed, scores, -1e30)
    highest = jnp.max(scores, axis=1, keepdims=True)
    weights = jnp.exp(scores - highest)
    probs = weights / jnp.sum(weights, axis=1, keepdims=True)
    dprob = jnp.dot(grad_rows, value_rows.T, preferred_element_type=jnp.float32)
    delta = jnp.sum(probs * dprob, axis=1, keepdims=True)
    dscore = probs * (dprob - delta)
    probs_b = probs.astype(jnp.bfloat16)
    dscore_b = dscore.astype(jnp.bfloat16)
    grad_query = jnp.dot(dscore_b, key_rows, preferred_element_type=jnp.float32) * factor
    grad_key = jnp.dot(dscore_b.T, query_rows, preferred_element_type=jnp.float32) * factor
    grad_value = jnp.dot(probs_b.T, grad_rows, preferred_element_type=jnp.float32)
    return (grad_query, grad_key, grad_value)


def cluster_grads(query_rows, key_rows, value_rows, grad_rows, factor):
    length = query_rows.shape[0]
    span = min(512, length)
    pieces = []
    total_key = jnp.zeros(key_rows.shape, jnp.float32)
    total_value = jnp.zeros(value_rows.shape, jnp.float32)
    for index in range(length // span):
        first = index * span
        end = first + span
        allowed = (
            jnp.arange(end, dtype=jnp.int32)[None, :]
            <= (first + jnp.arange(span, dtype=jnp.int32))[:, None]
        )
        part_query, part_key, part_value = cluster_block(
            query_rows[first:end],
            key_rows[:end],
            value_rows[:end],
            grad_rows[first:end],
            allowed,
            factor,
        )
        pieces.append(part_query)
        total_key = total_key.at[:end].add(part_key)
        total_value = total_value.at[:end].add(part_value)
    return (jnp.concatenate(pieces, axis=0), total_key, total_value)


def window_block(query_rows, key_rows, value_rows, grad_rows, allowed, factor):
    scores = (
        jnp.einsum("qhd,khd->hqk", query_rows, key_rows, preferred_element_type=jnp.float32)
        * factor
    )
    scores = jnp.where(allowed[None], scores, -1e30)
    highest = jnp.max(scores, axis=2, keepdims=True)
    weights = jnp.exp(scores - highest)
    probs = weights / jnp.sum(weights, axis=2, keepdims=True)
    dprob = jnp.einsum("qhd,khd->hqk", grad_rows, value_rows, preferred_element_type=jnp.float32)
    delta = jnp.sum(probs * dprob, axis=2, keepdims=True)
    dscore = probs * (dprob - delta)
    probs_b = probs.astype(jnp.bfloat16)
    dscore_b = dscore.astype(jnp.bfloat16)
    grad_query = (
        jnp.einsum("hqk,khd->qhd", dscore_b, key_rows, preferred_element_type=jnp.float32) * factor
    )
    grad_key = (
        jnp.einsum("hqk,qhd->khd", dscore_b, query_rows, preferred_element_type=jnp.float32)
        * factor
    )
    grad_value = jnp.einsum("hqk,qhd->khd", probs_b, grad_rows, preferred_element_type=jnp.float32)
    return (grad_query, grad_key, grad_value)


def window_mask(query_pos, key_pos):
    return (
        (key_pos[None, :] > query_pos[:, None] - WIN)
        & (key_pos[None, :] <= query_pos[:, None])
        & (key_pos[None, :] >= 0)
    )


def general_body(query, key, value, grad_sent, out_weight, assign):
    tok_rows = query.shape[1]
    heads = HR + HL
    devices = lax.axis_size("seq")
    place = lax.axis_index("seq")
    factor = HD ** (-0.5)
    boundary = from_behind(grad_sent, "section", -1)[0]
    attn_grad = lax.dot_general(
        boundary, out_weight[0], (((1,), (1,)), ((), ())), preferred_element_type=jnp.float32
    ).astype(jnp.bfloat16)
    query_heads = query[0].reshape(tok_rows, heads, HD)
    key_heads = key[0].reshape(tok_rows, heads, HD)
    value_heads = value[0].reshape(tok_rows, heads, HD)
    grad_heads = attn_grad.reshape(tok_rows, heads, HD)
    clusters = tok_rows * devices // CS
    owned = HR * tok_rows // CS
    capacity = 7 * CS // (4 * devices)
    unit_rows = capacity // 7
    width = owned * capacity
    head_slots = clusters * capacity
    labels = assign[0]
    members = (labels[:, :, None] == jnp.arange(clusters, dtype=jnp.int32)[None, None, :]).astype(
        jnp.bfloat16
    )
    token_ids = jnp.arange(tok_rows, dtype=jnp.int32)
    lower = (token_ids[:, None] >= token_ids[None, :]).astype(jnp.bfloat16)
    running_counts = jnp.einsum("ts,hsc->htc", lower, members, preferred_element_type=jnp.float32)
    ranks = (jnp.sum(running_counts * members.astype(jnp.float32), axis=2) - 1.0).astype(jnp.int32)
    local_slot = labels * capacity + ranks
    slot_hit = jnp.arange(head_slots, dtype=jnp.int32)[None, :, None] == local_slot[:, None, :]
    slot_table = slot_hit.astype(jnp.bfloat16)
    routed_in = jnp.concatenate(
        [query_heads[:, :HR], key_heads[:, :HR], value_heads[:, :HR], grad_heads[:, :HR]], axis=2
    )
    packed = jnp.einsum(
        "hst,thd->hsd", slot_table, routed_in, preferred_element_type=jnp.float32
    ).astype(jnp.bfloat16)
    packed = packed.reshape(devices, width, 4 * HD)
    token_pos = place * tok_rows + token_ids
    slot_pos = jnp.max(jnp.where(slot_hit, token_pos[None, None, :], -1), axis=2).reshape(
        devices, width
    )
    send_query = packed[:, :, :HD]
    send_key = packed[:, :, HD : 2 * HD]
    send_value = packed[:, :, 2 * HD : 3 * HD]
    send_grad = packed[:, :, 3 * HD :]
    arrived_query, arrived_key, arrived_value, arrived_grad, arrived_pos = (
        lax.all_to_all(send_query, "seq", split_axis=0, concat_axis=0, tiled=True),
        lax.all_to_all(send_key, "seq", split_axis=0, concat_axis=0, tiled=True),
        lax.all_to_all(send_value, "seq", split_axis=0, concat_axis=0, tiled=True),
        lax.all_to_all(send_grad, "seq", split_axis=0, concat_axis=0, tiled=True),
        lax.all_to_all(slot_pos, "seq", split_axis=0, concat_axis=0, tiled=True),
    )
    arrived_all = jnp.concatenate([arrived_query, arrived_key, arrived_value, arrived_grad], axis=2)
    unit_index = jnp.arange(7, dtype=jnp.int32)
    target_units = jnp.arange(CS // unit_rows, dtype=jnp.int32)
    block = arrived_all.reshape(devices * 7, unit_rows * 4 * HD)
    live_counts = jnp.sum((arrived_pos >= 0).astype(jnp.int32), axis=1)
    units = live_counts // unit_rows
    starts = jnp.cumsum(units) - units
    picker = (target_units[:, None, None] == starts[None, :, None] + unit_index[None, None, :]) & (
        unit_index[None, None, :] < units[None, :, None]
    )
    picker = picker.reshape(CS // unit_rows, devices * 7).astype(jnp.bfloat16)
    compact = (
        jnp.dot(picker, block, preferred_element_type=jnp.float32)
        .astype(jnp.bfloat16)
        .reshape(CS, 4 * HD)
    )
    results = cluster_grads(
        compact[:, :HD],
        compact[:, HD : 2 * HD],
        compact[:, 2 * HD : 3 * HD],
        compact[:, 3 * HD :],
        factor,
    )
    answer = jnp.concatenate([result.astype(jnp.bfloat16) for result in results], axis=1).reshape(
        CS // unit_rows, unit_rows * 3 * HD
    )
    spread = jnp.dot(picker.T, answer, preferred_element_type=jnp.float32).astype(jnp.bfloat16)
    outgoing = spread.reshape(devices, capacity, 3 * HD)
    back_query, back_key, back_value = (
        lax.all_to_all(outgoing[:, :, :HD], "seq", split_axis=0, concat_axis=0, tiled=True),
        lax.all_to_all(outgoing[:, :, HD : 2 * HD], "seq", split_axis=0, concat_axis=0, tiled=True),
        lax.all_to_all(outgoing[:, :, 2 * HD :], "seq", split_axis=0, concat_axis=0, tiled=True),
    )
    back_all = jnp.concatenate([back_query, back_key, back_value], axis=2).reshape(
        HR, head_slots, 3 * HD
    )
    routed_out = jnp.einsum(
        "hst,hsd->thd", slot_table, back_all, preferred_element_type=jnp.float32
    ).astype(jnp.bfloat16)
    routed_query = routed_out[:, :, :HD]
    routed_key = routed_out[:, :, HD : 2 * HD]
    routed_value = routed_out[:, :, 2 * HD :]
    local_query = query_heads[:, HR:]
    local_key = key_heads[:, HR:]
    local_value = value_heads[:, HR:]
    local_grad = grad_heads[:, HR:]
    prior_key, prior_value = shifted((local_key, local_value), "seq", 1)
    keys_all = jnp.concatenate([prior_key, local_key], axis=0)
    values_all = jnp.concatenate([prior_value, local_value], axis=0)
    key_positions = (place - 1) * tok_rows + jnp.arange(2 * tok_rows, dtype=jnp.int32)
    query_positions = place * tok_rows + jnp.arange(tok_rows, dtype=jnp.int32)
    span = min(512, tok_rows)
    total_key = jnp.zeros((2 * tok_rows, HL, HD), jnp.float32)
    total_value = jnp.zeros((2 * tok_rows, HL, HD), jnp.float32)
    start = tok_rows - WIN
    allowed = window_mask(query_positions, key_positions)
    part_query, part_key, part_value = window_block(
        local_query, keys_all, values_all, local_grad, allowed, factor
    )
    total_key = total_key.at[start : start + span + WIN].add(part_key)
    total_value = total_value.at[start : start + span + WIN].add(part_value)
    tail = tok_rows - WIN
    carried_key, carried_value = (
        shifted(total_key[tail:tok_rows].astype(jnp.bfloat16), "seq", -1).astype(jnp.float32),
        shifted(total_value[tail:tok_rows].astype(jnp.bfloat16), "seq", -1).astype(jnp.float32),
    )
    local_dk = total_key[tok_rows:].at[tail:].add(carried_key)
    local_dv = total_value[tok_rows:].at[tail:].add(carried_value)
    local_dq = part_query.astype(jnp.bfloat16)
    grad_query = jnp.concatenate([routed_query, local_dq], axis=1).reshape(1, tok_rows, heads * HD)
    grad_key = jnp.concatenate([routed_key, local_dk.astype(jnp.bfloat16)], axis=1).reshape(
        1, tok_rows, heads * HD
    )
    grad_value = jnp.concatenate([routed_value, local_dv.astype(jnp.bfloat16)], axis=1).reshape(
        1, tok_rows, heads * HD
    )
    return (grad_query, grad_key, grad_value)


def body(query, key, value, grad_sent, out_weight, assign):
    clusters = query.shape[1] * lax.axis_size("seq") // CS
    plan = pair_body if clusters == 2 else general_body
    return plan(query, key, value, grad_sent, out_weight, assign)


def solution(mesh):
    placed = (
        P("section", "seq", None),
        P("section", "seq", None),
        P("section", "seq", None),
        P("section", "seq", None),
        P("section", None, None),
        P("section", None, "seq"),
    )
    return jax.shard_map(
        body,
        mesh=mesh,
        in_specs=placed,
        out_specs=(P("section", "seq", None), P("section", "seq", None), P("section", "seq", None)),
        check_vma=False,
    )
```

```python
import functools

import jax
import jax.numpy as jnp
from jax import lax
from jax.experimental import pallas as pl
from jax.experimental.pallas import tpu as pltpu
from jax.sharding import PartitionSpec as P

HR = 4
HL = 4
HD = 128
CS = 2048
WIN = 512
QB = 256
MIB = 1024 * 1024
SPLIT_MIB = 56
NT = (((1,), (1,)), ((), ()))
F32 = jnp.float32
BF16 = jnp.bfloat16


def vmem(count=1):
    return [pl.BlockSpec(memory_space=pltpu.VMEM)] * count


def smem(count=1):
    return [pl.BlockSpec(memory_space=pltpu.SMEM)] * count


def params(mib):
    return pltpu.CompilerParams(vmem_limit_bytes=mib * MIB)


def dot(a, b):
    return jnp.dot(a, b, preferred_element_type=F32)


def dot_nt(a, b):
    return lax.dot_general(a, b, NT, preferred_element_type=F32)


def takes(microseconds):
    return pl.CostEstimate(
        flops=int(microseconds * 1.1e9), bytes_accessed=int(microseconds * 3.5e6), transcendentals=0
    )


def rows(start, size):
    return pl.ds(pl.multiple_of(start, size), size)


def start_all(copies):
    for copy in copies:
        copy.start()


def wait_all(copies):
    for copy in copies:
        copy.wait()


def head_columns(place, d):
    return pl.ds(pl.multiple_of(lax.rem(place[0] + d, HR) * HD, HD), HD)


def split_kernel(place, labels, q_hbm, k_hbm, v_hbm, x0, x1, x2, x3, own, send, held, sems):
    tok = q_hbm.shape[0]
    copies = [pltpu.make_async_copy(source, held.at[i], sems.at[i]) for i, source in enumerate((q_hbm, k_hbm, v_hbm))]
    start_all(copies)
    for d, x in enumerate((x0, x1, x2, x3)):
        line = labels[pl.ds(lax.rem(place[0] + d, HR), 1), :].astype(F32)
        parts = [line[:, r * HD : (r + 1) * HD] for r in range(tok // HD)]
        parts.append(jnp.zeros((16 - tok // HD, HD), F32))
        x[2 * tok :, :] = jnp.concatenate(parts, axis=0).astype(BF16)
    width = HL * HD // 2
    for i in range(3):
        copies[i].wait()
        for d, x in enumerate((x0, x1, x2, x3)):
            if i < 2:
                x[i * tok : (i + 1) * tok, :] = held[i, :, head_columns(place, d)]
        for out, side in ((send, 1 - place[1]), (own, place[1])):
            out[i] = held[i, :, pl.ds(pl.multiple_of(HR * HD + side * width, width), width)]


def split_value_kernel(place, _after1, _after2, _after3, v_ref, x0, x1, x2, x3):
    for d, x in enumerate((x0, x1, x2, x3)):
        x[...] = v_ref[:, head_columns(place, d)]


def project_kernel(place, _after, _after_local, rows_ref, weight, g0, g1, g2, g3, own_ref, send_ref):
    step = pl.program_id(0)
    part = dot_nt(rows_ref[...], weight[...]).astype(BF16)

    @pl.when(step < HR // 2)
    def _():
        for i in range(2):
            d = lax.rem(2 * step + i - place[0] + 4, 4)
            for e, g in enumerate((g0, g1, g2, g3)):

                @pl.when(d == e)
                def _(g=g, i=i):
                    g[...] = part[:, i * HD : (i + 1) * HD]

    @pl.when(step >= HR // 2)
    def _():
        @pl.when(step - HR // 2 == place[1])
        def _():
            own_ref[...] = part

        @pl.when(step - HR // 2 != place[1])
        def _():
            send_ref[...] = part


def pack_kernel(unit, place, _after, x0, x1, x2, x3, sorted_ref, send_ref, slot_row, slot_col, kept_ref):
    tok = x0.shape[0] - 16
    tok = tok // 2
    side = place[1]
    lane = lax.broadcasted_iota(jnp.int32, (1, tok), 1).astype(F32)
    labels = []
    for x in (x0, x1, x2, x3):
        block = x[2 * tok :, :].astype(F32)
        labels.append(jnp.concatenate([block[r : r + 1, :] for r in range(tok // 128)], axis=1))
    label = jnp.concatenate(labels + [jnp.zeros((4, tok), F32)], axis=0)
    upper = (
        lax.broadcasted_iota(jnp.int32, (tok, tok), 0) <= lax.broadcasted_iota(jnp.int32, (tok, tok), 1)
    ).astype(BF16)
    ones = dot(label.astype(BF16), upper)
    totals = [jnp.sum(row).astype(jnp.int32) for row in labels]
    whole = totals[0] + totals[1] + totals[2] + totals[3]
    half = CS // 2
    keep_one = jnp.where(side == 0, (whole > half).astype(jnp.int32), (whole >= half).astype(jnp.int32))
    keep_f = keep_one.astype(F32)
    slots = []
    for d in range(4):
        kept = jnp.where(keep_one == 1, totals[d], tok - totals[d])
        kept_ref[d] = kept // unit
        is_kept = labels[d] * keep_f + (1.0 - labels[d]) * (1.0 - keep_f)
        ones_d = ones[d : d + 1, :]
        count = ones_d * keep_f + (lane + 1.0 - ones_d) * (1.0 - keep_f)
        slot = jnp.where(is_kept > 0.5, count - 1.0, kept.astype(F32) + lane - count)
        slots.append(slot)
    slots_all = jnp.concatenate(slots + [jnp.zeros((124, tok), F32)], axis=0)
    slot_row[...] = slots_all[:8, :]
    slot_col[...] = slots_all.T
    row_index = lax.broadcasted_iota(jnp.int32, (tok, tok), 0).astype(F32)
    for d, x in enumerate((x0, x1, x2, x3)):
        move = (row_index == slots[d]).astype(BF16)
        for i in range(2):
            sorted_ref[d, i] = dot(move, x[i * tok : (i + 1) * tok, :]).astype(BF16)
    offset = jnp.int32(0)
    info_row = lax.broadcasted_iota(jnp.int32, (16, HD), 0)
    info = jnp.zeros((16, HD), F32)
    for d in range(4):
        kept = kept_ref[d]
        info = jnp.where(info_row == d, kept.astype(F32), info)

        def put(u, carry, d=d, offset=offset, kept=kept):
            for i in range(2):
                send_ref[rows(i * half + (offset + u - kept) * unit, unit), :] = sorted_ref[d, i, rows(u * unit, unit), :]
            return carry

        lax.fori_loop(kept, tok // unit, put, 0)
        offset = offset + tok // unit - kept
    send_ref[2 * half :, :] = info.astype(BF16)


def pack_value_kernel(unit, kept_ref, _after, slot_row, x0, x1, x2, x3, local_ref, sorted_ref, send_ref):
    pack_one(unit, kept_ref, slot_row, (x0, x1, x2, x3), sorted_ref, send_ref)
    tok = local_ref.shape[0]
    for h in range(HL // 2):
        at = CS // 2 + h * tok
        send_ref[at : at + tok, :] = local_ref[:, h * HD : (h + 1) * HD]


def pack_grad_kernel(
    unit, place, kept_ref, _after, slot_row, x0, x1, x2, x3, own, got, sorted_ref, send_ref, edge_ref
):
    pack_one(unit, kept_ref, slot_row, (x0, x1, x2, x3), sorted_ref, send_ref)
    for side, block in ((1, own), (0, got)):

        @pl.when(place[1] == side)
        def _(block=block):
            edge_ref[...] = block[1:]


def pack_one(unit, kept_ref, slot_row, blocks, sorted_ref, send_ref):
    tok = sorted_ref.shape[1]
    row_index = lax.broadcasted_iota(jnp.int32, (tok, tok), 0).astype(F32)
    for d, x in enumerate(blocks):
        move = (row_index == slot_row[d : d + 1, :]).astype(BF16)
        sorted_ref[d] = dot(move, x[...]).astype(BF16)
    offset = jnp.int32(0)
    for d in range(4):
        kept = kept_ref[d]

        def put(u, carry, d=d, offset=offset, kept=kept):
            send_ref[rows((offset + u - kept) * unit, unit), :] = sorted_ref[d, rows(u * unit, unit), :]
            return carry

        lax.fori_loop(kept, tok // unit, put, 0)
        offset = offset + tok // unit - kept


def each_unit(units, place, kept_ref, got_ref, own, got):
    first, side = place[0], place[1]
    pos = jnp.int32(0)
    for z in range(4):
        d = lax.rem(first - z + 4, 4)
        kept = kept_ref[d]
        came = units - got_ref[d]
        at = jnp.int32(0)
        for e in range(4):
            at = at + jnp.where(e < d, units - got_ref[e], 0)
        own_pos = pos + jnp.where(side == 0, 0, came)
        got_pos = pos + jnp.where(side == 0, kept, 0)

        def own_step(u, carry, d=d, own_pos=own_pos):
            own(d, u, own_pos + u)
            return carry

        def got_step(u, carry, at=at, got_pos=got_pos):
            got(at + u, got_pos + u)
            return carry

        lax.fori_loop(0, kept, own_step, 0)
        lax.fori_loop(0, came, got_step, 0)
        pos = pos + kept + came


def probs_kernel(unit, place, kept_ref, _after, sorted_ref, came_ref, got_ref, q_ref, k_ref, kt_ref, p_ref, s_ref):
    tok = sorted_ref.shape[2]
    half = CS // 2
    info = came_ref[2 * half :, :].astype(F32)
    for d in range(4):
        got_ref[d] = jnp.max(info[d : d + 1, :]).astype(jnp.int32)
    outs = (q_ref, k_ref)

    def own(d, u, to):
        for i in range(2):
            outs[i][rows(to * unit, unit), :] = sorted_ref[d, i, rows(u * unit, unit), :]

    def got(at, to):
        for i in range(2):
            outs[i][rows(to * unit, unit), :] = came_ref[rows(i * half + at * unit, unit), :]

    each_unit(tok // unit, place, kept_ref, got_ref, own, got)
    kt_ref[...] = k_ref[...].astype(F32).T.astype(BF16)
    factor = HD**-0.5
    low = lax.broadcasted_iota(jnp.int32, (QB, QB), 0) <= lax.broadcasted_iota(jnp.int32, (QB, QB), 1)
    for j in range(CS // QB):
        q = q_ref[j * QB : (j + 1) * QB, :]
        top = None
        for i in range(j + 1):
            s = dot_nt(k_ref[i * QB : (i + 1) * QB, :], q) * factor
            if i == j:
                s = jnp.where(low, s, -1e30)
            s_ref[i * QB : (i + 1) * QB, :] = s
            peak = jnp.max(s.reshape(QB // 8, 8, QB), axis=0)
            top = peak if top is None else jnp.maximum(top, peak)
        top = jnp.max(top, axis=0, keepdims=True)
        total = None
        for i in range(j + 1):
            w = jnp.exp(s_ref[i * QB : (i + 1) * QB, :] - top)
            s_ref[i * QB : (i + 1) * QB, :] = w
            part = jnp.sum(w.reshape(QB // 8, 8, QB), axis=0)
            total = part if total is None else total + part
        scale = 1.0 / jnp.sum(total, axis=0, keepdims=True)
        for i in range(j + 1):
            p_ref[i * QB : (i + 1) * QB, j * QB : (j + 1) * QB] = (s_ref[i * QB : (i + 1) * QB, :] * scale).astype(BF16)


def mix_kernel(
    unit, place, kept_ref, got_ref, _after, sorted_ref, came_ref, p_ref, own, got, g_own, v_ref, ot_ref, edge_ref, vt
):
    tok = own.shape[1]

    @pl.when(place[1] == 0)
    def _():
        edge_ref[0] = own[0]
        edge_ref[1] = g_own[...]

    @pl.when(place[1] == 1)
    def _():
        edge_ref[0] = got[0]
        for h in range(HL // 2):
            at = CS // 2 + h * tok
            edge_ref[1, :, h * HD : (h + 1) * HD] = came_ref[at : at + tok, :]

    def kept(d, u, to):
        v_ref[rows(to * unit, unit), :] = sorted_ref[d, rows(u * unit, unit), :]

    def came(at, to):
        v_ref[rows(to * unit, unit), :] = came_ref[rows(at * unit, unit), :]

    each_unit(sorted_ref.shape[1] // unit, place, kept_ref, got_ref, kept, came)
    vt[...] = v_ref[...].astype(F32).T.astype(BF16)
    for j in range(CS // QB):
        end = (j + 1) * QB
        ot_ref[:, j * QB : end] = dot(vt[:, :end], p_ref[:end, j * QB : end])


def grads_kernel(
    unit, place, kept_ref, got_ref, sorted_ref, came_ref, q_ref, k_ref, v_ref, kt_ref, ot_ref, p_ref,
    own_v, back_v, own_ref, back_ref, g_ref, dqt, res,
):
    tok = sorted_ref.shape[1]
    half = CS // 2
    count = CS // QB
    def own(d, u, to):
        g_ref[rows(to * unit, unit), :] = sorted_ref[d, rows(u * unit, unit), :]

    def got(at, to):
        g_ref[rows(to * unit, unit), :] = came_ref[rows(at * unit, unit), :]

    each_unit(tok // unit, place, kept_ref, got_ref, own, got)
    delta = jnp.sum(g_ref[...].astype(F32).T * ot_ref[...], axis=0, keepdims=True)
    factor = HD**-0.5
    for i in range(count):
        lo, hi = i * QB, (i + 1) * QB
        p = p_ref[lo:hi, lo:]
        g = g_ref[lo:, :]
        res[2, lo:hi, :] = dot(p, g).astype(BF16)
        dp = dot_nt(v_ref[lo:hi, :], g)
        ds = (p.astype(F32) * (dp - delta[:, lo:])).astype(BF16)
        res[1, lo:hi, :] = (dot(ds, q_ref[lo:, :]) * factor).astype(BF16)
        part = dot(kt_ref[:, lo:hi], ds)
        dqt[:, lo:] = part if i == 0 else dqt[:, lo:] + part
    res[0] = (dqt[...].T * factor).astype(BF16)

    def own_out(d, u, to):
        own_v[d, 0, rows(u * unit, unit), :] = res[2, rows(to * unit, unit), :]
        for i in range(2):
            own_ref[d, i, rows(u * unit, unit), :] = res[i, rows(to * unit, unit), :]

    def got_out(at, to):
        back_v[0, rows(at * unit, unit), :] = res[2, rows(to * unit, unit), :]
        for i in range(2):
            back_ref[i, rows(at * unit, unit), :] = res[i, rows(to * unit, unit), :]

    each_unit(tok // unit, place, kept_ref, got_ref, own_out, got_out)


def unsort_kernel(unit, distances, kept_ref, _after, _after_edge, slot_col, own_ref, back_ref, *refs):
    *outs, full = refs
    tok = own_ref.shape[2]
    count = own_ref.shape[1]
    col_index = lax.broadcasted_iota(jnp.int32, (tok, tok), 1).astype(F32)
    offset = jnp.int32(0)
    for d in range(HR):
        kept = kept_ref[d]
        if d in distances:
            n = distances.index(d)

            def own(u, carry, d=d, n=n):
                for i in range(count):
                    full[n, i, rows(u * unit, unit), :] = own_ref[d, i, rows(u * unit, unit), :]
                return carry

            def got(u, carry, n=n, offset=offset, kept=kept):
                for i in range(count):
                    full[n, i, rows(u * unit, unit), :] = back_ref[i, rows((offset + u - kept) * unit, unit), :]
                return carry

            lax.fori_loop(0, kept, own, 0)
            lax.fori_loop(kept, tok // unit, got, 0)
            move = (col_index == slot_col[:, d : d + 1]).astype(BF16)
            for i in range(count):
                outs[n][i] = dot(move, full[n, i]).astype(BF16)
        offset = offset + tok // unit - kept


def window_kernel(
    place, _after, own, got, g_own, g_came, edge, dq_ref, early_ref, late_ref, stats_ref, *scratch
):
    tok = own.shape[1]
    pair = 2 * tok
    factor = HD**-0.5
    r = lax.broadcasted_iota(jnp.int32, (QB, QB), 0)
    c = lax.broadcasted_iota(jnp.int32, (QB, QB), 1)
    span = WIN + QB
    started = place[0] > 0
    own_at, got_at = place[1] * tok, (1 - place[1]) * tok
    for h in range(HL // 2):
        part = slice(h * HD, (h + 1) * HD)
        queries, grads, keys, values, kt, dk, dv = (ref.at[h] for ref in scratch)
        g_got = g_came[CS // 2 + h * tok : CS // 2 + (h + 1) * tok, :]
        for at, block, g_block in ((own_at, own, g_own[:, part]), (got_at, got, g_got)):
            queries[rows(at, tok), :] = block[0, :, part]
            grads[rows(at, tok), :] = g_block
            keys[rows(at + WIN, tok), :] = block[1, :, part]
            values[rows(at + WIN, tok), :] = block[2, :, part]
        keys[:WIN, :] = edge[0, :, part]
        values[:WIN, :] = edge[1, :, part]
        kt[...] = keys[...].astype(F32).T.astype(BF16)
        for j in range(pair // QB):
            lo, hi = j * QB, j * QB + span
            q = queries[j * QB : (j + 1) * QB, :]
            g = grads[j * QB : (j + 1) * QB, :]
            s = dot_nt(keys[lo:hi, :], q) * factor
            first = jnp.where(r > c, s[:QB], -1e30)
            last = jnp.where(r <= c, s[span - QB :], -1e30)
            s = jnp.concatenate([first, s[QB : span - QB], last], axis=0)
            if lo < WIN:
                s = jnp.concatenate([jnp.where(started, s[: WIN - lo], -1e30), s[WIN - lo :]], axis=0)
            top = jnp.max(s, axis=0, keepdims=True)
            w = jnp.exp(s - top)
            scale = 1.0 / jnp.sum(w, axis=0, keepdims=True)
            p = w * scale
            dp = dot_nt(values[lo:hi, :], g)
            delta = jnp.sum(p * dp, axis=0, keepdims=True)
            pb = p.astype(BF16)
            ds = (p * (dp - delta)).astype(BF16)
            side, at = divmod(j * QB, tok)
            dq_ref[side, at : at + QB, part] = (dot(kt[:, lo:hi], ds).T * factor).astype(BF16)
            if side == 0:
                for n, line in enumerate((top, scale, delta)):
                    stats_ref[3 * h + n : 3 * h + n + 1, at : at + QB] = line
            skip = max(0, WIN - lo)
            low = max(lo, WIN) - WIN
            part_k = dot(ds[skip:], q) * factor
            part_v = dot(pb[skip:], g)
            end = hi - WIN
            if end - QB > low:
                dk[low : end - QB, :] = dk[low : end - QB, :] + part_k[:-QB]
                dv[low : end - QB, :] = dv[low : end - QB, :] + part_v[:-QB]
            dk[end - QB : end, :] = part_k[-QB:]
            dv[end - QB : end, :] = part_v[-QB:]
        for i, total in enumerate((dk, dv)):
            early_ref[i, :, part] = total[:tok, :].astype(BF16)
            late_ref[i, :, part] = total[tok:, :]
    stats_ref[6:, :] = jnp.zeros((2, tok), F32)


def settle_kernel(place, _after, dq_ref, early_ref, late_ref, edge, ahead, stats, own, send, late):
    tok = edge.shape[1]
    factor = HD**-0.5
    r = lax.broadcasted_iota(jnp.int32, (QB, QB), 0)
    c = lax.broadcasted_iota(jnp.int32, (QB, QB), 1)
    for h in range(HL // 2):
        part = slice(h * HD, (h + 1) * HD)
        for j in range(tok // QB):
            at = slice(j * QB, (j + 1) * QB)
            q, g = ahead[0, at, part], ahead[1, at, part]
            top, scale, delta = (stats[3 * h + n : 3 * h + n + 1, at] for n in range(3))
            s = dot_nt(edge[0, j * QB :, part], q) * factor
            p = jnp.exp(s - top) * scale
            first = jnp.where(r > c, p[:QB], 0.0)
            p = first if j == tok // QB - 1 else jnp.concatenate([first, p[QB:]], axis=0)
            ds = p * (dot_nt(edge[1, j * QB :, part], g) - delta)
            add_k = dot(ds.astype(BF16), q) * factor
            add_v = dot(p.astype(BF16), g)
            for i, add in enumerate((add_k, add_v)):
                base = late_ref[i, :, part] if j == 0 else late[h, i, j * QB :, :]
                late[h, i, j * QB :, :] = base + add
    for side, (near, far) in enumerate(((own, send), (send, own))):

        @pl.when(place[1] == side)
        def _(near=near, far=far):
            near[0] = dq_ref[0]
            near[1:] = early_ref[...]
            far[0] = dq_ref[1]
            for h in range(HL // 2):
                for i in range(2):
                    far[1 + i, :, h * HD : (h + 1) * HD] = late[h, i].astype(BF16)


def join_value_kernel(place, _after, v0, v1, v2, v3, out):
    for d, v in enumerate((v0, v1, v2, v3)):
        out[:, head_columns(place, d)] = v[0]


def join_kernel(place, value_ref, y0, y1, y2, y3, own, got, dq_ref, dk_ref, dv_ref):
    outs = (dq_ref, dk_ref, dv_ref)
    dv_ref[:, : HR * HD] = value_ref[...]
    for d, y in enumerate((y0, y1, y2, y3)):
        at = head_columns(place, d)
        for i in range(2):
            outs[i][:, at] = y[i]
    width = HL * HD // 2
    for n in range(2):
        side = place[1] if n == 0 else 1 - place[1]
        at = pl.ds(pl.multiple_of(HR * HD + side * width, width), width)
        for i in range(3):
            outs[i][:, at] = own[i] if n == 0 else got[i]


def struct(*shape, dtype=BF16):
    return jax.ShapeDtypeStruct(shape, dtype)


def pair_body(query, key, value, grad_sent, out_weight, assign):
    tok = query.shape[1]
    devices = lax.axis_size("seq")
    place = lax.axis_index("seq")
    first, side = place // 2, place % 2
    where = jnp.stack([first, side]).astype(jnp.int32)
    unit = CS // (4 * devices)
    half = CS // 2

    def among_groups(block, shift):
        route = [(i, ((i // 2 + shift) % HR) * 2 + i % 2) for i in range(devices)]
        return lax.ppermute(block, "seq", route)

    def swap(block):
        return lax.ppermute(block, "seq", [(i, i ^ 1) for i in range(devices)])

    hbm = [pl.BlockSpec(memory_space=pltpu.HBM)]
    width = HL * HD // 2
    boundary = from_behind(grad_sent, "section", -1)[0]
    *sent, local_own, local_send = pl.pallas_call(
        split_kernel,
        out_shape=[struct(2 * tok + 16, HD)] * HR + [struct(3, tok, width)] * 2,
        in_specs=smem() + vmem() + hbm * 3,
        out_specs=vmem(6),
        scratch_shapes=[pltpu.VMEM((3, tok, query.shape[2]), BF16), pltpu.SemaphoreType.DMA((3,))],
        compiler_params=params(SPLIT_MIB),
        cost_estimate=takes(2),
        name="split",
    )(where, assign[0], query[0], key[0], value[0])
    arrived = [sent[0]] + [among_groups(sent[d], d) for d in range(1, HR)]
    local_got = swap(local_send)
    v_sent = pl.pallas_call(
        split_value_kernel,
        out_shape=[struct(tok, HD)] * HR,
        in_specs=smem() + vmem(4),
        out_specs=vmem(4),
        compiler_params=params(20),
        cost_estimate=takes(1),
        name="split_value",
    )(where, *arrived[1:], value[0])
    v_arrived = [v_sent[0]] + [among_groups(v_sent[d], d) for d in range(1, HR)]

    ordered, send, slot_row, slot_col, kept = pl.pallas_call(
        functools.partial(pack_kernel, unit),
        out_shape=[
            struct(HR, 2, tok, HD),
            struct(2 * half + 16, HD),
            struct(8, tok, dtype=F32),
            struct(tok, HD, dtype=F32),
            struct(HR, dtype=jnp.int32),
        ],
        in_specs=smem() + vmem(5),
        out_specs=vmem(4) + smem(),
        compiler_params=params(32),
        cost_estimate=takes(2.6),
        name="pack",
    )(where, v_sent[0], *arrived)
    came = swap(send)

    *g_sent, g_own, g_send = pl.pallas_call(
        project_kernel,
        grid=(4,),
        out_shape=[struct(tok, HD)] * HR + [struct(tok, width)] * 2,
        in_specs=smem()
        + [
            pl.BlockSpec((16, HD), lambda n: (0, 0)),
            pl.BlockSpec((1, 16, HD), lambda n: (0, 0, 0)),
            pl.BlockSpec(boundary.shape, lambda n: (0, 0)),
            pl.BlockSpec((2 * HD, boundary.shape[1]), lambda n: (n, 0)),
        ],
        out_specs=[pl.BlockSpec((tok, HD), lambda n: (0, 0))] * HR
        + [pl.BlockSpec((tok, width), lambda n: (0, 0))] * 2,
        compiler_params=params(32),
        cost_estimate=takes(3.8),
        name="project",
    )(where, send, local_got, boundary, out_weight[0])
    g_arrived = [g_sent[0]] + [among_groups(g_sent[d], d) for d in range(1, HR)]

    v_ordered, v_out = pl.pallas_call(
        functools.partial(pack_value_kernel, unit),
        out_shape=[struct(HR, tok, HD), struct(half + HL // 2 * tok, HD)],
        in_specs=smem() + vmem(7),
        out_specs=vmem(2),
        compiler_params=params(20),
        cost_estimate=takes(1.6),
        name="pack_value",
    )(kept, g_sent[0], slot_row, *v_arrived, g_send)
    v_came = swap(v_out)

    got, q, k, kt, p = pl.pallas_call(
        functools.partial(probs_kernel, unit),
        out_shape=[struct(HR, dtype=jnp.int32)] + [struct(CS, HD)] * 2 + [struct(HD, CS), struct(CS, CS)],
        in_specs=smem(2) + vmem(3),
        out_specs=smem() + vmem(4),
        scratch_shapes=[pltpu.VMEM((CS, QB), F32)],
        compiler_params=params(24),
        cost_estimate=takes(5),
        name="probs",
    )(where, kept, v_out, ordered, came)

    g_ordered, g_out, edge = pl.pallas_call(
        functools.partial(pack_grad_kernel, unit),
        out_shape=[struct(HR, tok, HD), struct(half, HD), struct(2, tok, width)],
        in_specs=smem(2) + vmem(8),
        out_specs=vmem(3),
        compiler_params=params(20),
        cost_estimate=takes(1.6),
        name="pack_grad",
    )(where, kept, kt, slot_row, *g_arrived, local_own, local_got)
    g_came = swap(g_out)
    ahead = [(i, i + 2) for i in range(devices - 2)]
    behind = [(i + 2, i) for i in range(devices - 2)]
    edge_got = lax.ppermute(edge, "seq", ahead)

    v, ot, query_edge = pl.pallas_call(
        functools.partial(mix_kernel, unit),
        out_shape=[struct(CS, HD), struct(HD, CS, dtype=F32), struct(2, tok, width)],
        in_specs=smem(3) + vmem(7),
        out_specs=vmem(3),
        scratch_shapes=[pltpu.VMEM((HD, CS), BF16)],
        compiler_params=params(20),
        cost_estimate=takes(1.7),
        name="mix",
    )(where, kept, got, edge, v_ordered, v_came, p, local_own, local_got, g_own)
    query_edge_got = lax.ppermute(query_edge, "seq", behind)

    own_v, back_v, own, back = pl.pallas_call(
        functools.partial(grads_kernel, unit),
        out_shape=[struct(HR, 1, tok, HD), struct(1, half, HD), struct(HR, 2, tok, HD), struct(2, half, HD)],
        in_specs=smem(3) + vmem(8),
        out_specs=vmem(4),
        scratch_shapes=[
            pltpu.VMEM((CS, HD), BF16),
            pltpu.VMEM((HD, CS), F32),
            pltpu.VMEM((3, CS, HD), BF16),
        ],
        compiler_params=params(24),
        cost_estimate=takes(6.3),
        name="grads",
    )(where, kept, got, g_ordered, g_came, q, k, v, kt, ot, p)

    def unsort(distances, after, after_edge, own, returned, name):
        count = own.shape[1]
        return pl.pallas_call(
            functools.partial(unsort_kernel, unit, distances),
            out_shape=[struct(count, tok, HD)] * len(distances),
            in_specs=smem() + vmem(5),
            out_specs=vmem(len(distances)),
            scratch_shapes=[pltpu.VMEM((len(distances), count, tok, HD), BF16)],
            compiler_params=params(20),
            cost_estimate=takes({'unsort_value':2.6,'unsort_first':0.1,'unsort_last':1.4}[name]),
            name=name,
        )(kept, after, after_edge, slot_col, own, returned)

    returned_v, returned = swap(back_v), swap(back)
    pair = 2 * tok
    dq_local, early, late, stats = pl.pallas_call(
        window_kernel,
        out_shape=[
            struct(2, tok, width),
            struct(2, tok, width),
            struct(2, tok, width, dtype=F32),
            struct(8, tok, dtype=F32),
        ],
        in_specs=smem() + vmem(6),
        out_specs=vmem(4),
        scratch_shapes=[
            pltpu.VMEM((HL // 2, pair, HD), BF16),
            pltpu.VMEM((HL // 2, pair, HD), BF16),
            pltpu.VMEM((HL // 2, pair + WIN, HD), BF16),
            pltpu.VMEM((HL // 2, pair + WIN, HD), BF16),
            pltpu.VMEM((HL // 2, HD, pair + WIN), BF16),
            pltpu.VMEM((HL // 2, pair, HD), F32),
            pltpu.VMEM((HL // 2, pair, HD), F32),
        ],
        compiler_params=params(24),
        cost_estimate=takes(4),
        name="window",
    )(where, back_v, local_own, local_got, g_own, v_came, edge_got)
    stats_got = lax.ppermute(stats, "seq", behind)
    natural_v = unsort((0, 1, 2, 3), stats, query_edge_got, own_v, returned_v, "unsort_value")
    home_v = [natural_v[0]] + [among_groups(natural_v[d], -d) for d in range(1, HR)]
    first_natural = unsort((0, 1, 2), natural_v[0], natural_v[0], own, returned, "unsort_first")
    settled_own, settled_send = pl.pallas_call(
        settle_kernel,
        out_shape=[struct(3, tok, width)] * 2,
        in_specs=smem() + vmem(7),
        out_specs=vmem(2),
        scratch_shapes=[pltpu.VMEM((HL // 2, 2, tok, HD), F32)],
        compiler_params=params(20),
        cost_estimate=takes(0.1),
        name="settle",
    )(where, first_natural[0], dq_local, early, late, edge, query_edge_got, stats_got)
    settled_got = swap(settled_send)
    value_left = pl.pallas_call(
        join_value_kernel,
        out_shape=struct(tok, HR * HD),
        in_specs=smem() + vmem(5),
        out_specs=vmem()[0],
        compiler_params=params(16),
        cost_estimate=takes(12),
        name="join_value",
    )(where, settled_send, *home_v)
    last_natural = unsort((3,), value_left, value_left, own, returned, "unsort_last")
    natural = [*first_natural, *last_natural]
    home = [natural[0]] + [among_groups(natural[d], -d) for d in range(1, HR)]

    outs = pl.pallas_call(
        join_kernel,
        out_shape=[struct(tok, (HR + HL) * HD)] * 3,
        in_specs=smem() + vmem(7),
        out_specs=vmem(3),
        compiler_params=params(32),
        cost_estimate=takes(2.8),
        name="join",
    )(where, value_left, *home, settled_own, settled_got)
    return tuple(out[None] for out in outs)


def from_behind(block, axis, distance):
    devices = range(lax.axis_size(axis))
    route = [((i - distance) % len(devices), i) for i in devices]
    return lax.ppermute(block, axis, route)


def shifted(block, axis, distance):
    devices = range(lax.axis_size(axis))
    route = [(i - distance, i) for i in devices if i - distance in devices]
    return lax.ppermute(block, axis, route)


def cluster_block(query_rows, key_rows, value_rows, grad_rows, allowed, factor):
    scores = jnp.dot(query_rows, key_rows.T, preferred_element_type=jnp.float32) * factor
    scores = jnp.where(allowed, scores, -1e30)
    highest = jnp.max(scores, axis=1, keepdims=True)
    weights = jnp.exp(scores - highest)
    probs = weights / jnp.sum(weights, axis=1, keepdims=True)
    dprob = jnp.dot(grad_rows, value_rows.T, preferred_element_type=jnp.float32)
    delta = jnp.sum(probs * dprob, axis=1, keepdims=True)
    dscore = probs * (dprob - delta)
    probs_b = probs.astype(jnp.bfloat16)
    dscore_b = dscore.astype(jnp.bfloat16)
    grad_query = jnp.dot(dscore_b, key_rows, preferred_element_type=jnp.float32) * factor
    grad_key = jnp.dot(dscore_b.T, query_rows, preferred_element_type=jnp.float32) * factor
    grad_value = jnp.dot(probs_b.T, grad_rows, preferred_element_type=jnp.float32)
    return (grad_query, grad_key, grad_value)


def cluster_grads(query_rows, key_rows, value_rows, grad_rows, factor):
    length = query_rows.shape[0]
    span = min(512, length)
    pieces = []
    total_key = jnp.zeros(key_rows.shape, jnp.float32)
    total_value = jnp.zeros(value_rows.shape, jnp.float32)
    for index in range(length // span):
        first = index * span
        end = first + span
        allowed = (
            jnp.arange(end, dtype=jnp.int32)[None, :]
            <= (first + jnp.arange(span, dtype=jnp.int32))[:, None]
        )
        part_query, part_key, part_value = cluster_block(
            query_rows[first:end],
            key_rows[:end],
            value_rows[:end],
            grad_rows[first:end],
            allowed,
            factor,
        )
        pieces.append(part_query)
        total_key = total_key.at[:end].add(part_key)
        total_value = total_value.at[:end].add(part_value)
    return (jnp.concatenate(pieces, axis=0), total_key, total_value)


def window_block(query_rows, key_rows, value_rows, grad_rows, allowed, factor):
    scores = (
        jnp.einsum("qhd,khd->hqk", query_rows, key_rows, preferred_element_type=jnp.float32)
        * factor
    )
    scores = jnp.where(allowed[None], scores, -1e30)
    highest = jnp.max(scores, axis=2, keepdims=True)
    weights = jnp.exp(scores - highest)
    probs = weights / jnp.sum(weights, axis=2, keepdims=True)
    dprob = jnp.einsum("qhd,khd->hqk", grad_rows, value_rows, preferred_element_type=jnp.float32)
    delta = jnp.sum(probs * dprob, axis=2, keepdims=True)
    dscore = probs * (dprob - delta)
    probs_b = probs.astype(jnp.bfloat16)
    dscore_b = dscore.astype(jnp.bfloat16)
    grad_query = (
        jnp.einsum("hqk,khd->qhd", dscore_b, key_rows, preferred_element_type=jnp.float32) * factor
    )
    grad_key = (
        jnp.einsum("hqk,qhd->khd", dscore_b, query_rows, preferred_element_type=jnp.float32)
        * factor
    )
    grad_value = jnp.einsum("hqk,qhd->khd", probs_b, grad_rows, preferred_element_type=jnp.float32)
    return (grad_query, grad_key, grad_value)


def window_mask(query_pos, key_pos):
    return (
        (key_pos[None, :] > query_pos[:, None] - WIN)
        & (key_pos[None, :] <= query_pos[:, None])
        & (key_pos[None, :] >= 0)
    )


def general_body(query, key, value, grad_sent, out_weight, assign):
    tok_rows = query.shape[1]
    heads = HR + HL
    devices = lax.axis_size("seq")
    place = lax.axis_index("seq")
    factor = HD ** (-0.5)
    boundary = from_behind(grad_sent, "section", -1)[0]
    attn_grad = lax.dot_general(
        boundary, out_weight[0], (((1,), (1,)), ((), ())), preferred_element_type=jnp.float32
    ).astype(jnp.bfloat16)
    query_heads = query[0].reshape(tok_rows, heads, HD)
    key_heads = key[0].reshape(tok_rows, heads, HD)
    value_heads = value[0].reshape(tok_rows, heads, HD)
    grad_heads = attn_grad.reshape(tok_rows, heads, HD)
    clusters = tok_rows * devices // CS
    owned = HR * tok_rows // CS
    capacity = 7 * CS // (4 * devices)
    unit_rows = capacity // 7
    width = owned * capacity
    head_slots = clusters * capacity
    labels = assign[0]
    members = (labels[:, :, None] == jnp.arange(clusters, dtype=jnp.int32)[None, None, :]).astype(
        jnp.bfloat16
    )
    token_ids = jnp.arange(tok_rows, dtype=jnp.int32)
    lower = (token_ids[:, None] >= token_ids[None, :]).astype(jnp.bfloat16)
    running_counts = jnp.einsum("ts,hsc->htc", lower, members, preferred_element_type=jnp.float32)
    ranks = (jnp.sum(running_counts * members.astype(jnp.float32), axis=2) - 1.0).astype(jnp.int32)
    local_slot = labels * capacity + ranks
    slot_hit = jnp.arange(head_slots, dtype=jnp.int32)[None, :, None] == local_slot[:, None, :]
    slot_table = slot_hit.astype(jnp.bfloat16)
    routed_in = jnp.concatenate(
        [query_heads[:, :HR], key_heads[:, :HR], value_heads[:, :HR], grad_heads[:, :HR]], axis=2
    )
    packed = jnp.einsum(
        "hst,thd->hsd", slot_table, routed_in, preferred_element_type=jnp.float32
    ).astype(jnp.bfloat16)
    packed = packed.reshape(devices, width, 4 * HD)
    token_pos = place * tok_rows + token_ids
    slot_pos = jnp.max(jnp.where(slot_hit, token_pos[None, None, :], -1), axis=2).reshape(
        devices, width
    )
    send_query = packed[:, :, :HD]
    send_key = packed[:, :, HD : 2 * HD]
    send_value = packed[:, :, 2 * HD : 3 * HD]
    send_grad = packed[:, :, 3 * HD :]
    arrived_query, arrived_key, arrived_value, arrived_grad, arrived_pos = (
        lax.all_to_all(send_query, "seq", split_axis=0, concat_axis=0, tiled=True),
        lax.all_to_all(send_key, "seq", split_axis=0, concat_axis=0, tiled=True),
        lax.all_to_all(send_value, "seq", split_axis=0, concat_axis=0, tiled=True),
        lax.all_to_all(send_grad, "seq", split_axis=0, concat_axis=0, tiled=True),
        lax.all_to_all(slot_pos, "seq", split_axis=0, concat_axis=0, tiled=True),
    )
    arrived_all = jnp.concatenate([arrived_query, arrived_key, arrived_value, arrived_grad], axis=2)
    unit_index = jnp.arange(7, dtype=jnp.int32)
    target_units = jnp.arange(CS // unit_rows, dtype=jnp.int32)
    block = arrived_all.reshape(devices * 7, unit_rows * 4 * HD)
    live_counts = jnp.sum((arrived_pos >= 0).astype(jnp.int32), axis=1)
    units = live_counts // unit_rows
    starts = jnp.cumsum(units) - units
    picker = (target_units[:, None, None] == starts[None, :, None] + unit_index[None, None, :]) & (
        unit_index[None, None, :] < units[None, :, None]
    )
    picker = picker.reshape(CS // unit_rows, devices * 7).astype(jnp.bfloat16)
    compact = (
        jnp.dot(picker, block, preferred_element_type=jnp.float32)
        .astype(jnp.bfloat16)
        .reshape(CS, 4 * HD)
    )
    results = cluster_grads(
        compact[:, :HD],
        compact[:, HD : 2 * HD],
        compact[:, 2 * HD : 3 * HD],
        compact[:, 3 * HD :],
        factor,
    )
    answer = jnp.concatenate([result.astype(jnp.bfloat16) for result in results], axis=1).reshape(
        CS // unit_rows, unit_rows * 3 * HD
    )
    spread = jnp.dot(picker.T, answer, preferred_element_type=jnp.float32).astype(jnp.bfloat16)
    outgoing = spread.reshape(devices, capacity, 3 * HD)
    back_query, back_key, back_value = (
        lax.all_to_all(outgoing[:, :, :HD], "seq", split_axis=0, concat_axis=0, tiled=True),
        lax.all_to_all(outgoing[:, :, HD : 2 * HD], "seq", split_axis=0, concat_axis=0, tiled=True),
        lax.all_to_all(outgoing[:, :, 2 * HD :], "seq", split_axis=0, concat_axis=0, tiled=True),
    )
    back_all = jnp.concatenate([back_query, back_key, back_value], axis=2).reshape(
        HR, head_slots, 3 * HD
    )
    routed_out = jnp.einsum(
        "hst,hsd->thd", slot_table, back_all, preferred_element_type=jnp.float32
    ).astype(jnp.bfloat16)
    routed_query = routed_out[:, :, :HD]
    routed_key = routed_out[:, :, HD : 2 * HD]
    routed_value = routed_out[:, :, 2 * HD :]
    local_query = query_heads[:, HR:]
    local_key = key_heads[:, HR:]
    local_value = value_heads[:, HR:]
    local_grad = grad_heads[:, HR:]
    prior_key, prior_value = shifted((local_key, local_value), "seq", 1)
    keys_all = jnp.concatenate([prior_key, local_key], axis=0)
    values_all = jnp.concatenate([prior_value, local_value], axis=0)
    key_positions = (place - 1) * tok_rows + jnp.arange(2 * tok_rows, dtype=jnp.int32)
    query_positions = place * tok_rows + jnp.arange(tok_rows, dtype=jnp.int32)
    span = min(512, tok_rows)
    total_key = jnp.zeros((2 * tok_rows, HL, HD), jnp.float32)
    total_value = jnp.zeros((2 * tok_rows, HL, HD), jnp.float32)
    start = tok_rows - WIN
    allowed = window_mask(query_positions, key_positions)
    part_query, part_key, part_value = window_block(
        local_query, keys_all, values_all, local_grad, allowed, factor
    )
    total_key = total_key.at[start : start + span + WIN].add(part_key)
    total_value = total_value.at[start : start + span + WIN].add(part_value)
    tail = tok_rows - WIN
    carried_key, carried_value = (
        shifted(total_key[tail:tok_rows].astype(jnp.bfloat16), "seq", -1).astype(jnp.float32),
        shifted(total_value[tail:tok_rows].astype(jnp.bfloat16), "seq", -1).astype(jnp.float32),
    )
    local_dk = total_key[tok_rows:].at[tail:].add(carried_key)
    local_dv = total_value[tok_rows:].at[tail:].add(carried_value)
    local_dq = part_query.astype(jnp.bfloat16)
    grad_query = jnp.concatenate([routed_query, local_dq], axis=1).reshape(1, tok_rows, heads * HD)
    grad_key = jnp.concatenate([routed_key, local_dk.astype(jnp.bfloat16)], axis=1).reshape(
        1, tok_rows, heads * HD
    )
    grad_value = jnp.concatenate([routed_value, local_dv.astype(jnp.bfloat16)], axis=1).reshape(
        1, tok_rows, heads * HD
    )
    return (grad_query, grad_key, grad_value)


def body(query, key, value, grad_sent, out_weight, assign):
    clusters = query.shape[1] * lax.axis_size("seq") // CS
    plan = pair_body if clusters == 2 else general_body
    return plan(query, key, value, grad_sent, out_weight, assign)


def solution(mesh):
    placed = (
        P("section", "seq", None),
        P("section", "seq", None),
        P("section", "seq", None),
        P("section", "seq", None),
        P("section", None, None),
        P("section", None, "seq"),
    )
    return jax.shard_map(
        body,
        mesh=mesh,
        in_specs=placed,
        out_specs=(P("section", "seq", None), P("section", "seq", None), P("section", "seq", None)),
        check_vma=False,
    )
```

```python
import functools

import jax
import jax.numpy as jnp
from jax import lax
from jax.experimental import pallas as pl
from jax.experimental.pallas import tpu as pltpu
from jax.sharding import PartitionSpec as P

HR = 4
HL = 4
HD = 128
CS = 2048
WIN = 512
QB = 256
MIB = 1024 * 1024
SPLIT_MIB = 56
NT = (((1,), (1,)), ((), ()))
F32 = jnp.float32
BF16 = jnp.bfloat16


def vmem(count=1):
    return [pl.BlockSpec(memory_space=pltpu.VMEM)] * count


def smem(count=1):
    return [pl.BlockSpec(memory_space=pltpu.SMEM)] * count


def params(mib):
    return pltpu.CompilerParams(vmem_limit_bytes=mib * MIB)


def dot(a, b):
    return jnp.dot(a, b, preferred_element_type=F32)


def dot_nt(a, b):
    return lax.dot_general(a, b, NT, preferred_element_type=F32)


def takes(microseconds):
    return pl.CostEstimate(
        flops=int(microseconds * 1.1e9), bytes_accessed=int(microseconds * 3.5e6), transcendentals=0
    )


def rows(start, size):
    return pl.ds(pl.multiple_of(start, size), size)


def start_all(copies):
    for copy in copies:
        copy.start()


def wait_all(copies):
    for copy in copies:
        copy.wait()


def head_columns(place, d):
    return pl.ds(pl.multiple_of(lax.rem(place[0] + d, HR) * HD, HD), HD)


def split_kernel(place, labels, q_hbm, k_hbm, v_hbm, x0, x1, x2, x3, own, send, held, sems):
    tok = q_hbm.shape[0]
    cuts = sems.shape[1]
    size = tok // cuts
    copies = []
    for i, source in enumerate((q_hbm, k_hbm, v_hbm)):
        for n in range(cuts):
            at = slice(n * size, (n + 1) * size)
            copies.append(pltpu.make_async_copy(source.at[at], held.at[i, at], sems.at[i, n]))
    start_all(copies)
    for d, x in enumerate((x0, x1, x2, x3)):
        line = labels[pl.ds(lax.rem(place[0] + d, HR), 1), :].astype(F32)
        parts = [line[:, r * HD : (r + 1) * HD] for r in range(tok // HD)]
        parts.append(jnp.zeros((16 - tok // HD, HD), F32))
        x[2 * tok :, :] = jnp.concatenate(parts, axis=0).astype(BF16)
    width = HL * HD // 2
    for i in range(3):
        wait_all(copies[i * cuts : (i + 1) * cuts])
        for d, x in enumerate((x0, x1, x2, x3)):
            if i < 2:
                x[i * tok : (i + 1) * tok, :] = held[i, :, head_columns(place, d)]
        for out, side in ((send, 1 - place[1]), (own, place[1])):
            out[i] = held[i, :, pl.ds(pl.multiple_of(HR * HD + side * width, width), width)]


def split_value_kernel(place, _after1, _after2, _after3, v_ref, x0, x1, x2, x3):
    for d, x in enumerate((x0, x1, x2, x3)):
        x[...] = v_ref[:, head_columns(place, d)]


def project_kernel(place, _after, _after_local, rows_ref, weight, g0, g1, g2, g3, own_ref, send_ref):
    step = pl.program_id(0)
    part = dot_nt(rows_ref[...], weight[...]).astype(BF16)

    @pl.when(step < HR // 2)
    def _():
        for i in range(2):
            d = lax.rem(2 * step + i - place[0] + 4, 4)
            for e, g in enumerate((g0, g1, g2, g3)):

                @pl.when(d == e)
                def _(g=g, i=i):
                    g[...] = part[:, i * HD : (i + 1) * HD]

    @pl.when(step >= HR // 2)
    def _():
        @pl.when(step - HR // 2 == place[1])
        def _():
            own_ref[...] = part

        @pl.when(step - HR // 2 != place[1])
        def _():
            send_ref[...] = part


def pack_kernel(unit, place, _after, x0, x1, x2, x3, sorted_ref, send_ref, slot_row, slot_col, kept_ref):
    tok = x0.shape[0] - 16
    tok = tok // 2
    side = place[1]
    lane = lax.broadcasted_iota(jnp.int32, (1, tok), 1).astype(F32)
    labels = []
    for x in (x0, x1, x2, x3):
        block = x[2 * tok :, :].astype(F32)
        labels.append(jnp.concatenate([block[r : r + 1, :] for r in range(tok // 128)], axis=1))
    label = jnp.concatenate(labels + [jnp.zeros((4, tok), F32)], axis=0)
    upper = (
        lax.broadcasted_iota(jnp.int32, (tok, tok), 0) <= lax.broadcasted_iota(jnp.int32, (tok, tok), 1)
    ).astype(BF16)
    ones = dot(label.astype(BF16), upper)
    totals = [jnp.sum(row).astype(jnp.int32) for row in labels]
    whole = totals[0] + totals[1] + totals[2] + totals[3]
    half = CS // 2
    keep_one = jnp.where(side == 0, (whole > half).astype(jnp.int32), (whole >= half).astype(jnp.int32))
    keep_f = keep_one.astype(F32)
    slots = []
    for d in range(4):
        kept = jnp.where(keep_one == 1, totals[d], tok - totals[d])
        kept_ref[d] = kept // unit
        is_kept = labels[d] * keep_f + (1.0 - labels[d]) * (1.0 - keep_f)
        ones_d = ones[d : d + 1, :]
        count = ones_d * keep_f + (lane + 1.0 - ones_d) * (1.0 - keep_f)
        slot = jnp.where(is_kept > 0.5, count - 1.0, kept.astype(F32) + lane - count)
        slots.append(slot)
    slots_all = jnp.concatenate(slots + [jnp.zeros((124, tok), F32)], axis=0)
    slot_row[...] = slots_all[:8, :]
    slot_col[...] = slots_all.T
    row_index = lax.broadcasted_iota(jnp.int32, (tok, tok), 0).astype(F32)
    for d, x in enumerate((x0, x1, x2, x3)):
        move = (row_index == slots[d]).astype(BF16)
        for i in range(2):
            sorted_ref[d, i] = dot(move, x[i * tok : (i + 1) * tok, :]).astype(BF16)
    offset = jnp.int32(0)
    info_row = lax.broadcasted_iota(jnp.int32, (16, HD), 0)
    info = jnp.zeros((16, HD), F32)
    for d in range(4):
        kept = kept_ref[d]
        info = jnp.where(info_row == d, kept.astype(F32), info)

        def put(u, carry, d=d, offset=offset, kept=kept):
            for i in range(2):
                send_ref[rows(i * half + (offset + u - kept) * unit, unit), :] = sorted_ref[d, i, rows(u * unit, unit), :]
            return carry

        lax.fori_loop(kept, tok // unit, put, 0)
        offset = offset + tok // unit - kept
    send_ref[2 * half :, :] = info.astype(BF16)


def pack_value_kernel(unit, kept_ref, _after, slot_row, x0, x1, x2, x3, local_ref, sorted_ref, send_ref):
    pack_one(unit, kept_ref, slot_row, (x0, x1, x2, x3), sorted_ref, send_ref)
    tok = local_ref.shape[0]
    for h in range(HL // 2):
        at = CS // 2 + h * tok
        send_ref[at : at + tok, :] = local_ref[:, h * HD : (h + 1) * HD]


def pack_grad_kernel(
    unit, place, kept_ref, _after, slot_row, x0, x1, x2, x3, own, got, sorted_ref, send_ref, edge_ref
):
    pack_one(unit, kept_ref, slot_row, (x0, x1, x2, x3), sorted_ref, send_ref)
    for side, block in ((1, own), (0, got)):

        @pl.when(place[1] == side)
        def _(block=block):
            edge_ref[...] = block[1:]


def pack_one(unit, kept_ref, slot_row, blocks, sorted_ref, send_ref):
    tok = sorted_ref.shape[1]
    row_index = lax.broadcasted_iota(jnp.int32, (tok, tok), 0).astype(F32)
    for d, x in enumerate(blocks):
        move = (row_index == slot_row[d : d + 1, :]).astype(BF16)
        sorted_ref[d] = dot(move, x[...]).astype(BF16)
    offset = jnp.int32(0)
    for d in range(4):
        kept = kept_ref[d]

        def put(u, carry, d=d, offset=offset, kept=kept):
            send_ref[rows((offset + u - kept) * unit, unit), :] = sorted_ref[d, rows(u * unit, unit), :]
            return carry

        lax.fori_loop(kept, tok // unit, put, 0)
        offset = offset + tok // unit - kept


def each_unit(units, place, kept_ref, got_ref, own, got):
    first, side = place[0], place[1]
    pos = jnp.int32(0)
    for z in range(4):
        d = lax.rem(first - z + 4, 4)
        kept = kept_ref[d]
        came = units - got_ref[d]
        at = jnp.int32(0)
        for e in range(4):
            at = at + jnp.where(e < d, units - got_ref[e], 0)
        own_pos = pos + jnp.where(side == 0, 0, came)
        got_pos = pos + jnp.where(side == 0, kept, 0)

        def own_step(u, carry, d=d, own_pos=own_pos):
            own(d, u, own_pos + u)
            return carry

        def got_step(u, carry, at=at, got_pos=got_pos):
            got(at + u, got_pos + u)
            return carry

        lax.fori_loop(0, kept, own_step, 0)
        lax.fori_loop(0, came, got_step, 0)
        pos = pos + kept + came


def probs_kernel(unit, place, kept_ref, _after, sorted_ref, came_ref, got_ref, q_ref, k_ref, kt_ref, p_ref, s_ref):
    tok = sorted_ref.shape[2]
    half = CS // 2
    info = came_ref[2 * half :, :].astype(F32)
    for d in range(4):
        got_ref[d] = jnp.max(info[d : d + 1, :]).astype(jnp.int32)
    outs = (q_ref, k_ref)

    def own(d, u, to):
        for i in range(2):
            outs[i][rows(to * unit, unit), :] = sorted_ref[d, i, rows(u * unit, unit), :]

    def got(at, to):
        for i in range(2):
            outs[i][rows(to * unit, unit), :] = came_ref[rows(i * half + at * unit, unit), :]

    each_unit(tok // unit, place, kept_ref, got_ref, own, got)
    kt_ref[...] = k_ref[...].astype(F32).T.astype(BF16)
    factor = HD**-0.5
    low = lax.broadcasted_iota(jnp.int32, (QB, QB), 0) <= lax.broadcasted_iota(jnp.int32, (QB, QB), 1)
    for j in range(CS // QB):
        q = q_ref[j * QB : (j + 1) * QB, :]
        top = None
        for i in range(j + 1):
            s = dot_nt(k_ref[i * QB : (i + 1) * QB, :], q) * factor
            if i == j:
                s = jnp.where(low, s, -1e30)
            s_ref[i * QB : (i + 1) * QB, :] = s
            peak = jnp.max(s.reshape(QB // 8, 8, QB), axis=0)
            top = peak if top is None else jnp.maximum(top, peak)
        top = jnp.max(top, axis=0, keepdims=True)
        total = None
        for i in range(j + 1):
            w = jnp.exp(s_ref[i * QB : (i + 1) * QB, :] - top)
            s_ref[i * QB : (i + 1) * QB, :] = w
            part = jnp.sum(w.reshape(QB // 8, 8, QB), axis=0)
            total = part if total is None else total + part
        scale = 1.0 / jnp.sum(total, axis=0, keepdims=True)
        for i in range(j + 1):
            p_ref[i * QB : (i + 1) * QB, j * QB : (j + 1) * QB] = (s_ref[i * QB : (i + 1) * QB, :] * scale).astype(BF16)


def mix_kernel(
    unit, place, kept_ref, got_ref, _after, sorted_ref, came_ref, p_ref, own, got, g_own, v_ref, ot_ref, edge_ref, vt
):
    tok = own.shape[1]

    @pl.when(place[1] == 0)
    def _():
        edge_ref[0] = own[0]
        edge_ref[1] = g_own[...]

    @pl.when(place[1] == 1)
    def _():
        edge_ref[0] = got[0]
        for h in range(HL // 2):
            at = CS // 2 + h * tok
            edge_ref[1, :, h * HD : (h + 1) * HD] = came_ref[at : at + tok, :]

    def kept(d, u, to):
        v_ref[rows(to * unit, unit), :] = sorted_ref[d, rows(u * unit, unit), :]

    def came(at, to):
        v_ref[rows(to * unit, unit), :] = came_ref[rows(at * unit, unit), :]

    each_unit(sorted_ref.shape[1] // unit, place, kept_ref, got_ref, kept, came)
    vt[...] = v_ref[...].astype(F32).T.astype(BF16)
    for j in range(CS // QB):
        end = (j + 1) * QB
        ot_ref[:, j * QB : end] = dot(vt[:, :end], p_ref[:end, j * QB : end])


def value_grads_kernel(unit, place, kept_ref, got_ref, _after, sorted_ref, came_ref, p_ref, g_ref, own_ref, back_ref, res):
    tok = sorted_ref.shape[1]

    def own(d, u, to):
        g_ref[rows(to * unit, unit), :] = sorted_ref[d, rows(u * unit, unit), :]

    def got(at, to):
        g_ref[rows(to * unit, unit), :] = came_ref[rows(at * unit, unit), :]

    each_unit(tok // unit, place, kept_ref, got_ref, own, got)
    for lo in range(0, CS, QB):
        res[lo : lo + QB, :] = dot(p_ref[lo : lo + QB, lo:], g_ref[lo:, :]).astype(BF16)

    def own_out(d, u, to):
        own_ref[d, 0, rows(u * unit, unit), :] = res[rows(to * unit, unit), :]

    def got_out(at, to):
        back_ref[0, rows(at * unit, unit), :] = res[rows(to * unit, unit), :]

    each_unit(tok // unit, place, kept_ref, got_ref, own_out, got_out)


def grads_kernel(
    unit, place, kept_ref, got_ref, _after, q_ref, k_ref, v_ref, kt_ref, ot_ref, p_ref, g_ref, own_ref, back_ref, dqt, res
):
    tok = own_ref.shape[2]
    delta = jnp.sum(g_ref[...].astype(F32).T * ot_ref[...], axis=0, keepdims=True)
    factor = HD**-0.5
    for lo in range(0, CS, QB):
        hi = lo + QB
        dp = dot_nt(v_ref[lo:hi, :], g_ref[lo:, :])
        ds = (p_ref[lo:hi, lo:].astype(F32) * (dp - delta[:, lo:])).astype(BF16)
        res[1, lo:hi, :] = (dot(ds, q_ref[lo:, :]) * factor).astype(BF16)
        part = dot(kt_ref[:, lo:hi], ds)
        dqt[:, lo:] = part if lo == 0 else dqt[:, lo:] + part
    res[0] = (dqt[...].T * factor).astype(BF16)

    def own_out(d, u, to):
        for i in range(2):
            own_ref[d, i, rows(u * unit, unit), :] = res[i, rows(to * unit, unit), :]

    def got_out(at, to):
        for i in range(2):
            back_ref[i, rows(at * unit, unit), :] = res[i, rows(to * unit, unit), :]

    each_unit(tok // unit, place, kept_ref, got_ref, own_out, got_out)


def unsort_kernel(unit, distances, kept_ref, _after, _after_edge, slot_col, own_ref, back_ref, *refs):
    *outs, full = refs
    tok = own_ref.shape[2]
    count = own_ref.shape[1]
    col_index = lax.broadcasted_iota(jnp.int32, (tok, tok), 1).astype(F32)
    offset = jnp.int32(0)
    for d in range(HR):
        kept = kept_ref[d]
        if d in distances:
            n = distances.index(d)

            def own(u, carry, d=d, n=n):
                for i in range(count):
                    full[n, i, rows(u * unit, unit), :] = own_ref[d, i, rows(u * unit, unit), :]
                return carry

            def got(u, carry, n=n, offset=offset, kept=kept):
                for i in range(count):
                    full[n, i, rows(u * unit, unit), :] = back_ref[i, rows((offset + u - kept) * unit, unit), :]
                return carry

            lax.fori_loop(0, kept, own, 0)
            lax.fori_loop(kept, tok // unit, got, 0)
            move = (col_index == slot_col[:, d : d + 1]).astype(BF16)
            for i in range(count):
                outs[n][i] = dot(move, full[n, i]).astype(BF16)
        offset = offset + tok // unit - kept


def window_kernel(
    place, _after, _after_edge, own, got, g_own, g_came, edge, dq_ref, early_ref, late_ref, stats_ref, *scratch
):
    tok = own.shape[1]
    pair = 2 * tok
    factor = HD**-0.5
    r = lax.broadcasted_iota(jnp.int32, (QB, QB), 0)
    c = lax.broadcasted_iota(jnp.int32, (QB, QB), 1)
    span = WIN + QB
    started = place[0] > 0
    own_at, got_at = place[1] * tok, (1 - place[1]) * tok
    for h in range(HL // 2):
        part = slice(h * HD, (h + 1) * HD)
        queries, grads, keys, values, kt, dk, dv = (ref.at[h] for ref in scratch)
        g_got = g_came[CS // 2 + h * tok : CS // 2 + (h + 1) * tok, :]
        for at, block, g_block in ((own_at, own, g_own[:, part]), (got_at, got, g_got)):
            queries[rows(at, tok), :] = block[0, :, part]
            grads[rows(at, tok), :] = g_block
            keys[rows(at + WIN, tok), :] = block[1, :, part]
            values[rows(at + WIN, tok), :] = block[2, :, part]
        keys[:WIN, :] = edge[0, :, part]
        values[:WIN, :] = edge[1, :, part]
        kt[...] = keys[...].astype(F32).T.astype(BF16)
        for j in range(pair // QB):
            lo, hi = j * QB, j * QB + span
            q = queries[j * QB : (j + 1) * QB, :]
            g = grads[j * QB : (j + 1) * QB, :]
            s = dot_nt(keys[lo:hi, :], q) * factor
            first = jnp.where(r > c, s[:QB], -1e30)
            last = jnp.where(r <= c, s[span - QB :], -1e30)
            s = jnp.concatenate([first, s[QB : span - QB], last], axis=0)
            if lo < WIN:
                s = jnp.concatenate([jnp.where(started, s[: WIN - lo], -1e30), s[WIN - lo :]], axis=0)
            top = jnp.max(s, axis=0, keepdims=True)
            w = jnp.exp(s - top)
            scale = 1.0 / jnp.sum(w, axis=0, keepdims=True)
            p = w * scale
            dp = dot_nt(values[lo:hi, :], g)
            delta = jnp.sum(p * dp, axis=0, keepdims=True)
            pb = p.astype(BF16)
            ds = (p * (dp - delta)).astype(BF16)
            side, at = divmod(j * QB, tok)
            dq_ref[side, at : at + QB, part] = (dot(kt[:, lo:hi], ds).T * factor).astype(BF16)
            if side == 0:
                for n, line in enumerate((top, scale, delta)):
                    stats_ref[3 * h + n : 3 * h + n + 1, at : at + QB] = line
            skip = max(0, WIN - lo)
            low = max(lo, WIN) - WIN
            part_k = dot(ds[skip:], q) * factor
            part_v = dot(pb[skip:], g)
            end = hi - WIN
            if end - QB > low:
                dk[low : end - QB, :] = dk[low : end - QB, :] + part_k[:-QB]
                dv[low : end - QB, :] = dv[low : end - QB, :] + part_v[:-QB]
            dk[end - QB : end, :] = part_k[-QB:]
            dv[end - QB : end, :] = part_v[-QB:]
        for i, total in enumerate((dk, dv)):
            early_ref[i, :, part] = total[:tok, :].astype(BF16)
            late_ref[i, :, part] = total[tok:, :]
    stats_ref[6:, :] = jnp.zeros((2, tok), F32)


def settle_kernel(place, _after, dq_ref, early_ref, late_ref, edge, ahead, stats, own, send, late):
    tok = edge.shape[1]
    factor = HD**-0.5
    r = lax.broadcasted_iota(jnp.int32, (QB, QB), 0)
    c = lax.broadcasted_iota(jnp.int32, (QB, QB), 1)
    for h in range(HL // 2):
        part = slice(h * HD, (h + 1) * HD)
        for j in range(tok // QB):
            at = slice(j * QB, (j + 1) * QB)
            q, g = ahead[0, at, part], ahead[1, at, part]
            top, scale, delta = (stats[3 * h + n : 3 * h + n + 1, at] for n in range(3))
            s = dot_nt(edge[0, j * QB :, part], q) * factor
            p = jnp.exp(s - top) * scale
            first = jnp.where(r > c, p[:QB], 0.0)
            p = first if j == tok // QB - 1 else jnp.concatenate([first, p[QB:]], axis=0)
            ds = p * (dot_nt(edge[1, j * QB :, part], g) - delta)
            add_k = dot(ds.astype(BF16), q) * factor
            add_v = dot(p.astype(BF16), g)
            for i, add in enumerate((add_k, add_v)):
                base = late_ref[i, :, part] if j == 0 else late[h, i, j * QB :, :]
                late[h, i, j * QB :, :] = base + add
    for side, (near, far) in enumerate(((own, send), (send, own))):

        @pl.when(place[1] == side)
        def _(near=near, far=far):
            near[0] = dq_ref[0]
            near[1:] = early_ref[...]
            far[0] = dq_ref[1]
            for h in range(HL // 2):
                for i in range(2):
                    far[1 + i, :, h * HD : (h + 1) * HD] = late[h, i].astype(BF16)


def join_value_kernel(place, _after, v0, v1, v2, v3, out):
    for d, v in enumerate((v0, v1, v2, v3)):
        out[:, head_columns(place, d)] = v[0]


def join_kernel(place, value_ref, y0, y1, y2, y3, own, got, dq_ref, dk_ref, dv_ref):
    outs = (dq_ref, dk_ref, dv_ref)
    dv_ref[:, : HR * HD] = value_ref[...]
    for d, y in enumerate((y0, y1, y2, y3)):
        at = head_columns(place, d)
        for i in range(2):
            outs[i][:, at] = y[i]
    width = HL * HD // 2
    for n in range(2):
        side = place[1] if n == 0 else 1 - place[1]
        at = pl.ds(pl.multiple_of(HR * HD + side * width, width), width)
        for i in range(3):
            outs[i][:, at] = own[i] if n == 0 else got[i]


def struct(*shape, dtype=BF16):
    return jax.ShapeDtypeStruct(shape, dtype)


def pair_body(query, key, value, grad_sent, out_weight, assign):
    tok = query.shape[1]
    devices = lax.axis_size("seq")
    place = lax.axis_index("seq")
    first, side = place // 2, place % 2
    where = jnp.stack([first, side]).astype(jnp.int32)
    unit = CS // (4 * devices)
    half = CS // 2

    def among_groups(block, shift):
        route = [(i, ((i // 2 + shift) % HR) * 2 + i % 2) for i in range(devices)]
        return lax.ppermute(block, "seq", route)

    def swap(block):
        return lax.ppermute(block, "seq", [(i, i ^ 1) for i in range(devices)])

    hbm = [pl.BlockSpec(memory_space=pltpu.HBM)]
    width = HL * HD // 2
    boundary = from_behind(grad_sent, "section", -1)[0]
    *sent, local_own, local_send = pl.pallas_call(
        split_kernel,
        out_shape=[struct(2 * tok + 16, HD)] * HR + [struct(3, tok, width)] * 2,
        in_specs=smem() + vmem() + hbm * 3,
        out_specs=vmem(6),
        scratch_shapes=[pltpu.VMEM((3, tok, query.shape[2]), BF16), pltpu.SemaphoreType.DMA((3, 4))],
        compiler_params=params(SPLIT_MIB),
        cost_estimate=takes(2),
        name="split",
    )(where, assign[0], query[0], key[0], value[0])
    arrived = [sent[0]] + [among_groups(sent[d], d) for d in range(1, HR)]
    local_got = swap(local_send)
    v_sent = pl.pallas_call(
        split_value_kernel,
        out_shape=[struct(tok, HD)] * HR,
        in_specs=smem() + vmem(4),
        out_specs=vmem(4),
        compiler_params=params(20),
        cost_estimate=takes(1),
        name="split_value",
    )(where, *arrived[1:], value[0])
    v_arrived = [v_sent[0]] + [among_groups(v_sent[d], d) for d in range(1, HR)]

    ordered, send, slot_row, slot_col, kept = pl.pallas_call(
        functools.partial(pack_kernel, unit),
        out_shape=[
            struct(HR, 2, tok, HD),
            struct(2 * half + 16, HD),
            struct(8, tok, dtype=F32),
            struct(tok, HD, dtype=F32),
            struct(HR, dtype=jnp.int32),
        ],
        in_specs=smem() + vmem(5),
        out_specs=vmem(4) + smem(),
        compiler_params=params(20),
        cost_estimate=takes(2.6),
        name="pack",
    )(where, v_sent[0], *arrived)
    came = swap(send)

    *g_sent, g_own, g_send = pl.pallas_call(
        project_kernel,
        grid=(4,),
        out_shape=[struct(tok, HD)] * HR + [struct(tok, width)] * 2,
        in_specs=smem()
        + [
            pl.BlockSpec((16, HD), lambda n: (0, 0)),
            pl.BlockSpec((1, 16, HD), lambda n: (0, 0, 0)),
            pl.BlockSpec(boundary.shape, lambda n: (0, 0)),
            pl.BlockSpec((2 * HD, boundary.shape[1]), lambda n: (n, 0)),
        ],
        out_specs=[pl.BlockSpec((tok, HD), lambda n: (0, 0))] * HR
        + [pl.BlockSpec((tok, width), lambda n: (0, 0))] * 2,
        compiler_params=params(20),
        cost_estimate=takes(3.8),
        name="project",
    )(where, send, local_got, boundary, out_weight[0])
    g_arrived = [g_sent[0]] + [among_groups(g_sent[d], d) for d in range(1, HR)]

    v_ordered, v_out = pl.pallas_call(
        functools.partial(pack_value_kernel, unit),
        out_shape=[struct(HR, tok, HD), struct(half + HL // 2 * tok, HD)],
        in_specs=smem() + vmem(7),
        out_specs=vmem(2),
        compiler_params=params(20),
        cost_estimate=takes(1.6),
        name="pack_value",
    )(kept, g_sent[0], slot_row, *v_arrived, g_send)
    v_came = swap(v_out)

    got, q, k, kt, p = pl.pallas_call(
        functools.partial(probs_kernel, unit),
        out_shape=[struct(HR, dtype=jnp.int32)] + [struct(CS, HD)] * 2 + [struct(HD, CS), struct(CS, CS)],
        in_specs=smem(2) + vmem(3),
        out_specs=smem() + vmem(4),
        scratch_shapes=[pltpu.VMEM((CS, QB), F32)],
        compiler_params=params(24),
        cost_estimate=takes(5),
        name="probs",
    )(where, kept, v_out, ordered, came)

    g_ordered, g_out, edge = pl.pallas_call(
        functools.partial(pack_grad_kernel, unit),
        out_shape=[struct(HR, tok, HD), struct(half, HD), struct(2, tok, width)],
        in_specs=smem(2) + vmem(8),
        out_specs=vmem(3),
        compiler_params=params(20),
        cost_estimate=takes(1.6),
        name="pack_grad",
    )(where, kept, kt, slot_row, *g_arrived, local_own, local_got)
    g_came = swap(g_out)
    ahead = [(i, i + 2) for i in range(devices - 2)]
    behind = [(i + 2, i) for i in range(devices - 2)]
    edge_got = lax.ppermute(edge, "seq", ahead)

    v, ot, query_edge = pl.pallas_call(
        functools.partial(mix_kernel, unit),
        out_shape=[struct(CS, HD), struct(HD, CS, dtype=F32), struct(2, tok, width)],
        in_specs=smem(3) + vmem(7),
        out_specs=vmem(3),
        scratch_shapes=[pltpu.VMEM((HD, CS), BF16)],
        compiler_params=params(20),
        cost_estimate=takes(1.7),
        name="mix",
    )(where, kept, got, edge, v_ordered, v_came, p, local_own, local_got, g_own)
    query_edge_got = lax.ppermute(query_edge, "seq", behind)

    g, own_v, back_v = pl.pallas_call(
        functools.partial(value_grads_kernel, unit),
        out_shape=[struct(CS, HD), struct(HR, 1, tok, HD), struct(1, half, HD)],
        in_specs=smem(3) + vmem(4),
        out_specs=vmem(3),
        scratch_shapes=[pltpu.VMEM((CS, HD), BF16)],
        compiler_params=params(16),
        cost_estimate=takes(2.4),
        name="value_grads",
    )(where, kept, got, ot, g_ordered, g_came, p)
    own, back = pl.pallas_call(
        functools.partial(grads_kernel, unit),
        out_shape=[struct(HR, 2, tok, HD), struct(2, half, HD)],
        in_specs=smem(3) + vmem(8),
        out_specs=vmem(2),
        scratch_shapes=[pltpu.VMEM((HD, CS), F32), pltpu.VMEM((2, CS, HD), BF16)],
        compiler_params=params(24),
        cost_estimate=takes(5),
        name="grads",
    )(where, kept, got, back_v, q, k, v, kt, ot, p, g)

    def unsort(distances, after, after_edge, own, returned, name):
        count = own.shape[1]
        return pl.pallas_call(
            functools.partial(unsort_kernel, unit, distances),
            out_shape=[struct(count, tok, HD)] * len(distances),
            in_specs=smem() + vmem(5),
            out_specs=vmem(len(distances)),
            scratch_shapes=[pltpu.VMEM((len(distances), count, tok, HD), BF16)],
            compiler_params=params(20),
            cost_estimate=takes({'unsort_value':2.6,'unsort_first':0.1,'unsort_last':1.4}[name]),
            name=name,
        )(kept, after, after_edge, slot_col, own, returned)

    returned_v, returned = swap(back_v), swap(back)
    pair = 2 * tok
    natural_v = unsort((0, 1, 2, 3), back, back, own_v, returned_v, "unsort_value")
    home_v = [natural_v[0]] + [among_groups(natural_v[d], -d) for d in range(1, HR)]
    dq_local, early, late, stats = pl.pallas_call(
        window_kernel,
        out_shape=[
            struct(2, tok, width),
            struct(2, tok, width),
            struct(2, tok, width, dtype=F32),
            struct(8, tok, dtype=F32),
        ],
        in_specs=smem() + vmem(7),
        out_specs=vmem(4),
        scratch_shapes=[
            pltpu.VMEM((HL // 2, pair, HD), BF16),
            pltpu.VMEM((HL // 2, pair, HD), BF16),
            pltpu.VMEM((HL // 2, pair + WIN, HD), BF16),
            pltpu.VMEM((HL // 2, pair + WIN, HD), BF16),
            pltpu.VMEM((HL // 2, HD, pair + WIN), BF16),
            pltpu.VMEM((HL // 2, pair, HD), F32),
            pltpu.VMEM((HL // 2, pair, HD), F32),
        ],
        compiler_params=params(24),
        cost_estimate=takes(0.1),
        name="window",
    )(where, natural_v[0], query_edge_got, local_own, local_got, g_own, v_came, edge_got)
    stats_got = lax.ppermute(stats, "seq", behind)
    first_natural = unsort((0, 1, 2), stats, stats, own, returned, "unsort_first")
    settled_own, settled_send = pl.pallas_call(
        settle_kernel,
        out_shape=[struct(3, tok, width)] * 2,
        in_specs=smem() + vmem(7),
        out_specs=vmem(2),
        scratch_shapes=[pltpu.VMEM((HL // 2, 2, tok, HD), F32)],
        compiler_params=params(20),
        cost_estimate=takes(0.1),
        name="settle",
    )(where, first_natural[0], dq_local, early, late, edge, query_edge_got, stats_got)
    settled_got = swap(settled_send)
    value_left = pl.pallas_call(
        join_value_kernel,
        out_shape=struct(tok, HR * HD),
        in_specs=smem() + vmem(5),
        out_specs=vmem()[0],
        compiler_params=params(16),
        cost_estimate=takes(12),
        name="join_value",
    )(where, settled_send, *home_v)
    last_natural = unsort((3,), value_left, value_left, own, returned, "unsort_last")
    natural = [*first_natural, *last_natural]
    home = [natural[0]] + [among_groups(natural[d], -d) for d in range(1, HR)]

    outs = pl.pallas_call(
        join_kernel,
        out_shape=[struct(tok, (HR + HL) * HD)] * 3,
        in_specs=smem() + vmem(7),
        out_specs=vmem(3),
        compiler_params=params(20),
        cost_estimate=takes(2.8),
        name="join",
    )(where, value_left, *home, settled_own, settled_got)
    return tuple(out[None] for out in outs)


def from_behind(block, axis, distance):
    devices = range(lax.axis_size(axis))
    route = [((i - distance) % len(devices), i) for i in devices]
    return lax.ppermute(block, axis, route)


def shifted(block, axis, distance):
    devices = range(lax.axis_size(axis))
    route = [(i - distance, i) for i in devices if i - distance in devices]
    return lax.ppermute(block, axis, route)


def cluster_block(query_rows, key_rows, value_rows, grad_rows, allowed, factor):
    scores = jnp.dot(query_rows, key_rows.T, preferred_element_type=jnp.float32) * factor
    scores = jnp.where(allowed, scores, -1e30)
    highest = jnp.max(scores, axis=1, keepdims=True)
    weights = jnp.exp(scores - highest)
    probs = weights / jnp.sum(weights, axis=1, keepdims=True)
    dprob = jnp.dot(grad_rows, value_rows.T, preferred_element_type=jnp.float32)
    delta = jnp.sum(probs * dprob, axis=1, keepdims=True)
    dscore = probs * (dprob - delta)
    probs_b = probs.astype(jnp.bfloat16)
    dscore_b = dscore.astype(jnp.bfloat16)
    grad_query = jnp.dot(dscore_b, key_rows, preferred_element_type=jnp.float32) * factor
    grad_key = jnp.dot(dscore_b.T, query_rows, preferred_element_type=jnp.float32) * factor
    grad_value = jnp.dot(probs_b.T, grad_rows, preferred_element_type=jnp.float32)
    return (grad_query, grad_key, grad_value)


def cluster_grads(query_rows, key_rows, value_rows, grad_rows, factor):
    length = query_rows.shape[0]
    span = min(512, length)
    pieces = []
    total_key = jnp.zeros(key_rows.shape, jnp.float32)
    total_value = jnp.zeros(value_rows.shape, jnp.float32)
    for index in range(length // span):
        first = index * span
        end = first + span
        allowed = (
            jnp.arange(end, dtype=jnp.int32)[None, :]
            <= (first + jnp.arange(span, dtype=jnp.int32))[:, None]
        )
        part_query, part_key, part_value = cluster_block(
            query_rows[first:end],
            key_rows[:end],
            value_rows[:end],
            grad_rows[first:end],
            allowed,
            factor,
        )
        pieces.append(part_query)
        total_key = total_key.at[:end].add(part_key)
        total_value = total_value.at[:end].add(part_value)
    return (jnp.concatenate(pieces, axis=0), total_key, total_value)


def window_block(query_rows, key_rows, value_rows, grad_rows, allowed, factor):
    scores = (
        jnp.einsum("qhd,khd->hqk", query_rows, key_rows, preferred_element_type=jnp.float32)
        * factor
    )
    scores = jnp.where(allowed[None], scores, -1e30)
    highest = jnp.max(scores, axis=2, keepdims=True)
    weights = jnp.exp(scores - highest)
    probs = weights / jnp.sum(weights, axis=2, keepdims=True)
    dprob = jnp.einsum("qhd,khd->hqk", grad_rows, value_rows, preferred_element_type=jnp.float32)
    delta = jnp.sum(probs * dprob, axis=2, keepdims=True)
    dscore = probs * (dprob - delta)
    probs_b = probs.astype(jnp.bfloat16)
    dscore_b = dscore.astype(jnp.bfloat16)
    grad_query = (
        jnp.einsum("hqk,khd->qhd", dscore_b, key_rows, preferred_element_type=jnp.float32) * factor
    )
    grad_key = (
        jnp.einsum("hqk,qhd->khd", dscore_b, query_rows, preferred_element_type=jnp.float32)
        * factor
    )
    grad_value = jnp.einsum("hqk,qhd->khd", probs_b, grad_rows, preferred_element_type=jnp.float32)
    return (grad_query, grad_key, grad_value)


def window_mask(query_pos, key_pos):
    return (
        (key_pos[None, :] > query_pos[:, None] - WIN)
        & (key_pos[None, :] <= query_pos[:, None])
        & (key_pos[None, :] >= 0)
    )


def general_body(query, key, value, grad_sent, out_weight, assign):
    tok_rows = query.shape[1]
    heads = HR + HL
    devices = lax.axis_size("seq")
    place = lax.axis_index("seq")
    factor = HD ** (-0.5)
    boundary = from_behind(grad_sent, "section", -1)[0]
    attn_grad = lax.dot_general(
        boundary, out_weight[0], (((1,), (1,)), ((), ())), preferred_element_type=jnp.float32
    ).astype(jnp.bfloat16)
    query_heads = query[0].reshape(tok_rows, heads, HD)
    key_heads = key[0].reshape(tok_rows, heads, HD)
    value_heads = value[0].reshape(tok_rows, heads, HD)
    grad_heads = attn_grad.reshape(tok_rows, heads, HD)
    clusters = tok_rows * devices // CS
    owned = HR * tok_rows // CS
    capacity = 7 * CS // (4 * devices)
    unit_rows = capacity // 7
    width = owned * capacity
    head_slots = clusters * capacity
    labels = assign[0]
    members = (labels[:, :, None] == jnp.arange(clusters, dtype=jnp.int32)[None, None, :]).astype(
        jnp.bfloat16
    )
    token_ids = jnp.arange(tok_rows, dtype=jnp.int32)
    lower = (token_ids[:, None] >= token_ids[None, :]).astype(jnp.bfloat16)
    running_counts = jnp.einsum("ts,hsc->htc", lower, members, preferred_element_type=jnp.float32)
    ranks = (jnp.sum(running_counts * members.astype(jnp.float32), axis=2) - 1.0).astype(jnp.int32)
    local_slot = labels * capacity + ranks
    slot_hit = jnp.arange(head_slots, dtype=jnp.int32)[None, :, None] == local_slot[:, None, :]
    slot_table = slot_hit.astype(jnp.bfloat16)
    routed_in = jnp.concatenate(
        [query_heads[:, :HR], key_heads[:, :HR], value_heads[:, :HR], grad_heads[:, :HR]], axis=2
    )
    packed = jnp.einsum(
        "hst,thd->hsd", slot_table, routed_in, preferred_element_type=jnp.float32
    ).astype(jnp.bfloat16)
    packed = packed.reshape(devices, width, 4 * HD)
    token_pos = place * tok_rows + token_ids
    slot_pos = jnp.max(jnp.where(slot_hit, token_pos[None, None, :], -1), axis=2).reshape(
        devices, width
    )
    send_query = packed[:, :, :HD]
    send_key = packed[:, :, HD : 2 * HD]
    send_value = packed[:, :, 2 * HD : 3 * HD]
    send_grad = packed[:, :, 3 * HD :]
    arrived_query, arrived_key, arrived_value, arrived_grad, arrived_pos = (
        lax.all_to_all(send_query, "seq", split_axis=0, concat_axis=0, tiled=True),
        lax.all_to_all(send_key, "seq", split_axis=0, concat_axis=0, tiled=True),
        lax.all_to_all(send_value, "seq", split_axis=0, concat_axis=0, tiled=True),
        lax.all_to_all(send_grad, "seq", split_axis=0, concat_axis=0, tiled=True),
        lax.all_to_all(slot_pos, "seq", split_axis=0, concat_axis=0, tiled=True),
    )
    arrived_all = jnp.concatenate([arrived_query, arrived_key, arrived_value, arrived_grad], axis=2)
    unit_index = jnp.arange(7, dtype=jnp.int32)
    target_units = jnp.arange(CS // unit_rows, dtype=jnp.int32)
    block = arrived_all.reshape(devices * 7, unit_rows * 4 * HD)
    live_counts = jnp.sum((arrived_pos >= 0).astype(jnp.int32), axis=1)
    units = live_counts // unit_rows
    starts = jnp.cumsum(units) - units
    picker = (target_units[:, None, None] == starts[None, :, None] + unit_index[None, None, :]) & (
        unit_index[None, None, :] < units[None, :, None]
    )
    picker = picker.reshape(CS // unit_rows, devices * 7).astype(jnp.bfloat16)
    compact = (
        jnp.dot(picker, block, preferred_element_type=jnp.float32)
        .astype(jnp.bfloat16)
        .reshape(CS, 4 * HD)
    )
    results = cluster_grads(
        compact[:, :HD],
        compact[:, HD : 2 * HD],
        compact[:, 2 * HD : 3 * HD],
        compact[:, 3 * HD :],
        factor,
    )
    answer = jnp.concatenate([result.astype(jnp.bfloat16) for result in results], axis=1).reshape(
        CS // unit_rows, unit_rows * 3 * HD
    )
    spread = jnp.dot(picker.T, answer, preferred_element_type=jnp.float32).astype(jnp.bfloat16)
    outgoing = spread.reshape(devices, capacity, 3 * HD)
    back_query, back_key, back_value = (
        lax.all_to_all(outgoing[:, :, :HD], "seq", split_axis=0, concat_axis=0, tiled=True),
        lax.all_to_all(outgoing[:, :, HD : 2 * HD], "seq", split_axis=0, concat_axis=0, tiled=True),
        lax.all_to_all(outgoing[:, :, 2 * HD :], "seq", split_axis=0, concat_axis=0, tiled=True),
    )
    back_all = jnp.concatenate([back_query, back_key, back_value], axis=2).reshape(
        HR, head_slots, 3 * HD
    )
    routed_out = jnp.einsum(
        "hst,hsd->thd", slot_table, back_all, preferred_element_type=jnp.float32
    ).astype(jnp.bfloat16)
    routed_query = routed_out[:, :, :HD]
    routed_key = routed_out[:, :, HD : 2 * HD]
    routed_value = routed_out[:, :, 2 * HD :]
    local_query = query_heads[:, HR:]
    local_key = key_heads[:, HR:]
    local_value = value_heads[:, HR:]
    local_grad = grad_heads[:, HR:]
    prior_key, prior_value = shifted((local_key, local_value), "seq", 1)
    keys_all = jnp.concatenate([prior_key, local_key], axis=0)
    values_all = jnp.concatenate([prior_value, local_value], axis=0)
    key_positions = (place - 1) * tok_rows + jnp.arange(2 * tok_rows, dtype=jnp.int32)
    query_positions = place * tok_rows + jnp.arange(tok_rows, dtype=jnp.int32)
    span = min(512, tok_rows)
    total_key = jnp.zeros((2 * tok_rows, HL, HD), jnp.float32)
    total_value = jnp.zeros((2 * tok_rows, HL, HD), jnp.float32)
    start = tok_rows - WIN
    allowed = window_mask(query_positions, key_positions)
    part_query, part_key, part_value = window_block(
        local_query, keys_all, values_all, local_grad, allowed, factor
    )
    total_key = total_key.at[start : start + span + WIN].add(part_key)
    total_value = total_value.at[start : start + span + WIN].add(part_value)
    tail = tok_rows - WIN
    carried_key, carried_value = (
        shifted(total_key[tail:tok_rows].astype(jnp.bfloat16), "seq", -1).astype(jnp.float32),
        shifted(total_value[tail:tok_rows].astype(jnp.bfloat16), "seq", -1).astype(jnp.float32),
    )
    local_dk = total_key[tok_rows:].at[tail:].add(carried_key)
    local_dv = total_value[tok_rows:].at[tail:].add(carried_value)
    local_dq = part_query.astype(jnp.bfloat16)
    grad_query = jnp.concatenate([routed_query, local_dq], axis=1).reshape(1, tok_rows, heads * HD)
    grad_key = jnp.concatenate([routed_key, local_dk.astype(jnp.bfloat16)], axis=1).reshape(
        1, tok_rows, heads * HD
    )
    grad_value = jnp.concatenate([routed_value, local_dv.astype(jnp.bfloat16)], axis=1).reshape(
        1, tok_rows, heads * HD
    )
    return (grad_query, grad_key, grad_value)


def body(query, key, value, grad_sent, out_weight, assign):
    clusters = query.shape[1] * lax.axis_size("seq") // CS
    plan = pair_body if clusters == 2 else general_body
    return plan(query, key, value, grad_sent, out_weight, assign)


def solution(mesh):
    placed = (
        P("section", "seq", None),
        P("section", "seq", None),
        P("section", "seq", None),
        P("section", "seq", None),
        P("section", None, None),
        P("section", None, "seq"),
    )
    return jax.shard_map(
        body,
        mesh=mesh,
        in_specs=placed,
        out_specs=(P("section", "seq", None), P("section", "seq", None), P("section", "seq", None)),
        check_vma=False,
    )
```

```python
import functools

import jax
import jax.numpy as jnp
from jax import lax
from jax.experimental import pallas as pl
from jax.experimental.pallas import tpu as pltpu
from jax.sharding import PartitionSpec as P

HR = 4
HL = 4
HD = 128
CS = 2048
WIN = 512
QB = 256
MIB = 1024 * 1024
SPLIT_MIB = 56
NT = (((1,), (1,)), ((), ()))
F32 = jnp.float32
BF16 = jnp.bfloat16


def vmem(count=1):
    return [pl.BlockSpec(memory_space=pltpu.VMEM)] * count


def smem(count=1):
    return [pl.BlockSpec(memory_space=pltpu.SMEM)] * count


def params(mib):
    return pltpu.CompilerParams(vmem_limit_bytes=mib * MIB)


def dot(a, b):
    return jnp.dot(a, b, preferred_element_type=F32)


def dot_nt(a, b):
    return lax.dot_general(a, b, NT, preferred_element_type=F32)


def takes(microseconds):
    return pl.CostEstimate(
        flops=int(microseconds * 1.1e9), bytes_accessed=int(microseconds * 3.5e6), transcendentals=0
    )


def rows(start, size):
    return pl.ds(pl.multiple_of(start, size), size)


def start_all(copies):
    for copy in copies:
        copy.start()


def wait_all(copies):
    for copy in copies:
        copy.wait()


def head_columns(place, d):
    return pl.ds(pl.multiple_of(lax.rem(place[0] + d, HR) * HD, HD), HD)


def split_kernel(place, labels, q_hbm, k_hbm, v_hbm, x0, x1, x2, x3, own, send, held, sems):
    tok = q_hbm.shape[0]
    cuts = sems.shape[1]
    size = tok // cuts
    copies = []
    for i, source in enumerate((q_hbm, k_hbm, v_hbm)):
        for n in range(cuts):
            at = slice(n * size, (n + 1) * size)
            copies.append(pltpu.make_async_copy(source.at[at], held.at[i, at], sems.at[i, n]))
    start_all(copies)
    for d, x in enumerate((x0, x1, x2, x3)):
        line = labels[pl.ds(lax.rem(place[0] + d, HR), 1), :].astype(F32)
        parts = [line[:, r * HD : (r + 1) * HD] for r in range(tok // HD)]
        parts.append(jnp.zeros((16 - tok // HD, HD), F32))
        x[2 * tok :, :] = jnp.concatenate(parts, axis=0).astype(BF16)
    width = HL * HD // 2
    for i in range(3):
        wait_all(copies[i * cuts : (i + 1) * cuts])
        for d, x in enumerate((x0, x1, x2, x3)):
            if i < 2:
                x[i * tok : (i + 1) * tok, :] = held[i, :, head_columns(place, d)]
        for out, side in ((send, 1 - place[1]), (own, place[1])):
            out[i] = held[i, :, pl.ds(pl.multiple_of(HR * HD + side * width, width), width)]


def split_value_kernel(place, _after, _after1, _after2, _after3, v_ref, x0, x1, x2, x3):
    for d, x in enumerate((x0, x1, x2, x3)):
        x[...] = v_ref[:, head_columns(place, d)]


def project_kernel(place, _after_local, rows_ref, weight, g0, g1, g2, g3, own_ref, send_ref):
    step = pl.program_id(0)
    part = dot_nt(rows_ref[...], weight[...]).astype(BF16)

    @pl.when(step < HR // 2)
    def _():
        for i in range(2):
            d = lax.rem(2 * step + i - place[0] + 4, 4)
            for e, g in enumerate((g0, g1, g2, g3)):

                @pl.when(d == e)
                def _(g=g, i=i):
                    g[...] = part[:, i * HD : (i + 1) * HD]

    @pl.when(step >= HR // 2)
    def _():
        @pl.when(step - HR // 2 == place[1])
        def _():
            own_ref[...] = part

        @pl.when(step - HR // 2 != place[1])
        def _():
            send_ref[...] = part


def pack_kernel(unit, place, _after, x0, x1, x2, x3, sorted_ref, send_ref, slot_row, slot_col, kept_ref):
    tok = x0.shape[0] - 16
    tok = tok // 2
    side = place[1]
    lane = lax.broadcasted_iota(jnp.int32, (1, tok), 1).astype(F32)
    labels = []
    for x in (x0, x1, x2, x3):
        block = x[2 * tok :, :].astype(F32)
        labels.append(jnp.concatenate([block[r : r + 1, :] for r in range(tok // 128)], axis=1))
    label = jnp.concatenate(labels + [jnp.zeros((4, tok), F32)], axis=0)
    upper = (
        lax.broadcasted_iota(jnp.int32, (tok, tok), 0) <= lax.broadcasted_iota(jnp.int32, (tok, tok), 1)
    ).astype(BF16)
    ones = dot(label.astype(BF16), upper)
    totals = [jnp.sum(row).astype(jnp.int32) for row in labels]
    whole = totals[0] + totals[1] + totals[2] + totals[3]
    half = CS // 2
    keep_one = jnp.where(side == 0, (whole > half).astype(jnp.int32), (whole >= half).astype(jnp.int32))
    keep_f = keep_one.astype(F32)
    slots = []
    for d in range(4):
        kept = jnp.where(keep_one == 1, totals[d], tok - totals[d])
        kept_ref[d] = kept // unit
        is_kept = labels[d] * keep_f + (1.0 - labels[d]) * (1.0 - keep_f)
        ones_d = ones[d : d + 1, :]
        count = ones_d * keep_f + (lane + 1.0 - ones_d) * (1.0 - keep_f)
        slot = jnp.where(is_kept > 0.5, count - 1.0, kept.astype(F32) + lane - count)
        slots.append(slot)
    slots_all = jnp.concatenate(slots + [jnp.zeros((124, tok), F32)], axis=0)
    slot_row[...] = slots_all[:8, :]
    slot_col[...] = slots_all.T
    row_index = lax.broadcasted_iota(jnp.int32, (tok, tok), 0).astype(F32)
    for d, x in enumerate((x0, x1, x2, x3)):
        move = (row_index == slots[d]).astype(BF16)
        for i in range(2):
            sorted_ref[d, i] = dot(move, x[i * tok : (i + 1) * tok, :]).astype(BF16)
    offset = jnp.int32(0)
    info_row = lax.broadcasted_iota(jnp.int32, (16, HD), 0)
    info = jnp.zeros((16, HD), F32)
    for d in range(4):
        kept = kept_ref[d]
        info = jnp.where(info_row == d, kept.astype(F32), info)

        def put(u, carry, d=d, offset=offset, kept=kept):
            for i in range(2):
                send_ref[rows(i * half + (offset + u - kept) * unit, unit), :] = sorted_ref[d, i, rows(u * unit, unit), :]
            return carry

        lax.fori_loop(kept, tok // unit, put, 0)
        offset = offset + tok // unit - kept
    send_ref[2 * half :, :] = info.astype(BF16)


def pack_value_kernel(unit, kept_ref, _after, _after_swap, slot_row, x0, x1, x2, x3, sorted_ref, send_ref):
    pack_one(unit, kept_ref, slot_row, (x0, x1, x2, x3), sorted_ref, send_ref)


def pack_grad_kernel(
    unit, place, kept_ref, _after, slot_row, x0, x1, x2, x3, own, got, sorted_ref, send_ref, edge_ref
):
    pack_one(unit, kept_ref, slot_row, (x0, x1, x2, x3), sorted_ref, send_ref)
    for side, block in ((1, own), (0, got)):

        @pl.when(place[1] == side)
        def _(block=block):
            edge_ref[...] = block[1:]


def pack_one(unit, kept_ref, slot_row, blocks, sorted_ref, send_ref):
    tok = sorted_ref.shape[1]
    row_index = lax.broadcasted_iota(jnp.int32, (tok, tok), 0).astype(F32)
    for d, x in enumerate(blocks):
        move = (row_index == slot_row[d : d + 1, :]).astype(BF16)
        sorted_ref[d] = dot(move, x[...]).astype(BF16)
    offset = jnp.int32(0)
    for d in range(4):
        kept = kept_ref[d]

        def put(u, carry, d=d, offset=offset, kept=kept):
            send_ref[rows((offset + u - kept) * unit, unit), :] = sorted_ref[d, rows(u * unit, unit), :]
            return carry

        lax.fori_loop(kept, tok // unit, put, 0)
        offset = offset + tok // unit - kept


def each_unit(units, place, kept_ref, got_ref, own, got):
    first, side = place[0], place[1]
    pos = jnp.int32(0)
    for z in range(4):
        d = lax.rem(first - z + 4, 4)
        kept = kept_ref[d]
        came = units - got_ref[d]
        at = jnp.int32(0)
        for e in range(4):
            at = at + jnp.where(e < d, units - got_ref[e], 0)
        own_pos = pos + jnp.where(side == 0, 0, came)
        got_pos = pos + jnp.where(side == 0, kept, 0)

        def own_step(u, carry, d=d, own_pos=own_pos):
            own(d, u, own_pos + u)
            return carry

        def got_step(u, carry, at=at, got_pos=got_pos):
            got(at + u, got_pos + u)
            return carry

        lax.fori_loop(0, kept, own_step, 0)
        lax.fori_loop(0, came, got_step, 0)
        pos = pos + kept + came


def probs_kernel(unit, place, kept_ref, _after, sorted_ref, came_ref, got_ref, q_ref, k_ref, kt_ref, p_ref, s_ref):
    tok = sorted_ref.shape[2]
    half = CS // 2
    info = came_ref[2 * half :, :].astype(F32)
    for d in range(4):
        got_ref[d] = jnp.max(info[d : d + 1, :]).astype(jnp.int32)
    outs = (q_ref, k_ref)

    def own(d, u, to):
        for i in range(2):
            outs[i][rows(to * unit, unit), :] = sorted_ref[d, i, rows(u * unit, unit), :]

    def got(at, to):
        for i in range(2):
            outs[i][rows(to * unit, unit), :] = came_ref[rows(i * half + at * unit, unit), :]

    each_unit(tok // unit, place, kept_ref, got_ref, own, got)
    kt_ref[...] = k_ref[...].astype(F32).T.astype(BF16)
    factor = HD**-0.5
    low = lax.broadcasted_iota(jnp.int32, (QB, QB), 0) <= lax.broadcasted_iota(jnp.int32, (QB, QB), 1)
    for j in range(CS // QB):
        q = q_ref[j * QB : (j + 1) * QB, :]
        top = None
        for i in range(j + 1):
            s = dot_nt(k_ref[i * QB : (i + 1) * QB, :], q) * factor
            if i == j:
                s = jnp.where(low, s, -1e30)
            s_ref[i * QB : (i + 1) * QB, :] = s
            peak = jnp.max(s.reshape(QB // 8, 8, QB), axis=0)
            top = peak if top is None else jnp.maximum(top, peak)
        top = jnp.max(top, axis=0, keepdims=True)
        total = None
        for i in range(j + 1):
            w = jnp.exp(s_ref[i * QB : (i + 1) * QB, :] - top)
            s_ref[i * QB : (i + 1) * QB, :] = w
            part = jnp.sum(w.reshape(QB // 8, 8, QB), axis=0)
            total = part if total is None else total + part
        scale = 1.0 / jnp.sum(total, axis=0, keepdims=True)
        for i in range(j + 1):
            p_ref[i * QB : (i + 1) * QB, j * QB : (j + 1) * QB] = (s_ref[i * QB : (i + 1) * QB, :] * scale).astype(BF16)


def mix_kernel(
    unit, place, kept_ref, got_ref, _after, sorted_ref, came_ref, p_ref, own, got, g_own, g_got, v_ref, ot_ref, edge_ref, vt
):
    tok = own.shape[1]

    @pl.when(place[1] == 0)
    def _():
        edge_ref[0] = own[0]
        edge_ref[1] = g_own[...]

    @pl.when(place[1] == 1)
    def _():
        edge_ref[0] = got[0]
        edge_ref[1] = g_got[...]

    def kept(d, u, to):
        v_ref[rows(to * unit, unit), :] = sorted_ref[d, rows(u * unit, unit), :]

    def came(at, to):
        v_ref[rows(to * unit, unit), :] = came_ref[rows(at * unit, unit), :]

    each_unit(sorted_ref.shape[1] // unit, place, kept_ref, got_ref, kept, came)
    vt[...] = v_ref[...].astype(F32).T.astype(BF16)
    for j in range(CS // QB):
        end = (j + 1) * QB
        ot_ref[:, j * QB : end] = dot(vt[:, :end], p_ref[:end, j * QB : end])


def value_grads_kernel(unit, place, kept_ref, got_ref, _after, sorted_ref, came_ref, p_ref, g_ref, own_ref, back_ref, res):
    tok = sorted_ref.shape[1]

    def own(d, u, to):
        g_ref[rows(to * unit, unit), :] = sorted_ref[d, rows(u * unit, unit), :]

    def got(at, to):
        g_ref[rows(to * unit, unit), :] = came_ref[rows(at * unit, unit), :]

    each_unit(tok // unit, place, kept_ref, got_ref, own, got)
    for lo in range(0, CS, QB):
        res[lo : lo + QB, :] = dot(p_ref[lo : lo + QB, lo:], g_ref[lo:, :]).astype(BF16)

    def own_out(d, u, to):
        own_ref[d, 0, rows(u * unit, unit), :] = res[rows(to * unit, unit), :]

    def got_out(at, to):
        back_ref[0, rows(at * unit, unit), :] = res[rows(to * unit, unit), :]

    each_unit(tok // unit, place, kept_ref, got_ref, own_out, got_out)


def grads_kernel(
    unit, place, kept_ref, got_ref, _after, q_ref, k_ref, v_ref, kt_ref, ot_ref, p_ref, g_ref, own_ref, back_ref, dqt, res
):
    tok = own_ref.shape[2]
    delta = jnp.sum(g_ref[...].astype(F32).T * ot_ref[...], axis=0, keepdims=True)
    factor = HD**-0.5
    for lo in range(0, CS, QB):
        hi = lo + QB
        dp = dot_nt(v_ref[lo:hi, :], g_ref[lo:, :])
        ds = (p_ref[lo:hi, lo:].astype(F32) * (dp - delta[:, lo:])).astype(BF16)
        res[1, lo:hi, :] = (dot(ds, q_ref[lo:, :]) * factor).astype(BF16)
        part = dot(kt_ref[:, lo:hi], ds)
        dqt[:, lo:] = part if lo == 0 else dqt[:, lo:] + part
    res[0] = (dqt[...].T * factor).astype(BF16)

    def own_out(d, u, to):
        for i in range(2):
            own_ref[d, i, rows(u * unit, unit), :] = res[i, rows(to * unit, unit), :]

    def got_out(at, to):
        for i in range(2):
            back_ref[i, rows(at * unit, unit), :] = res[i, rows(to * unit, unit), :]

    each_unit(tok // unit, place, kept_ref, got_ref, own_out, got_out)


def unsort_kernel(unit, distances, kept_ref, _after, _after_edge, slot_col, own_ref, back_ref, *refs):
    *outs, full = refs
    tok = own_ref.shape[2]
    count = own_ref.shape[1]
    col_index = lax.broadcasted_iota(jnp.int32, (tok, tok), 1).astype(F32)
    offset = jnp.int32(0)
    for d in range(HR):
        kept = kept_ref[d]
        if d in distances:
            n = distances.index(d)

            def own(u, carry, d=d, n=n):
                for i in range(count):
                    full[n, i, rows(u * unit, unit), :] = own_ref[d, i, rows(u * unit, unit), :]
                return carry

            def got(u, carry, n=n, offset=offset, kept=kept):
                for i in range(count):
                    full[n, i, rows(u * unit, unit), :] = back_ref[i, rows((offset + u - kept) * unit, unit), :]
                return carry

            lax.fori_loop(0, kept, own, 0)
            lax.fori_loop(kept, tok // unit, got, 0)
            move = (col_index == slot_col[:, d : d + 1]).astype(BF16)
            for i in range(count):
                outs[n][i] = dot(move, full[n, i]).astype(BF16)
        offset = offset + tok // unit - kept


def window_kernel(
    place, _after, _after_edge, own, got, g_own, g_got, edge, dq_ref, early_ref, late_ref, stats_ref, *scratch
):
    tok = own.shape[1]
    pair = 2 * tok
    factor = HD**-0.5
    r = lax.broadcasted_iota(jnp.int32, (QB, QB), 0)
    c = lax.broadcasted_iota(jnp.int32, (QB, QB), 1)
    span = WIN + QB
    started = place[0] > 0
    own_at, got_at = place[1] * tok, (1 - place[1]) * tok
    for h in range(HL // 2):
        part = slice(h * HD, (h + 1) * HD)
        queries, grads, keys, values, kt, dk, dv = (ref.at[h] for ref in scratch)
        for at, block, g_block in ((own_at, own, g_own[:, part]), (got_at, got, g_got[:, part])):
            queries[rows(at, tok), :] = block[0, :, part]
            grads[rows(at, tok), :] = g_block
            keys[rows(at + WIN, tok), :] = block[1, :, part]
            values[rows(at + WIN, tok), :] = block[2, :, part]
        keys[:WIN, :] = edge[0, :, part]
        values[:WIN, :] = edge[1, :, part]
        kt[...] = keys[...].astype(F32).T.astype(BF16)
        for j in range(pair // QB):
            lo, hi = j * QB, j * QB + span
            q = queries[j * QB : (j + 1) * QB, :]
            g = grads[j * QB : (j + 1) * QB, :]
            s = dot_nt(keys[lo:hi, :], q) * factor
            first = jnp.where(r > c, s[:QB], -1e30)
            last = jnp.where(r <= c, s[span - QB :], -1e30)
            s = jnp.concatenate([first, s[QB : span - QB], last], axis=0)
            if lo < WIN:
                s = jnp.concatenate([jnp.where(started, s[: WIN - lo], -1e30), s[WIN - lo :]], axis=0)
            top = jnp.max(s, axis=0, keepdims=True)
            w = jnp.exp(s - top)
            scale = 1.0 / jnp.sum(w, axis=0, keepdims=True)
            p = w * scale
            dp = dot_nt(values[lo:hi, :], g)
            delta = jnp.sum(p * dp, axis=0, keepdims=True)
            pb = p.astype(BF16)
            ds = (p * (dp - delta)).astype(BF16)
            side, at = divmod(j * QB, tok)
            dq_ref[side, at : at + QB, part] = (dot(kt[:, lo:hi], ds).T * factor).astype(BF16)
            if side == 0:
                for n, line in enumerate((top, scale, delta)):
                    stats_ref[3 * h + n : 3 * h + n + 1, at : at + QB] = line
            skip = max(0, WIN - lo)
            low = max(lo, WIN) - WIN
            part_k = dot(ds[skip:], q) * factor
            part_v = dot(pb[skip:], g)
            end = hi - WIN
            if end - QB > low:
                dk[low : end - QB, :] = dk[low : end - QB, :] + part_k[:-QB]
                dv[low : end - QB, :] = dv[low : end - QB, :] + part_v[:-QB]
            dk[end - QB : end, :] = part_k[-QB:]
            dv[end - QB : end, :] = part_v[-QB:]
        for i, total in enumerate((dk, dv)):
            early_ref[i, :, part] = total[:tok, :].astype(BF16)
            late_ref[i, :, part] = total[tok:, :]
    stats_ref[6:, :] = jnp.zeros((2, tok), F32)


def settle_kernel(place, _after, dq_ref, early_ref, late_ref, edge, ahead, stats, own, send, late):
    tok = edge.shape[1]
    factor = HD**-0.5
    r = lax.broadcasted_iota(jnp.int32, (QB, QB), 0)
    c = lax.broadcasted_iota(jnp.int32, (QB, QB), 1)
    for h in range(HL // 2):
        part = slice(h * HD, (h + 1) * HD)
        for j in range(tok // QB):
            at = slice(j * QB, (j + 1) * QB)
            q, g = ahead[0, at, part], ahead[1, at, part]
            top, scale, delta = (stats[3 * h + n : 3 * h + n + 1, at] for n in range(3))
            s = dot_nt(edge[0, j * QB :, part], q) * factor
            p = jnp.exp(s - top) * scale
            first = jnp.where(r > c, p[:QB], 0.0)
            p = first if j == tok // QB - 1 else jnp.concatenate([first, p[QB:]], axis=0)
            ds = p * (dot_nt(edge[1, j * QB :, part], g) - delta)
            add_k = dot(ds.astype(BF16), q) * factor
            add_v = dot(p.astype(BF16), g)
            for i, add in enumerate((add_k, add_v)):
                base = late_ref[i, :, part] if j == 0 else late[h, i, j * QB :, :]
                late[h, i, j * QB :, :] = base + add
    for side, (near, far) in enumerate(((own, send), (send, own))):

        @pl.when(place[1] == side)
        def _(near=near, far=far):
            near[0] = dq_ref[0]
            near[1:] = early_ref[...]
            far[0] = dq_ref[1]
            for h in range(HL // 2):
                for i in range(2):
                    far[1 + i, :, h * HD : (h + 1) * HD] = late[h, i].astype(BF16)


def join_value_kernel(place, _after, v0, v1, v2, v3, out):
    for d, v in enumerate((v0, v1, v2, v3)):
        out[:, head_columns(place, d)] = v[0]


def join_kernel(place, value_ref, own, got, dq_ref, dk_ref, dv_ref):
    outs = (dq_ref, dk_ref, dv_ref)
    dv_ref[:, : HR * HD] = value_ref[...]
    width = HL * HD // 2
    for n in range(2):
        side = place[1] if n == 0 else 1 - place[1]
        at = pl.ds(pl.multiple_of(HR * HD + side * width, width), width)
        for i in range(3):
            outs[i][:, at] = own[i] if n == 0 else got[i]


def finish_kernel(place, y0, y1, y2, y3, _dq, _dk, dq_hbm, dk_hbm, sems):
    copies = []
    for d, y in enumerate((y0, y1, y2, y3)):
        for i, out in enumerate((dq_hbm, dk_hbm)):
            copies.append(pltpu.make_async_copy(y.at[i], out.at[:, head_columns(place, d)], sems.at[d, i]))
    start_all(copies)
    wait_all(copies)


def struct(*shape, dtype=BF16):
    return jax.ShapeDtypeStruct(shape, dtype)


def pair_body(query, key, value, grad_sent, out_weight, assign):
    tok = query.shape[1]
    devices = lax.axis_size("seq")
    place = lax.axis_index("seq")
    first, side = place // 2, place % 2
    where = jnp.stack([first, side]).astype(jnp.int32)
    unit = CS // (4 * devices)
    half = CS // 2

    def among_groups(block, shift):
        route = [(i, ((i // 2 + shift) % HR) * 2 + i % 2) for i in range(devices)]
        return lax.ppermute(block, "seq", route)

    def swap(block):
        return lax.ppermute(block, "seq", [(i, i ^ 1) for i in range(devices)])

    hbm = [pl.BlockSpec(memory_space=pltpu.HBM)]
    width = HL * HD // 2
    boundary = from_behind(grad_sent, "section", -1)[0]
    *sent, local_own, local_send = pl.pallas_call(
        split_kernel,
        out_shape=[struct(2 * tok + 16, HD)] * HR + [struct(3, tok, width)] * 2,
        in_specs=smem() + vmem() + hbm * 3,
        out_specs=vmem(6),
        scratch_shapes=[pltpu.VMEM((3, tok, query.shape[2]), BF16), pltpu.SemaphoreType.DMA((3, 4))],
        compiler_params=params(SPLIT_MIB),
        cost_estimate=takes(2),
        name="split",
    )(where, assign[0], query[0], key[0], value[0])
    arrived = [sent[0]] + [among_groups(sent[d], d) for d in range(1, HR)]
    local_got = swap(local_send)
    *g_sent, g_own, g_send = pl.pallas_call(
        project_kernel,
        grid=(4,),
        out_shape=[struct(tok, HD)] * HR + [struct(tok, width)] * 2,
        in_specs=smem()
        + [
            pl.BlockSpec((1, 16, HD), lambda n: (0, 0, 0)),
            pl.BlockSpec(boundary.shape, lambda n: (0, 0)),
            pl.BlockSpec((2 * HD, boundary.shape[1]), lambda n: (n, 0)),
        ],
        out_specs=[pl.BlockSpec((tok, HD), lambda n: (0, 0))] * HR
        + [pl.BlockSpec((tok, width), lambda n: (0, 0))] * 2,
        compiler_params=params(20),
        cost_estimate=takes(3.8),
        name="project",
    )(where, local_got, boundary, out_weight[0])
    g_arrived = [g_sent[0]] + [among_groups(g_sent[d], d) for d in range(1, HR)]

    g_got = swap(g_send)
    v_sent = pl.pallas_call(
        split_value_kernel,
        out_shape=[struct(tok, HD)] * HR,
        in_specs=smem() + vmem(5),
        out_specs=vmem(4),
        compiler_params=params(20),
        cost_estimate=takes(1),
        name="split_value",
    )(where, g_sent[0], *arrived[1:], value[0])
    v_arrived = [v_sent[0]] + [among_groups(v_sent[d], d) for d in range(1, HR)]

    ordered, send, slot_row, slot_col, kept = pl.pallas_call(
        functools.partial(pack_kernel, unit),
        out_shape=[
            struct(HR, 2, tok, HD),
            struct(2 * half + 16, HD),
            struct(8, tok, dtype=F32),
            struct(tok, HD, dtype=F32),
            struct(HR, dtype=jnp.int32),
        ],
        in_specs=smem() + vmem(5),
        out_specs=vmem(4) + smem(),
        compiler_params=params(20),
        cost_estimate=takes(0.1),
        name="pack",
    )(where, v_sent[0], *arrived)
    came = swap(send)

    v_ordered, v_out = pl.pallas_call(
        functools.partial(pack_value_kernel, unit),
        out_shape=[struct(HR, tok, HD), struct(half, HD)],
        in_specs=smem() + vmem(7),
        out_specs=vmem(2),
        compiler_params=params(20),
        cost_estimate=takes(12),
        name="pack_value",
    )(kept, send, g_got, slot_row, *v_arrived)
    v_came = swap(v_out)

    got, q, k, kt, p = pl.pallas_call(
        functools.partial(probs_kernel, unit),
        out_shape=[struct(HR, dtype=jnp.int32)] + [struct(CS, HD)] * 2 + [struct(HD, CS), struct(CS, CS)],
        in_specs=smem(2) + vmem(3),
        out_specs=smem() + vmem(4),
        scratch_shapes=[pltpu.VMEM((CS, QB), F32)],
        compiler_params=params(24),
        cost_estimate=takes(5),
        name="probs",
    )(where, kept, v_out, ordered, came)

    g_ordered, g_out, edge = pl.pallas_call(
        functools.partial(pack_grad_kernel, unit),
        out_shape=[struct(HR, tok, HD), struct(half, HD), struct(2, tok, width)],
        in_specs=smem(2) + vmem(8),
        out_specs=vmem(3),
        compiler_params=params(20),
        cost_estimate=takes(1.6),
        name="pack_grad",
    )(where, kept, kt, slot_row, *g_arrived, local_own, local_got)
    g_came = swap(g_out)
    ahead = [(i, i + 2) for i in range(devices - 2)]
    behind = [(i + 2, i) for i in range(devices - 2)]
    edge_got = lax.ppermute(edge, "seq", ahead)

    v, ot, query_edge = pl.pallas_call(
        functools.partial(mix_kernel, unit),
        out_shape=[struct(CS, HD), struct(HD, CS, dtype=F32), struct(2, tok, width)],
        in_specs=smem(3) + vmem(8),
        out_specs=vmem(3),
        scratch_shapes=[pltpu.VMEM((HD, CS), BF16)],
        compiler_params=params(20),
        cost_estimate=takes(1.7),
        name="mix",
    )(where, kept, got, edge, v_ordered, v_came, p, local_own, local_got, g_own, g_got)
    query_edge_got = lax.ppermute(query_edge, "seq", behind)

    g, own_v, back_v = pl.pallas_call(
        functools.partial(value_grads_kernel, unit),
        out_shape=[struct(CS, HD), struct(HR, 1, tok, HD), struct(1, half, HD)],
        in_specs=smem(3) + vmem(4),
        out_specs=vmem(3),
        scratch_shapes=[pltpu.VMEM((CS, HD), BF16)],
        compiler_params=params(16),
        cost_estimate=takes(2.4),
        name="value_grads",
    )(where, kept, got, ot, g_ordered, g_came, p)
    own, back = pl.pallas_call(
        functools.partial(grads_kernel, unit),
        out_shape=[struct(HR, 2, tok, HD), struct(2, half, HD)],
        in_specs=smem(3) + vmem(8),
        out_specs=vmem(2),
        scratch_shapes=[pltpu.VMEM((HD, CS), F32), pltpu.VMEM((2, CS, HD), BF16)],
        compiler_params=params(24),
        cost_estimate=takes(5),
        name="grads",
    )(where, kept, got, back_v, q, k, v, kt, ot, p, g)

    def unsort(distances, after, after_edge, own, returned, name):
        count = own.shape[1]
        return pl.pallas_call(
            functools.partial(unsort_kernel, unit, distances),
            out_shape=[struct(count, tok, HD)] * len(distances),
            in_specs=smem() + vmem(5),
            out_specs=vmem(len(distances)),
            scratch_shapes=[pltpu.VMEM((len(distances), count, tok, HD), BF16)],
            compiler_params=params(20),
            cost_estimate=takes({'unsort_value':2.6,'unsort_first':0.1,'unsort_last':1.4}[name]),
            name=name,
        )(kept, after, after_edge, slot_col, own, returned)

    returned_v, returned = swap(back_v), swap(back)
    pair = 2 * tok
    natural_v = unsort((0, 1, 2, 3), back, back, own_v, returned_v, "unsort_value")
    home_v = [natural_v[0]] + [among_groups(natural_v[d], -d) for d in range(1, HR)]
    dq_local, early, late, stats = pl.pallas_call(
        window_kernel,
        out_shape=[
            struct(2, tok, width),
            struct(2, tok, width),
            struct(2, tok, width, dtype=F32),
            struct(8, tok, dtype=F32),
        ],
        in_specs=smem() + vmem(7),
        out_specs=vmem(4),
        scratch_shapes=[
            pltpu.VMEM((HL // 2, pair, HD), BF16),
            pltpu.VMEM((HL // 2, pair, HD), BF16),
            pltpu.VMEM((HL // 2, pair + WIN, HD), BF16),
            pltpu.VMEM((HL // 2, pair + WIN, HD), BF16),
            pltpu.VMEM((HL // 2, HD, pair + WIN), BF16),
            pltpu.VMEM((HL // 2, pair, HD), F32),
            pltpu.VMEM((HL // 2, pair, HD), F32),
        ],
        compiler_params=params(24),
        cost_estimate=takes(0.1),
        name="window",
    )(where, natural_v[0], query_edge_got, local_own, local_got, g_own, g_got, edge_got)
    stats_got = lax.ppermute(stats, "seq", behind)
    first_natural = unsort((0, 1, 3), stats, stats, own, returned, "unsort_first")
    settled_own, settled_send = pl.pallas_call(
        settle_kernel,
        out_shape=[struct(3, tok, width)] * 2,
        in_specs=smem() + vmem(7),
        out_specs=vmem(2),
        scratch_shapes=[pltpu.VMEM((HL // 2, 2, tok, HD), F32)],
        compiler_params=params(20),
        cost_estimate=takes(0.1),
        name="settle",
    )(where, first_natural[0], dq_local, early, late, edge, query_edge_got, stats_got)
    settled_got = swap(settled_send)
    value_left = pl.pallas_call(
        join_value_kernel,
        out_shape=struct(tok, HR * HD),
        in_specs=smem() + vmem(5),
        out_specs=vmem()[0],
        compiler_params=params(16),
        cost_estimate=takes(12),
        name="join_value",
    )(where, settled_send, *home_v)
    last_natural = unsort((2,), value_left, value_left, own, returned, "unsort_last")
    natural = [*first_natural]
    natural.insert(2, *last_natural)
    home = [natural[0]] + [among_groups(natural[d], -d) for d in range(1, HR)]

    dq_part, dk_part, dv = pl.pallas_call(
        join_kernel,
        out_shape=[struct(tok, (HR + HL) * HD)] * 3,
        in_specs=smem() + vmem(3),
        out_specs=vmem(3),
        compiler_params=params(20),
        cost_estimate=takes(2),
        name="join",
    )(where, value_left, settled_own, settled_got)
    dq, dk = pl.pallas_call(
        finish_kernel,
        out_shape=[struct(tok, (HR + HL) * HD)] * 2,
        in_specs=smem() + vmem(4) + hbm * 2,
        out_specs=hbm * 2,
        input_output_aliases={5: 0, 6: 1},
        scratch_shapes=[pltpu.SemaphoreType.DMA((HR, 2))],
        compiler_params=params(16),
        cost_estimate=takes(1.5),
        name="finish",
    )(where, *home, dq_part, dk_part)
    outs = (dq, dk, dv)
    return tuple(out[None] for out in outs)


def from_behind(block, axis, distance):
    devices = range(lax.axis_size(axis))
    route = [((i - distance) % len(devices), i) for i in devices]
    return lax.ppermute(block, axis, route)


def shifted(block, axis, distance):
    devices = range(lax.axis_size(axis))
    route = [(i - distance, i) for i in devices if i - distance in devices]
    return lax.ppermute(block, axis, route)


def cluster_block(query_rows, key_rows, value_rows, grad_rows, allowed, factor):
    scores = jnp.dot(query_rows, key_rows.T, preferred_element_type=jnp.float32) * factor
    scores = jnp.where(allowed, scores, -1e30)
    highest = jnp.max(scores, axis=1, keepdims=True)
    weights = jnp.exp(scores - highest)
    probs = weights / jnp.sum(weights, axis=1, keepdims=True)
    dprob = jnp.dot(grad_rows, value_rows.T, preferred_element_type=jnp.float32)
    delta = jnp.sum(probs * dprob, axis=1, keepdims=True)
    dscore = probs * (dprob - delta)
    probs_b = probs.astype(jnp.bfloat16)
    dscore_b = dscore.astype(jnp.bfloat16)
    grad_query = jnp.dot(dscore_b, key_rows, preferred_element_type=jnp.float32) * factor
    grad_key = jnp.dot(dscore_b.T, query_rows, preferred_element_type=jnp.float32) * factor
    grad_value = jnp.dot(probs_b.T, grad_rows, preferred_element_type=jnp.float32)
    return (grad_query, grad_key, grad_value)


def cluster_grads(query_rows, key_rows, value_rows, grad_rows, factor):
    length = query_rows.shape[0]
    span = min(512, length)
    pieces = []
    total_key = jnp.zeros(key_rows.shape, jnp.float32)
    total_value = jnp.zeros(value_rows.shape, jnp.float32)
    for index in range(length // span):
        first = index * span
        end = first + span
        allowed = (
            jnp.arange(end, dtype=jnp.int32)[None, :]
            <= (first + jnp.arange(span, dtype=jnp.int32))[:, None]
        )
        part_query, part_key, part_value = cluster_block(
            query_rows[first:end],
            key_rows[:end],
            value_rows[:end],
            grad_rows[first:end],
            allowed,
            factor,
        )
        pieces.append(part_query)
        total_key = total_key.at[:end].add(part_key)
        total_value = total_value.at[:end].add(part_value)
    return (jnp.concatenate(pieces, axis=0), total_key, total_value)


def window_block(query_rows, key_rows, value_rows, grad_rows, allowed, factor):
    scores = (
        jnp.einsum("qhd,khd->hqk", query_rows, key_rows, preferred_element_type=jnp.float32)
        * factor
    )
    scores = jnp.where(allowed[None], scores, -1e30)
    highest = jnp.max(scores, axis=2, keepdims=True)
    weights = jnp.exp(scores - highest)
    probs = weights / jnp.sum(weights, axis=2, keepdims=True)
    dprob = jnp.einsum("qhd,khd->hqk", grad_rows, value_rows, preferred_element_type=jnp.float32)
    delta = jnp.sum(probs * dprob, axis=2, keepdims=True)
    dscore = probs * (dprob - delta)
    probs_b = probs.astype(jnp.bfloat16)
    dscore_b = dscore.astype(jnp.bfloat16)
    grad_query = (
        jnp.einsum("hqk,khd->qhd", dscore_b, key_rows, preferred_element_type=jnp.float32) * factor
    )
    grad_key = (
        jnp.einsum("hqk,qhd->khd", dscore_b, query_rows, preferred_element_type=jnp.float32)
        * factor
    )
    grad_value = jnp.einsum("hqk,qhd->khd", probs_b, grad_rows, preferred_element_type=jnp.float32)
    return (grad_query, grad_key, grad_value)


def window_mask(query_pos, key_pos):
    return (
        (key_pos[None, :] > query_pos[:, None] - WIN)
        & (key_pos[None, :] <= query_pos[:, None])
        & (key_pos[None, :] >= 0)
    )


def general_body(query, key, value, grad_sent, out_weight, assign):
    tok_rows = query.shape[1]
    heads = HR + HL
    devices = lax.axis_size("seq")
    place = lax.axis_index("seq")
    factor = HD ** (-0.5)
    boundary = from_behind(grad_sent, "section", -1)[0]
    attn_grad = lax.dot_general(
        boundary, out_weight[0], (((1,), (1,)), ((), ())), preferred_element_type=jnp.float32
    ).astype(jnp.bfloat16)
    query_heads = query[0].reshape(tok_rows, heads, HD)
    key_heads = key[0].reshape(tok_rows, heads, HD)
    value_heads = value[0].reshape(tok_rows, heads, HD)
    grad_heads = attn_grad.reshape(tok_rows, heads, HD)
    clusters = tok_rows * devices // CS
    owned = HR * tok_rows // CS
    capacity = 7 * CS // (4 * devices)
    unit_rows = capacity // 7
    width = owned * capacity
    head_slots = clusters * capacity
    labels = assign[0]
    members = (labels[:, :, None] == jnp.arange(clusters, dtype=jnp.int32)[None, None, :]).astype(
        jnp.bfloat16
    )
    token_ids = jnp.arange(tok_rows, dtype=jnp.int32)
    lower = (token_ids[:, None] >= token_ids[None, :]).astype(jnp.bfloat16)
    running_counts = jnp.einsum("ts,hsc->htc", lower, members, preferred_element_type=jnp.float32)
    ranks = (jnp.sum(running_counts * members.astype(jnp.float32), axis=2) - 1.0).astype(jnp.int32)
    local_slot = labels * capacity + ranks
    slot_hit = jnp.arange(head_slots, dtype=jnp.int32)[None, :, None] == local_slot[:, None, :]
    slot_table = slot_hit.astype(jnp.bfloat16)
    routed_in = jnp.concatenate(
        [query_heads[:, :HR], key_heads[:, :HR], value_heads[:, :HR], grad_heads[:, :HR]], axis=2
    )
    packed = jnp.einsum(
        "hst,thd->hsd", slot_table, routed_in, preferred_element_type=jnp.float32
    ).astype(jnp.bfloat16)
    packed = packed.reshape(devices, width, 4 * HD)
    token_pos = place * tok_rows + token_ids
    slot_pos = jnp.max(jnp.where(slot_hit, token_pos[None, None, :], -1), axis=2).reshape(
        devices, width
    )
    send_query = packed[:, :, :HD]
    send_key = packed[:, :, HD : 2 * HD]
    send_value = packed[:, :, 2 * HD : 3 * HD]
    send_grad = packed[:, :, 3 * HD :]
    arrived_query, arrived_key, arrived_value, arrived_grad, arrived_pos = (
        lax.all_to_all(send_query, "seq", split_axis=0, concat_axis=0, tiled=True),
        lax.all_to_all(send_key, "seq", split_axis=0, concat_axis=0, tiled=True),
        lax.all_to_all(send_value, "seq", split_axis=0, concat_axis=0, tiled=True),
        lax.all_to_all(send_grad, "seq", split_axis=0, concat_axis=0, tiled=True),
        lax.all_to_all(slot_pos, "seq", split_axis=0, concat_axis=0, tiled=True),
    )
    arrived_all = jnp.concatenate([arrived_query, arrived_key, arrived_value, arrived_grad], axis=2)
    unit_index = jnp.arange(7, dtype=jnp.int32)
    target_units = jnp.arange(CS // unit_rows, dtype=jnp.int32)
    block = arrived_all.reshape(devices * 7, unit_rows * 4 * HD)
    live_counts = jnp.sum((arrived_pos >= 0).astype(jnp.int32), axis=1)
    units = live_counts // unit_rows
    starts = jnp.cumsum(units) - units
    picker = (target_units[:, None, None] == starts[None, :, None] + unit_index[None, None, :]) & (
        unit_index[None, None, :] < units[None, :, None]
    )
    picker = picker.reshape(CS // unit_rows, devices * 7).astype(jnp.bfloat16)
    compact = (
        jnp.dot(picker, block, preferred_element_type=jnp.float32)
        .astype(jnp.bfloat16)
        .reshape(CS, 4 * HD)
    )
    results = cluster_grads(
        compact[:, :HD],
        compact[:, HD : 2 * HD],
        compact[:, 2 * HD : 3 * HD],
        compact[:, 3 * HD :],
        factor,
    )
    answer = jnp.concatenate([result.astype(jnp.bfloat16) for result in results], axis=1).reshape(
        CS // unit_rows, unit_rows * 3 * HD
    )
    spread = jnp.dot(picker.T, answer, preferred_element_type=jnp.float32).astype(jnp.bfloat16)
    outgoing = spread.reshape(devices, capacity, 3 * HD)
    back_query, back_key, back_value = (
        lax.all_to_all(outgoing[:, :, :HD], "seq", split_axis=0, concat_axis=0, tiled=True),
        lax.all_to_all(outgoing[:, :, HD : 2 * HD], "seq", split_axis=0, concat_axis=0, tiled=True),
        lax.all_to_all(outgoing[:, :, 2 * HD :], "seq", split_axis=0, concat_axis=0, tiled=True),
    )
    back_all = jnp.concatenate([back_query, back_key, back_value], axis=2).reshape(
        HR, head_slots, 3 * HD
    )
    routed_out = jnp.einsum(
        "hst,hsd->thd", slot_table, back_all, preferred_element_type=jnp.float32
    ).astype(jnp.bfloat16)
    routed_query = routed_out[:, :, :HD]
    routed_key = routed_out[:, :, HD : 2 * HD]
    routed_value = routed_out[:, :, 2 * HD :]
    local_query = query_heads[:, HR:]
    local_key = key_heads[:, HR:]
    local_value = value_heads[:, HR:]
    local_grad = grad_heads[:, HR:]
    prior_key, prior_value = shifted((local_key, local_value), "seq", 1)
    keys_all = jnp.concatenate([prior_key, local_key], axis=0)
    values_all = jnp.concatenate([prior_value, local_value], axis=0)
    key_positions = (place - 1) * tok_rows + jnp.arange(2 * tok_rows, dtype=jnp.int32)
    query_positions = place * tok_rows + jnp.arange(tok_rows, dtype=jnp.int32)
    span = min(512, tok_rows)
    total_key = jnp.zeros((2 * tok_rows, HL, HD), jnp.float32)
    total_value = jnp.zeros((2 * tok_rows, HL, HD), jnp.float32)
    start = tok_rows - WIN
    allowed = window_mask(query_positions, key_positions)
    part_query, part_key, part_value = window_block(
        local_query, keys_all, values_all, local_grad, allowed, factor
    )
    total_key = total_key.at[start : start + span + WIN].add(part_key)
    total_value = total_value.at[start : start + span + WIN].add(part_value)
    tail = tok_rows - WIN
    carried_key, carried_value = (
        shifted(total_key[tail:tok_rows].astype(jnp.bfloat16), "seq", -1).astype(jnp.float32),
        shifted(total_value[tail:tok_rows].astype(jnp.bfloat16), "seq", -1).astype(jnp.float32),
    )
    local_dk = total_key[tok_rows:].at[tail:].add(carried_key)
    local_dv = total_value[tok_rows:].at[tail:].add(carried_value)
    local_dq = part_query.astype(jnp.bfloat16)
    grad_query = jnp.concatenate([routed_query, local_dq], axis=1).reshape(1, tok_rows, heads * HD)
    grad_key = jnp.concatenate([routed_key, local_dk.astype(jnp.bfloat16)], axis=1).reshape(
        1, tok_rows, heads * HD
    )
    grad_value = jnp.concatenate([routed_value, local_dv.astype(jnp.bfloat16)], axis=1).reshape(
        1, tok_rows, heads * HD
    )
    return (grad_query, grad_key, grad_value)


def body(query, key, value, grad_sent, out_weight, assign):
    clusters = query.shape[1] * lax.axis_size("seq") // CS
    plan = pair_body if clusters == 2 else general_body
    return plan(query, key, value, grad_sent, out_weight, assign)


def solution(mesh):
    placed = (
        P("section", "seq", None),
        P("section", "seq", None),
        P("section", "seq", None),
        P("section", "seq", None),
        P("section", None, None),
        P("section", None, "seq"),
    )
    return jax.shard_map(
        body,
        mesh=mesh,
        in_specs=placed,
        out_specs=(P("section", "seq", None), P("section", "seq", None), P("section", "seq", None)),
        check_vma=False,
    )
```

```python
import functools

import jax
import jax.numpy as jnp
from jax import lax
from jax.experimental import pallas as pl
from jax.experimental.pallas import tpu as pltpu
from jax.sharding import PartitionSpec as P

HR = 4
HL = 4
HD = 128
CS = 2048
WIN = 512
QB = 256
MIB = 1024 * 1024
SPLIT_MIB = 56
NT = (((1,), (1,)), ((), ()))
F32 = jnp.float32
BF16 = jnp.bfloat16


def vmem(count=1):
    return [pl.BlockSpec(memory_space=pltpu.VMEM)] * count


def smem(count=1):
    return [pl.BlockSpec(memory_space=pltpu.SMEM)] * count


def params(mib):
    return pltpu.CompilerParams(vmem_limit_bytes=mib * MIB)


def dot(a, b):
    return jnp.dot(a, b, preferred_element_type=F32)


def dot_nt(a, b):
    return lax.dot_general(a, b, NT, preferred_element_type=F32)


def takes(microseconds):
    return pl.CostEstimate(
        flops=int(microseconds * 1.1e9), bytes_accessed=int(microseconds * 3.5e6), transcendentals=0
    )


def rows(start, size):
    return pl.ds(pl.multiple_of(start, size), size)


def start_all(copies):
    for copy in copies:
        copy.start()


def wait_all(copies):
    for copy in copies:
        copy.wait()


def head_columns(place, d):
    return pl.ds(pl.multiple_of(lax.rem(place[0] + d, HR) * HD, HD), HD)


def split_kernel(place, labels, q_hbm, k_hbm, v_hbm, x0, x1, x2, x3, own, send, held, sems):
    tok = q_hbm.shape[0]
    cuts = sems.shape[1]
    size = tok // cuts
    copies = []
    for i, source in enumerate((q_hbm, k_hbm, v_hbm)):
        for n in range(cuts):
            at = slice(n * size, (n + 1) * size)
            copies.append(pltpu.make_async_copy(source.at[at], held.at[i, at], sems.at[i, n]))
    start_all(copies)
    for d, x in enumerate((x0, x1, x2, x3)):
        line = labels[pl.ds(lax.rem(place[0] + d, HR), 1), :].astype(F32)
        parts = [line[:, r * HD : (r + 1) * HD] for r in range(tok // HD)]
        parts.append(jnp.zeros((16 - tok // HD, HD), F32))
        x[2 * tok :, :] = jnp.concatenate(parts, axis=0).astype(BF16)
    width = HL * HD // 2
    for i in range(3):
        wait_all(copies[i * cuts : (i + 1) * cuts])
        for d, x in enumerate((x0, x1, x2, x3)):
            if i < 2:
                x[i * tok : (i + 1) * tok, :] = held[i, :, head_columns(place, d)]
        for out, side in ((send, 1 - place[1]), (own, place[1])):
            out[i] = held[i, :, pl.ds(pl.multiple_of(HR * HD + side * width, width), width)]


def split_value_kernel(place, _after, _after1, _after2, _after3, v_ref, x0, x1, x2, x3):
    for d, x in enumerate((x0, x1, x2, x3)):
        x[...] = v_ref[:, head_columns(place, d)]


def project_kernel(place, _after_local, rows_ref, weight, g0, g1, g2, g3, own_ref, send_ref):
    step = pl.program_id(0)
    part = dot_nt(rows_ref[...], weight[...]).astype(BF16)

    @pl.when(step < HR // 2)
    def _():
        for i in range(2):
            d = lax.rem(2 * step + i - place[0] + 4, 4)
            for e, g in enumerate((g0, g1, g2, g3)):

                @pl.when(d == e)
                def _(g=g, i=i):
                    g[...] = part[:, i * HD : (i + 1) * HD]

    @pl.when(step >= HR // 2)
    def _():
        @pl.when(step - HR // 2 == place[1])
        def _():
            own_ref[...] = part

        @pl.when(step - HR // 2 != place[1])
        def _():
            send_ref[...] = part


def pack_kernel(unit, place, _after, x0, x1, x2, x3, sorted_ref, send_ref, slot_row, slot_col, kept_ref):
    tok = x0.shape[0] - 16
    tok = tok // 2
    side = place[1]
    lane = lax.broadcasted_iota(jnp.int32, (1, tok), 1).astype(F32)
    labels = []
    for x in (x0, x1, x2, x3):
        block = x[2 * tok :, :].astype(F32)
        labels.append(jnp.concatenate([block[r : r + 1, :] for r in range(tok // 128)], axis=1))
    label = jnp.concatenate(labels + [jnp.zeros((4, tok), F32)], axis=0)
    upper = (
        lax.broadcasted_iota(jnp.int32, (tok, tok), 0) <= lax.broadcasted_iota(jnp.int32, (tok, tok), 1)
    ).astype(BF16)
    ones = dot(label.astype(BF16), upper)
    totals = [jnp.sum(row).astype(jnp.int32) for row in labels]
    whole = totals[0] + totals[1] + totals[2] + totals[3]
    half = CS // 2
    keep_one = jnp.where(side == 0, (whole > half).astype(jnp.int32), (whole >= half).astype(jnp.int32))
    keep_f = keep_one.astype(F32)
    slots = []
    for d in range(4):
        kept = jnp.where(keep_one == 1, totals[d], tok - totals[d])
        kept_ref[d] = kept // unit
        is_kept = labels[d] * keep_f + (1.0 - labels[d]) * (1.0 - keep_f)
        ones_d = ones[d : d + 1, :]
        count = ones_d * keep_f + (lane + 1.0 - ones_d) * (1.0 - keep_f)
        slot = jnp.where(is_kept > 0.5, count - 1.0, kept.astype(F32) + lane - count)
        slots.append(slot)
    slots_all = jnp.concatenate(slots + [jnp.zeros((124, tok), F32)], axis=0)
    slot_row[...] = slots_all[:8, :]
    slot_col[...] = slots_all.T
    row_index = lax.broadcasted_iota(jnp.int32, (tok, tok), 0).astype(F32)
    for d, x in enumerate((x0, x1, x2, x3)):
        move = (row_index == slots[d]).astype(BF16)
        for i in range(2):
            sorted_ref[d, i] = dot(move, x[i * tok : (i + 1) * tok, :]).astype(BF16)
    offset = jnp.int32(0)
    info_row = lax.broadcasted_iota(jnp.int32, (16, HD), 0)
    info = jnp.zeros((16, HD), F32)
    for d in range(4):
        kept = kept_ref[d]
        info = jnp.where(info_row == d, kept.astype(F32), info)

        def put(u, carry, d=d, offset=offset, kept=kept):
            for i in range(2):
                send_ref[rows(i * half + (offset + u - kept) * unit, unit), :] = sorted_ref[d, i, rows(u * unit, unit), :]
            return carry

        lax.fori_loop(kept, tok // unit, put, 0)
        offset = offset + tok // unit - kept
    send_ref[2 * half :, :] = info.astype(BF16)


def pack_value_kernel(unit, kept_ref, _after, _after_swap, slot_row, x0, x1, x2, x3, sorted_ref, send_ref):
    pack_one(unit, kept_ref, slot_row, (x0, x1, x2, x3), sorted_ref, send_ref)


def pack_grad_kernel(
    unit, place, kept_ref, _after, slot_row, x0, x1, x2, x3, own, got, sorted_ref, send_ref, edge_ref
):
    pack_one(unit, kept_ref, slot_row, (x0, x1, x2, x3), sorted_ref, send_ref)
    for side, block in ((1, own), (0, got)):

        @pl.when(place[1] == side)
        def _(block=block):
            edge_ref[...] = block[1:]


def pack_one(unit, kept_ref, slot_row, blocks, sorted_ref, send_ref):
    tok = sorted_ref.shape[1]
    row_index = lax.broadcasted_iota(jnp.int32, (tok, tok), 0).astype(F32)
    for d, x in enumerate(blocks):
        move = (row_index == slot_row[d : d + 1, :]).astype(BF16)
        sorted_ref[d] = dot(move, x[...]).astype(BF16)
    offset = jnp.int32(0)
    for d in range(4):
        kept = kept_ref[d]

        def put(u, carry, d=d, offset=offset, kept=kept):
            send_ref[rows((offset + u - kept) * unit, unit), :] = sorted_ref[d, rows(u * unit, unit), :]
            return carry

        lax.fori_loop(kept, tok // unit, put, 0)
        offset = offset + tok // unit - kept


def each_unit(units, place, kept_ref, got_ref, own, got):
    first, side = place[0], place[1]
    pos = jnp.int32(0)
    for z in range(4):
        d = lax.rem(first - z + 4, 4)
        kept = kept_ref[d]
        came = units - got_ref[d]
        at = jnp.int32(0)
        for e in range(4):
            at = at + jnp.where(e < d, units - got_ref[e], 0)
        own_pos = pos + jnp.where(side == 0, 0, came)
        got_pos = pos + jnp.where(side == 0, kept, 0)

        def own_step(u, carry, d=d, own_pos=own_pos):
            own(d, u, own_pos + u)
            return carry

        def got_step(u, carry, at=at, got_pos=got_pos):
            got(at + u, got_pos + u)
            return carry

        lax.fori_loop(0, kept, own_step, 0)
        lax.fori_loop(0, came, got_step, 0)
        pos = pos + kept + came


def probs_kernel(unit, place, kept_ref, _after, sorted_ref, came_ref, got_ref, q_ref, k_ref, kt_ref, p_ref, s_ref):
    tok = sorted_ref.shape[2]
    half = CS // 2
    info = came_ref[2 * half :, :].astype(F32)
    for d in range(4):
        got_ref[d] = jnp.max(info[d : d + 1, :]).astype(jnp.int32)
    outs = (q_ref, k_ref)

    def own(d, u, to):
        for i in range(2):
            outs[i][rows(to * unit, unit), :] = sorted_ref[d, i, rows(u * unit, unit), :]

    def got(at, to):
        for i in range(2):
            outs[i][rows(to * unit, unit), :] = came_ref[rows(i * half + at * unit, unit), :]

    each_unit(tok // unit, place, kept_ref, got_ref, own, got)
    kt_ref[...] = k_ref[...].astype(F32).T.astype(BF16)
    factor = HD**-0.5
    low = lax.broadcasted_iota(jnp.int32, (QB, QB), 0) <= lax.broadcasted_iota(jnp.int32, (QB, QB), 1)
    for j in range(CS // QB):
        q = q_ref[j * QB : (j + 1) * QB, :]
        top = None
        for i in range(j + 1):
            s = dot_nt(k_ref[i * QB : (i + 1) * QB, :], q) * factor
            if i == j:
                s = jnp.where(low, s, -1e30)
            s_ref[i * QB : (i + 1) * QB, :] = s
            peak = jnp.max(s.reshape(QB // 8, 8, QB), axis=0)
            top = peak if top is None else jnp.maximum(top, peak)
        top = jnp.max(top, axis=0, keepdims=True)
        total = None
        for i in range(j + 1):
            w = jnp.exp(s_ref[i * QB : (i + 1) * QB, :] - top)
            s_ref[i * QB : (i + 1) * QB, :] = w
            part = jnp.sum(w.reshape(QB // 8, 8, QB), axis=0)
            total = part if total is None else total + part
        scale = 1.0 / jnp.sum(total, axis=0, keepdims=True)
        for i in range(j + 1):
            p_ref[i * QB : (i + 1) * QB, j * QB : (j + 1) * QB] = (s_ref[i * QB : (i + 1) * QB, :] * scale).astype(BF16)


def mix_kernel(
    unit, place, kept_ref, got_ref, _after, sorted_ref, came_ref, p_ref, own, got, g_own, g_got, v_ref, ot_ref, edge_ref, vt
):
    tok = own.shape[1]

    @pl.when(place[1] == 0)
    def _():
        edge_ref[0] = own[0]
        edge_ref[1] = g_own[...]

    @pl.when(place[1] == 1)
    def _():
        edge_ref[0] = got[0]
        edge_ref[1] = g_got[...]

    def kept(d, u, to):
        v_ref[rows(to * unit, unit), :] = sorted_ref[d, rows(u * unit, unit), :]

    def came(at, to):
        v_ref[rows(to * unit, unit), :] = came_ref[rows(at * unit, unit), :]

    each_unit(sorted_ref.shape[1] // unit, place, kept_ref, got_ref, kept, came)
    vt[...] = v_ref[...].astype(F32).T.astype(BF16)
    for j in range(CS // QB):
        end = (j + 1) * QB
        ot_ref[:, j * QB : end] = dot(vt[:, :end], p_ref[:end, j * QB : end])


def value_grads_kernel(unit, place, kept_ref, got_ref, _after, sorted_ref, came_ref, p_ref, g_ref, own_ref, back_ref, res):
    tok = sorted_ref.shape[1]

    def own(d, u, to):
        g_ref[rows(to * unit, unit), :] = sorted_ref[d, rows(u * unit, unit), :]

    def got(at, to):
        g_ref[rows(to * unit, unit), :] = came_ref[rows(at * unit, unit), :]

    each_unit(tok // unit, place, kept_ref, got_ref, own, got)
    for lo in range(0, CS, QB):
        res[lo : lo + QB, :] = dot(p_ref[lo : lo + QB, lo:], g_ref[lo:, :]).astype(BF16)

    def own_out(d, u, to):
        own_ref[d, 0, rows(u * unit, unit), :] = res[rows(to * unit, unit), :]

    def got_out(at, to):
        back_ref[0, rows(at * unit, unit), :] = res[rows(to * unit, unit), :]

    each_unit(tok // unit, place, kept_ref, got_ref, own_out, got_out)


def grads_kernel(
    unit, place, kept_ref, got_ref, _after, q_ref, k_ref, v_ref, kt_ref, ot_ref, p_ref, g_ref, own_ref, back_ref, dqt, res
):
    tok = own_ref.shape[2]
    delta = jnp.sum(g_ref[...].astype(F32).T * ot_ref[...], axis=0, keepdims=True)
    factor = HD**-0.5
    for lo in range(0, CS, QB):
        hi = lo + QB
        dp = dot_nt(v_ref[lo:hi, :], g_ref[lo:, :])
        ds = (p_ref[lo:hi, lo:].astype(F32) * (dp - delta[:, lo:])).astype(BF16)
        res[1, lo:hi, :] = (dot(ds, q_ref[lo:, :]) * factor).astype(BF16)
        part = dot(kt_ref[:, lo:hi], ds)
        dqt[:, lo:] = part if lo == 0 else dqt[:, lo:] + part
    res[0] = (dqt[...].T * factor).astype(BF16)

    def own_out(d, u, to):
        for i in range(2):
            own_ref[d, i, rows(u * unit, unit), :] = res[i, rows(to * unit, unit), :]

    def got_out(at, to):
        for i in range(2):
            back_ref[i, rows(at * unit, unit), :] = res[i, rows(to * unit, unit), :]

    each_unit(tok // unit, place, kept_ref, got_ref, own_out, got_out)


def unsort_kernel(unit, distances, kept_ref, _after, _after_edge, slot_col, own_ref, back_ref, *refs):
    *outs, full = refs
    tok = own_ref.shape[2]
    count = own_ref.shape[1]
    col_index = lax.broadcasted_iota(jnp.int32, (tok, tok), 1).astype(F32)
    offset = jnp.int32(0)
    for d in range(HR):
        kept = kept_ref[d]
        if d in distances:
            n = distances.index(d)

            def own(u, carry, d=d, n=n):
                for i in range(count):
                    full[n, i, rows(u * unit, unit), :] = own_ref[d, i, rows(u * unit, unit), :]
                return carry

            def got(u, carry, n=n, offset=offset, kept=kept):
                for i in range(count):
                    full[n, i, rows(u * unit, unit), :] = back_ref[i, rows((offset + u - kept) * unit, unit), :]
                return carry

            lax.fori_loop(0, kept, own, 0)
            lax.fori_loop(kept, tok // unit, got, 0)
            move = (col_index == slot_col[:, d : d + 1]).astype(BF16)
            for i in range(count):
                outs[n][i] = dot(move, full[n, i]).astype(BF16)
        offset = offset + tok // unit - kept


def window_kernel(
    place, _after, _after_edge, own, got, g_own, g_got, edge, dq_ref, early_ref, late_ref, stats_ref, *scratch
):
    tok = own.shape[1]
    pair = 2 * tok
    factor = HD**-0.5
    r = lax.broadcasted_iota(jnp.int32, (QB, QB), 0)
    c = lax.broadcasted_iota(jnp.int32, (QB, QB), 1)
    span = WIN + QB
    started = place[0] > 0
    own_at, got_at = place[1] * tok, (1 - place[1]) * tok
    for h in range(HL // 2):
        part = slice(h * HD, (h + 1) * HD)
        queries, grads, keys, values, kt, dk, dv = (ref.at[h] for ref in scratch)
        for at, block, g_block in ((own_at, own, g_own[:, part]), (got_at, got, g_got[:, part])):
            queries[rows(at, tok), :] = block[0, :, part]
            grads[rows(at, tok), :] = g_block
            keys[rows(at + WIN, tok), :] = block[1, :, part]
            values[rows(at + WIN, tok), :] = block[2, :, part]
        keys[:WIN, :] = edge[0, :, part]
        values[:WIN, :] = edge[1, :, part]
        kt[...] = keys[...].astype(F32).T.astype(BF16)
        for j in range(pair // QB):
            lo, hi = j * QB, j * QB + span
            q = queries[j * QB : (j + 1) * QB, :]
            g = grads[j * QB : (j + 1) * QB, :]
            s = dot_nt(keys[lo:hi, :], q) * factor
            first = jnp.where(r > c, s[:QB], -1e30)
            last = jnp.where(r <= c, s[span - QB :], -1e30)
            s = jnp.concatenate([first, s[QB : span - QB], last], axis=0)
            if lo < WIN:
                s = jnp.concatenate([jnp.where(started, s[: WIN - lo], -1e30), s[WIN - lo :]], axis=0)
            top = jnp.max(s, axis=0, keepdims=True)
            w = jnp.exp(s - top)
            scale = 1.0 / jnp.sum(w, axis=0, keepdims=True)
            p = w * scale
            dp = dot_nt(values[lo:hi, :], g)
            delta = jnp.sum(p * dp, axis=0, keepdims=True)
            pb = p.astype(BF16)
            ds = (p * (dp - delta)).astype(BF16)
            side, at = divmod(j * QB, tok)
            dq_ref[side, at : at + QB, part] = (dot(kt[:, lo:hi], ds).T * factor).astype(BF16)
            if side == 0:
                for n, line in enumerate((top, scale, delta)):
                    stats_ref[3 * h + n : 3 * h + n + 1, at : at + QB] = line
            skip = max(0, WIN - lo)
            low = max(lo, WIN) - WIN
            part_k = dot(ds[skip:], q) * factor
            part_v = dot(pb[skip:], g)
            end = hi - WIN
            if end - QB > low:
                dk[low : end - QB, :] = dk[low : end - QB, :] + part_k[:-QB]
                dv[low : end - QB, :] = dv[low : end - QB, :] + part_v[:-QB]
            dk[end - QB : end, :] = part_k[-QB:]
            dv[end - QB : end, :] = part_v[-QB:]
        for i, total in enumerate((dk, dv)):
            early_ref[i, :, part] = total[:tok, :].astype(BF16)
            late_ref[i, :, part] = total[tok:, :]
    stats_ref[6:, :] = jnp.zeros((2, tok), F32)


def settle_kernel(place, _after, dq_ref, early_ref, late_ref, edge, ahead, stats, own, send, late):
    tok = edge.shape[1]
    factor = HD**-0.5
    r = lax.broadcasted_iota(jnp.int32, (QB, QB), 0)
    c = lax.broadcasted_iota(jnp.int32, (QB, QB), 1)
    for h in range(HL // 2):
        part = slice(h * HD, (h + 1) * HD)
        for j in range(tok // QB):
            at = slice(j * QB, (j + 1) * QB)
            q, g = ahead[0, at, part], ahead[1, at, part]
            top, scale, delta = (stats[3 * h + n : 3 * h + n + 1, at] for n in range(3))
            s = dot_nt(edge[0, j * QB :, part], q) * factor
            p = jnp.exp(s - top) * scale
            first = jnp.where(r > c, p[:QB], 0.0)
            p = first if j == tok // QB - 1 else jnp.concatenate([first, p[QB:]], axis=0)
            ds = p * (dot_nt(edge[1, j * QB :, part], g) - delta)
            add_k = dot(ds.astype(BF16), q) * factor
            add_v = dot(p.astype(BF16), g)
            for i, add in enumerate((add_k, add_v)):
                base = late_ref[i, :, part] if j == 0 else late[h, i, j * QB :, :]
                late[h, i, j * QB :, :] = base + add
    for side, (near, far) in enumerate(((own, send), (send, own))):

        @pl.when(place[1] == side)
        def _(near=near, far=far):
            near[0] = dq_ref[0]
            near[1:] = early_ref[...]
            far[0] = dq_ref[1]
            for h in range(HL // 2):
                for i in range(2):
                    far[1 + i, :, h * HD : (h + 1) * HD] = late[h, i].astype(BF16)


def join_value_kernel(place, _after, v0, v1, v2, v3, out):
    for d, v in enumerate((v0, v1, v2, v3)):
        out[:, head_columns(place, d)] = v[0]


def join_kernel(place, value_ref, own, got, dq_ref, dk_ref, dv_ref):
    outs = (dq_ref, dk_ref, dv_ref)
    dv_ref[:, : HR * HD] = value_ref[...]
    width = HL * HD // 2
    for n in range(2):
        side = place[1] if n == 0 else 1 - place[1]
        at = pl.ds(pl.multiple_of(HR * HD + side * width, width), width)
        for i in range(3):
            outs[i][:, at] = own[i] if n == 0 else got[i]


def finish_kernel(place, y0, y1, y2, y3, _dq, _dk, dq_hbm, dk_hbm, sems):
    copies = []
    for d, y in enumerate((y0, y1, y2, y3)):
        for i, out in enumerate((dq_hbm, dk_hbm)):
            copies.append(pltpu.make_async_copy(y.at[i], out.at[:, head_columns(place, d)], sems.at[d, i]))
    start_all(copies)
    wait_all(copies)


def struct(*shape, dtype=BF16):
    return jax.ShapeDtypeStruct(shape, dtype)


def pair_body(query, key, value, grad_sent, out_weight, assign):
    tok = query.shape[1]
    devices = lax.axis_size("seq")
    place = lax.axis_index("seq")
    first, side = place // 2, place % 2
    where = jnp.stack([first, side]).astype(jnp.int32)
    unit = CS // (4 * devices)
    half = CS // 2

    def among_groups(block, shift):
        route = [(i, ((i // 2 + shift) % HR) * 2 + i % 2) for i in range(devices)]
        return lax.ppermute(block, "seq", route)

    def swap(block):
        return lax.ppermute(block, "seq", [(i, i ^ 1) for i in range(devices)])

    hbm = [pl.BlockSpec(memory_space=pltpu.HBM)]
    width = HL * HD // 2
    boundary = from_behind(grad_sent, "section", -1)[0]
    *sent, local_own, local_send = pl.pallas_call(
        split_kernel,
        out_shape=[struct(2 * tok + 16, HD)] * HR + [struct(3, tok, width)] * 2,
        in_specs=smem() + vmem() + hbm * 3,
        out_specs=vmem(6),
        scratch_shapes=[pltpu.VMEM((3, tok, query.shape[2]), BF16), pltpu.SemaphoreType.DMA((3, 4))],
        compiler_params=params(SPLIT_MIB),
        cost_estimate=takes(2),
        name="split",
    )(where, assign[0], query[0], key[0], value[0])
    arrived = [sent[0]] + [among_groups(sent[d], d) for d in range(1, HR)]
    local_got = swap(local_send)
    *g_sent, g_own, g_send = pl.pallas_call(
        project_kernel,
        grid=(4,),
        out_shape=[struct(tok, HD)] * HR + [struct(tok, width)] * 2,
        in_specs=smem()
        + [
            pl.BlockSpec((1, 16, HD), lambda n: (0, 0, 0)),
            pl.BlockSpec(boundary.shape, lambda n: (0, 0)),
            pl.BlockSpec((2 * HD, boundary.shape[1]), lambda n: (n, 0)),
        ],
        out_specs=[pl.BlockSpec((tok, HD), lambda n: (0, 0))] * HR
        + [pl.BlockSpec((tok, width), lambda n: (0, 0))] * 2,
        compiler_params=params(20),
        cost_estimate=takes(3.8),
        name="project",
    )(where, local_got, boundary, out_weight[0])
    g_arrived = [g_sent[0]] + [among_groups(g_sent[d], d) for d in range(1, HR)]

    g_got = swap(g_send)
    v_sent = pl.pallas_call(
        split_value_kernel,
        out_shape=[struct(tok, HD)] * HR,
        in_specs=smem() + vmem(5),
        out_specs=vmem(4),
        compiler_params=params(20),
        cost_estimate=takes(1),
        name="split_value",
    )(where, g_sent[0], *arrived[1:], value[0])
    v_arrived = [v_sent[0]] + [among_groups(v_sent[d], d) for d in range(1, HR)]

    ordered, send, slot_row, slot_col, kept = pl.pallas_call(
        functools.partial(pack_kernel, unit),
        out_shape=[
            struct(HR, 2, tok, HD),
            struct(2 * half + 16, HD),
            struct(8, tok, dtype=F32),
            struct(tok, HD, dtype=F32),
            struct(HR, dtype=jnp.int32),
        ],
        in_specs=smem() + vmem(5),
        out_specs=vmem(4) + smem(),
        compiler_params=params(20),
        cost_estimate=takes(0.1),
        name="pack",
    )(where, v_sent[0], *arrived)
    came = swap(send)

    v_ordered, v_out = pl.pallas_call(
        functools.partial(pack_value_kernel, unit),
        out_shape=[struct(HR, tok, HD), struct(half, HD)],
        in_specs=smem() + vmem(7),
        out_specs=vmem(2),
        compiler_params=params(20),
        cost_estimate=takes(12),
        name="pack_value",
    )(kept, send, g_got, slot_row, *v_arrived)
    v_came = swap(v_out)

    got, q, k, kt, p = pl.pallas_call(
        functools.partial(probs_kernel, unit),
        out_shape=[struct(HR, dtype=jnp.int32)] + [struct(CS, HD)] * 2 + [struct(HD, CS), struct(CS, CS)],
        in_specs=smem(2) + vmem(3),
        out_specs=smem() + vmem(4),
        scratch_shapes=[pltpu.VMEM((CS, QB), F32)],
        compiler_params=params(24),
        cost_estimate=takes(5),
        name="probs",
    )(where, kept, v_out, ordered, came)

    g_ordered, g_out, edge = pl.pallas_call(
        functools.partial(pack_grad_kernel, unit),
        out_shape=[struct(HR, tok, HD), struct(half, HD), struct(2, tok, width)],
        in_specs=smem(2) + vmem(8),
        out_specs=vmem(3),
        compiler_params=params(20),
        cost_estimate=takes(1.6),
        name="pack_grad",
    )(where, kept, kt, slot_row, *g_arrived, local_own, local_got)
    g_came = swap(g_out)
    ahead = [(i, i + 2) for i in range(devices - 2)]
    behind = [(i + 2, i) for i in range(devices - 2)]
    edge_got = lax.ppermute(edge, "seq", ahead)

    v, ot, query_edge = pl.pallas_call(
        functools.partial(mix_kernel, unit),
        out_shape=[struct(CS, HD), struct(HD, CS, dtype=F32), struct(2, tok, width)],
        in_specs=smem(3) + vmem(8),
        out_specs=vmem(3),
        scratch_shapes=[pltpu.VMEM((HD, CS), BF16)],
        compiler_params=params(20),
        cost_estimate=takes(1.7),
        name="mix",
    )(where, kept, got, edge, v_ordered, v_came, p, local_own, local_got, g_own, g_got)
    query_edge_got = lax.ppermute(query_edge, "seq", behind)

    g, own_v, back_v = pl.pallas_call(
        functools.partial(value_grads_kernel, unit),
        out_shape=[struct(CS, HD), struct(HR, 1, tok, HD), struct(1, half, HD)],
        in_specs=smem(3) + vmem(4),
        out_specs=vmem(3),
        scratch_shapes=[pltpu.VMEM((CS, HD), BF16)],
        compiler_params=params(16),
        cost_estimate=takes(2.4),
        name="value_grads",
    )(where, kept, got, ot, g_ordered, g_came, p)
    own, back = pl.pallas_call(
        functools.partial(grads_kernel, unit),
        out_shape=[struct(HR, 2, tok, HD), struct(2, half, HD)],
        in_specs=smem(3) + vmem(8),
        out_specs=vmem(2),
        scratch_shapes=[pltpu.VMEM((HD, CS), F32), pltpu.VMEM((2, CS, HD), BF16)],
        compiler_params=params(24),
        cost_estimate=takes(5),
        name="grads",
    )(where, kept, got, back_v, q, k, v, kt, ot, p, g)

    def unsort(distances, after, after_edge, own, returned, name):
        count = own.shape[1]
        return pl.pallas_call(
            functools.partial(unsort_kernel, unit, distances),
            out_shape=[struct(count, tok, HD)] * len(distances),
            in_specs=smem() + vmem(5),
            out_specs=vmem(len(distances)),
            scratch_shapes=[pltpu.VMEM((len(distances), count, tok, HD), BF16)],
            compiler_params=params(20),
            cost_estimate=takes({'unsort_value':2.6,'unsort_first':0.1,'unsort_last':1.4}[name]),
            name=name,
        )(kept, after, after_edge, slot_col, own, returned)

    returned_v, returned = swap(back_v), swap(back)
    pair = 2 * tok
    natural_v = unsort((0, 1, 2, 3), back, back, own_v, returned_v, "unsort_value")
    home_v = [natural_v[0]] + [among_groups(natural_v[d], -d) for d in range(1, HR)]
    dq_local, early, late, stats = pl.pallas_call(
        window_kernel,
        out_shape=[
            struct(2, tok, width),
            struct(2, tok, width),
            struct(2, tok, width, dtype=F32),
            struct(8, tok, dtype=F32),
        ],
        in_specs=smem() + vmem(7),
        out_specs=vmem(4),
        scratch_shapes=[
            pltpu.VMEM((HL // 2, pair, HD), BF16),
            pltpu.VMEM((HL // 2, pair, HD), BF16),
            pltpu.VMEM((HL // 2, pair + WIN, HD), BF16),
            pltpu.VMEM((HL // 2, pair + WIN, HD), BF16),
            pltpu.VMEM((HL // 2, HD, pair + WIN), BF16),
            pltpu.VMEM((HL // 2, pair, HD), F32),
            pltpu.VMEM((HL // 2, pair, HD), F32),
        ],
        compiler_params=params(24),
        cost_estimate=takes(0.1),
        name="window",
    )(where, natural_v[0], query_edge_got, local_own, local_got, g_own, g_got, edge_got)
    stats_got = lax.ppermute(stats, "seq", behind)
    first_natural = unsort((0, 1, 3), stats, stats, own, returned, "unsort_first")
    value_left = pl.pallas_call(
        join_value_kernel,
        out_shape=struct(tok, HR * HD),
        in_specs=smem() + vmem(5),
        out_specs=vmem()[0],
        compiler_params=params(16),
        cost_estimate=takes(12),
        name="join_value",
    )(where, first_natural[0], *home_v)
    settled_own, settled_send = pl.pallas_call(
        settle_kernel,
        out_shape=[struct(3, tok, width)] * 2,
        in_specs=smem() + vmem(7),
        out_specs=vmem(2),
        scratch_shapes=[pltpu.VMEM((HL // 2, 2, tok, HD), F32)],
        compiler_params=params(20),
        cost_estimate=takes(0.1),
        name="settle",
    )(where, value_left, dq_local, early, late, edge, query_edge_got, stats_got)
    settled_got = swap(settled_send)
    last_natural = unsort((2,), settled_send, settled_send, own, returned, "unsort_last")
    natural = [*first_natural]
    natural.insert(2, *last_natural)
    home = [natural[0]] + [among_groups(natural[d], -d) for d in range(1, HR)]

    dq_part, dk_part, dv = pl.pallas_call(
        join_kernel,
        out_shape=[struct(tok, (HR + HL) * HD)] * 3,
        in_specs=smem() + vmem(3),
        out_specs=vmem(3),
        compiler_params=params(20),
        cost_estimate=takes(2),
        name="join",
    )(where, value_left, settled_own, settled_got)
    dq, dk = pl.pallas_call(
        finish_kernel,
        out_shape=[struct(tok, (HR + HL) * HD)] * 2,
        in_specs=smem() + vmem(4) + hbm * 2,
        out_specs=hbm * 2,
        input_output_aliases={5: 0, 6: 1},
        scratch_shapes=[pltpu.SemaphoreType.DMA((HR, 2))],
        compiler_params=params(16),
        cost_estimate=takes(1.5),
        name="finish",
    )(where, *home, dq_part, dk_part)
    outs = (dq, dk, dv)
    return tuple(out[None] for out in outs)


def from_behind(block, axis, distance):
    devices = range(lax.axis_size(axis))
    route = [((i - distance) % len(devices), i) for i in devices]
    return lax.ppermute(block, axis, route)


def shifted(block, axis, distance):
    devices = range(lax.axis_size(axis))
    route = [(i - distance, i) for i in devices if i - distance in devices]
    return lax.ppermute(block, axis, route)


def cluster_block(query_rows, key_rows, value_rows, grad_rows, allowed, factor):
    scores = jnp.dot(query_rows, key_rows.T, preferred_element_type=jnp.float32) * factor
    scores = jnp.where(allowed, scores, -1e30)
    highest = jnp.max(scores, axis=1, keepdims=True)
    weights = jnp.exp(scores - highest)
    probs = weights / jnp.sum(weights, axis=1, keepdims=True)
    dprob = jnp.dot(grad_rows, value_rows.T, preferred_element_type=jnp.float32)
    delta = jnp.sum(probs * dprob, axis=1, keepdims=True)
    dscore = probs * (dprob - delta)
    probs_b = probs.astype(jnp.bfloat16)
    dscore_b = dscore.astype(jnp.bfloat16)
    grad_query = jnp.dot(dscore_b, key_rows, preferred_element_type=jnp.float32) * factor
    grad_key = jnp.dot(dscore_b.T, query_rows, preferred_element_type=jnp.float32) * factor
    grad_value = jnp.dot(probs_b.T, grad_rows, preferred_element_type=jnp.float32)
    return (grad_query, grad_key, grad_value)


def cluster_grads(query_rows, key_rows, value_rows, grad_rows, factor):
    length = query_rows.shape[0]
    span = min(512, length)
    pieces = []
    total_key = jnp.zeros(key_rows.shape, jnp.float32)
    total_value = jnp.zeros(value_rows.shape, jnp.float32)
    for index in range(length // span):
        first = index * span
        end = first + span
        allowed = (
            jnp.arange(end, dtype=jnp.int32)[None, :]
            <= (first + jnp.arange(span, dtype=jnp.int32))[:, None]
        )
        part_query, part_key, part_value = cluster_block(
            query_rows[first:end],
            key_rows[:end],
            value_rows[:end],
            grad_rows[first:end],
            allowed,
            factor,
        )
        pieces.append(part_query)
        total_key = total_key.at[:end].add(part_key)
        total_value = total_value.at[:end].add(part_value)
    return (jnp.concatenate(pieces, axis=0), total_key, total_value)


def window_block(query_rows, key_rows, value_rows, grad_rows, allowed, factor):
    scores = (
        jnp.einsum("qhd,khd->hqk", query_rows, key_rows, preferred_element_type=jnp.float32)
        * factor
    )
    scores = jnp.where(allowed[None], scores, -1e30)
    highest = jnp.max(scores, axis=2, keepdims=True)
    weights = jnp.exp(scores - highest)
    probs = weights / jnp.sum(weights, axis=2, keepdims=True)
    dprob = jnp.einsum("qhd,khd->hqk", grad_rows, value_rows, preferred_element_type=jnp.float32)
    delta = jnp.sum(probs * dprob, axis=2, keepdims=True)
    dscore = probs * (dprob - delta)
    probs_b = probs.astype(jnp.bfloat16)
    dscore_b = dscore.astype(jnp.bfloat16)
    grad_query = (
        jnp.einsum("hqk,khd->qhd", dscore_b, key_rows, preferred_element_type=jnp.float32) * factor
    )
    grad_key = (
        jnp.einsum("hqk,qhd->khd", dscore_b, query_rows, preferred_element_type=jnp.float32)
        * factor
    )
    grad_value = jnp.einsum("hqk,qhd->khd", probs_b, grad_rows, preferred_element_type=jnp.float32)
    return (grad_query, grad_key, grad_value)


def window_mask(query_pos, key_pos):
    return (
        (key_pos[None, :] > query_pos[:, None] - WIN)
        & (key_pos[None, :] <= query_pos[:, None])
        & (key_pos[None, :] >= 0)
    )


def general_body(query, key, value, grad_sent, out_weight, assign):
    tok_rows = query.shape[1]
    heads = HR + HL
    devices = lax.axis_size("seq")
    place = lax.axis_index("seq")
    factor = HD ** (-0.5)
    boundary = from_behind(grad_sent, "section", -1)[0]
    attn_grad = lax.dot_general(
        boundary, out_weight[0], (((1,), (1,)), ((), ())), preferred_element_type=jnp.float32
    ).astype(jnp.bfloat16)
    query_heads = query[0].reshape(tok_rows, heads, HD)
    key_heads = key[0].reshape(tok_rows, heads, HD)
    value_heads = value[0].reshape(tok_rows, heads, HD)
    grad_heads = attn_grad.reshape(tok_rows, heads, HD)
    clusters = tok_rows * devices // CS
    owned = HR * tok_rows // CS
    capacity = 7 * CS // (4 * devices)
    unit_rows = capacity // 7
    width = owned * capacity
    head_slots = clusters * capacity
    labels = assign[0]
    members = (labels[:, :, None] == jnp.arange(clusters, dtype=jnp.int32)[None, None, :]).astype(
        jnp.bfloat16
    )
    token_ids = jnp.arange(tok_rows, dtype=jnp.int32)
    lower = (token_ids[:, None] >= token_ids[None, :]).astype(jnp.bfloat16)
    running_counts = jnp.einsum("ts,hsc->htc", lower, members, preferred_element_type=jnp.float32)
    ranks = (jnp.sum(running_counts * members.astype(jnp.float32), axis=2) - 1.0).astype(jnp.int32)
    local_slot = labels * capacity + ranks
    slot_hit = jnp.arange(head_slots, dtype=jnp.int32)[None, :, None] == local_slot[:, None, :]
    slot_table = slot_hit.astype(jnp.bfloat16)
    routed_in = jnp.concatenate(
        [query_heads[:, :HR], key_heads[:, :HR], value_heads[:, :HR], grad_heads[:, :HR]], axis=2
    )
    packed = jnp.einsum(
        "hst,thd->hsd", slot_table, routed_in, preferred_element_type=jnp.float32
    ).astype(jnp.bfloat16)
    packed = packed.reshape(devices, width, 4 * HD)
    token_pos = place * tok_rows + token_ids
    slot_pos = jnp.max(jnp.where(slot_hit, token_pos[None, None, :], -1), axis=2).reshape(
        devices, width
    )
    send_query = packed[:, :, :HD]
    send_key = packed[:, :, HD : 2 * HD]
    send_value = packed[:, :, 2 * HD : 3 * HD]
    send_grad = packed[:, :, 3 * HD :]
    arrived_query, arrived_key, arrived_value, arrived_grad, arrived_pos = (
        lax.all_to_all(send_query, "seq", split_axis=0, concat_axis=0, tiled=True),
        lax.all_to_all(send_key, "seq", split_axis=0, concat_axis=0, tiled=True),
        lax.all_to_all(send_value, "seq", split_axis=0, concat_axis=0, tiled=True),
        lax.all_to_all(send_grad, "seq", split_axis=0, concat_axis=0, tiled=True),
        lax.all_to_all(slot_pos, "seq", split_axis=0, concat_axis=0, tiled=True),
    )
    arrived_all = jnp.concatenate([arrived_query, arrived_key, arrived_value, arrived_grad], axis=2)
    unit_index = jnp.arange(7, dtype=jnp.int32)
    target_units = jnp.arange(CS // unit_rows, dtype=jnp.int32)
    block = arrived_all.reshape(devices * 7, unit_rows * 4 * HD)
    live_counts = jnp.sum((arrived_pos >= 0).astype(jnp.int32), axis=1)
    units = live_counts // unit_rows
    starts = jnp.cumsum(units) - units
    picker = (target_units[:, None, None] == starts[None, :, None] + unit_index[None, None, :]) & (
        unit_index[None, None, :] < units[None, :, None]
    )
    picker = picker.reshape(CS // unit_rows, devices * 7).astype(jnp.bfloat16)
    compact = (
        jnp.dot(picker, block, preferred_element_type=jnp.float32)
        .astype(jnp.bfloat16)
        .reshape(CS, 4 * HD)
    )
    results = cluster_grads(
        compact[:, :HD],
        compact[:, HD : 2 * HD],
        compact[:, 2 * HD : 3 * HD],
        compact[:, 3 * HD :],
        factor,
    )
    answer = jnp.concatenate([result.astype(jnp.bfloat16) for result in results], axis=1).reshape(
        CS // unit_rows, unit_rows * 3 * HD
    )
    spread = jnp.dot(picker.T, answer, preferred_element_type=jnp.float32).astype(jnp.bfloat16)
    outgoing = spread.reshape(devices, capacity, 3 * HD)
    back_query, back_key, back_value = (
        lax.all_to_all(outgoing[:, :, :HD], "seq", split_axis=0, concat_axis=0, tiled=True),
        lax.all_to_all(outgoing[:, :, HD : 2 * HD], "seq", split_axis=0, concat_axis=0, tiled=True),
        lax.all_to_all(outgoing[:, :, 2 * HD :], "seq", split_axis=0, concat_axis=0, tiled=True),
    )
    back_all = jnp.concatenate([back_query, back_key, back_value], axis=2).reshape(
        HR, head_slots, 3 * HD
    )
    routed_out = jnp.einsum(
        "hst,hsd->thd", slot_table, back_all, preferred_element_type=jnp.float32
    ).astype(jnp.bfloat16)
    routed_query = routed_out[:, :, :HD]
    routed_key = routed_out[:, :, HD : 2 * HD]
    routed_value = routed_out[:, :, 2 * HD :]
    local_query = query_heads[:, HR:]
    local_key = key_heads[:, HR:]
    local_value = value_heads[:, HR:]
    local_grad = grad_heads[:, HR:]
    prior_key, prior_value = shifted((local_key, local_value), "seq", 1)
    keys_all = jnp.concatenate([prior_key, local_key], axis=0)
    values_all = jnp.concatenate([prior_value, local_value], axis=0)
    key_positions = (place - 1) * tok_rows + jnp.arange(2 * tok_rows, dtype=jnp.int32)
    query_positions = place * tok_rows + jnp.arange(tok_rows, dtype=jnp.int32)
    span = min(512, tok_rows)
    total_key = jnp.zeros((2 * tok_rows, HL, HD), jnp.float32)
    total_value = jnp.zeros((2 * tok_rows, HL, HD), jnp.float32)
    start = tok_rows - WIN
    allowed = window_mask(query_positions, key_positions)
    part_query, part_key, part_value = window_block(
        local_query, keys_all, values_all, local_grad, allowed, factor
    )
    total_key = total_key.at[start : start + span + WIN].add(part_key)
    total_value = total_value.at[start : start + span + WIN].add(part_value)
    tail = tok_rows - WIN
    carried_key, carried_value = (
        shifted(total_key[tail:tok_rows].astype(jnp.bfloat16), "seq", -1).astype(jnp.float32),
        shifted(total_value[tail:tok_rows].astype(jnp.bfloat16), "seq", -1).astype(jnp.float32),
    )
    local_dk = total_key[tok_rows:].at[tail:].add(carried_key)
    local_dv = total_value[tok_rows:].at[tail:].add(carried_value)
    local_dq = part_query.astype(jnp.bfloat16)
    grad_query = jnp.concatenate([routed_query, local_dq], axis=1).reshape(1, tok_rows, heads * HD)
    grad_key = jnp.concatenate([routed_key, local_dk.astype(jnp.bfloat16)], axis=1).reshape(
        1, tok_rows, heads * HD
    )
    grad_value = jnp.concatenate([routed_value, local_dv.astype(jnp.bfloat16)], axis=1).reshape(
        1, tok_rows, heads * HD
    )
    return (grad_query, grad_key, grad_value)


def body(query, key, value, grad_sent, out_weight, assign):
    clusters = query.shape[1] * lax.axis_size("seq") // CS
    plan = pair_body if clusters == 2 else general_body
    return plan(query, key, value, grad_sent, out_weight, assign)


def solution(mesh):
    placed = (
        P("section", "seq", None),
        P("section", "seq", None),
        P("section", "seq", None),
        P("section", "seq", None),
        P("section", None, None),
        P("section", None, "seq"),
    )
    return jax.shard_map(
        body,
        mesh=mesh,
        in_specs=placed,
        out_specs=(P("section", "seq", None), P("section", "seq", None), P("section", "seq", None)),
        check_vma=False,
    )
```
